32 devices in a mesh: dp: 8 (over z, y), fsdp: 4 (over x, core).
Axes of the slice: x: 2, y: 2, z: 4, core: 2. Of those that a mesh axis runs over, the one named last changes fastest.
Arguments:
- tokens: bfloat16 [16384, 768], P(('dp', 'fsdp')), may hold values from -6 to 6
- cotangent: bfloat16 [16384, 768], P(('dp', 'fsdp')), may hold values from -6 to 6
- segment_ids: int32 [16384], P('dp'), may hold values from 0 to 24, as said below
- segment_starts: int32 [16384], P('dp'), may hold values from 0 to 2047, as said below
- padding_mask: int32 [16384], P('dp'), may hold values from 0 to 1, as said below
- lead_index: int32 [8], P('dp'), may hold values from 0 to 19
- input_weights: float32 [2, 768, 2304], P(None, ('dp', 'fsdp')), may hold values from -0.21875 to 0.21875
- input_moment: float32 [2, 768, 2304], P(None, ('dp', 'fsdp')), may hold values from -224 to 224
- input_square: float32 [2, 768, 2304], P(None, ('dp', 'fsdp')), may hold values from 737.28 to 11796.48
- output_weights: float32 [2, 768, 768], P(None, ('dp', 'fsdp')), may hold values from -0.875 to 0.875
- output_moment: float32 [2, 768, 768], P(None, ('dp', 'fsdp')), may hold values from -160 to 160
- output_square: float32 [2, 768, 768], P(None, ('dp', 'fsdp')), may hold values from 327.68 to 5242.88
- expand_weights: float32 [2, 768, 3072], P(None, ('dp', 'fsdp')), may hold values from -0.21875 to 0.21875
- expand_moment: float32 [2, 768, 3072], P(None, ('dp', 'fsdp')), may hold values from -192 to 192
- expand_square: float32 [2, 768, 3072], P(None, ('dp', 'fsdp')), may hold values from 491.52 to 8192
- shrink_weights: float32 [2, 3072, 768], P(None, ('dp', 'fsdp')), may hold values from -0.109375 to 0.109375
- shrink_moment: float32 [2, 3072, 768], P(None, ('dp', 'fsdp')), may hold values from -448 to 448
- shrink_square: float32 [2, 3072, 768], P(None, ('dp', 'fsdp')), may hold values from 2949.12 to 47185.92
- bias_vector: float32 [2, 9, 768], P(None, None, ('dp', 'fsdp')), may hold values from -4 to 4
- bias_moment: float32 [2, 9, 768], P(None, None, ('dp', 'fsdp')), may hold values from -384 to 384
- bias_square: float32 [2, 9, 768], P(None, None, ('dp', 'fsdp')), may hold values from 2048 to 32768
- lead_table: float32 [2, 20, 3072], P(None, None, ('dp', 'fsdp')), may hold values from -4 to 4
- lead_moment: float32 [2, 20, 3072], P(None, None, ('dp', 'fsdp')), may hold values from -80 to 80
- lead_square: float32 [2, 20, 3072], P(None, None, ('dp', 'fsdp')), may hold values from 102.375 to 1638
Outputs:
- out_tokens: float32 [16384, 768], P(('dp', 'fsdp'))
- in_grad: float32 [16384, 768], P(('dp', 'fsdp'))
- input_updated: float32 [2, 768, 2304], P(None, ('dp', 'fsdp'))
- input_moments: float32 [2, 768, 2304], P(None, ('dp', 'fsdp'))
- input_squares: float32 [2, 768, 2304], P(None, ('dp', 'fsdp'))
- input_copies: bfloat16 [2, 768, 2304], P(None, ('dp', 'fsdp'))
- output_updated: float32 [2, 768, 768], P(None, ('dp', 'fsdp'))
- output_moments: float32 [2, 768, 768], P(None, ('dp', 'fsdp'))
- output_squares: float32 [2, 768, 768], P(None, ('dp', 'fsdp'))
- output_copies: bfloat16 [2, 768, 768], P(None, ('dp', 'fsdp'))
- expand_updated: float32 [2, 768, 3072], P(None, ('dp', 'fsdp'))
- expand_moments: float32 [2, 768, 3072], P(None, ('dp', 'fsdp'))
- expand_squares: float32 [2, 768, 3072], P(None, ('dp', 'fsdp'))
- expand_copies: bfloat16 [2, 768, 3072], P(None, ('dp', 'fsdp'))
- shrink_updated: float32 [2, 3072, 768], P(None, ('dp', 'fsdp'))
- shrink_moments: float32 [2, 3072, 768], P(None, ('dp', 'fsdp'))
- shrink_squares: float32 [2, 3072, 768], P(None, ('dp', 'fsdp'))
- shrink_copies: bfloat16 [2, 3072, 768], P(None, ('dp', 'fsdp'))
- bias_updated: float32 [2, 9, 768], P(None, None, ('dp', 'fsdp'))
- bias_moments: float32 [2, 9, 768], P(None, None, ('dp', 'fsdp'))
- bias_squares: float32 [2, 9, 768], P(None, None, ('dp', 'fsdp'))
- bias_copies: bfloat16 [2, 9, 768], P(None, None, ('dp', 'fsdp'))
- lead_updated: float32 [2, 20, 3072], P(None, None, ('dp', 'fsdp'))
- lead_moments: float32 [2, 20, 3072], P(None, None, ('dp', 'fsdp'))
- lead_squares: float32 [2, 20, 3072], P(None, None, ('dp', 'fsdp'))
- lead_copies: bfloat16 [2, 20, 3072], P(None, None, ('dp', 'fsdp'))
The draws below stay inside these ranges and needn't reach their ends.
Inputs may be any that keep to these rules, and one draw needn't show every extreme that they name: `segment_ids`: in each sequence of 2048 patches the window number starts at 0 and rises by one at each new window; every window but a sequence's last holds 64 to 512 consecutive patches, and some window of every sequence holds exactly 512; the last one may be cut by the sequence's end. `segment_starts`: equal for all patches of one window: the position of its first patch within the sequence. `padding_mask`: 0 exactly on the patches of a sequence's last window where it is cut by the sequence's end.
All inputs are finite; a program needn't handle non-finite values.
Results may differ from the reference program's by a relative error of at most 0.015.
Values may be sent and summed in bfloat16 or wider, within the bound.
A program may use at most 384 MiB of HBM per device.

```python
import math
import jax
import jax.numpy as jnp
from jax import lax

D = 768
FF = 3072
HEADS = 12
HEAD_DIM = 64
LEADS = 20
LAYERS = 2
WIN_MIN = 64
WIN_MAX = 512
STEP = 10
LENGTH = 2048
SEQS = 8
TOKENS = 16384
BIAS_ROWS = 9
MOD_LEN = 3072


def window_layout(key):
    slot_count = LENGTH // WIN_MIN
    seq_keys = jax.random.split(jax.random.fold_in(key, 7), SEQS)
    dense_seq = jax.random.randint(jax.random.fold_in(key, 11), (), 0, SEQS)
    dense_flags = (jnp.arange(SEQS, dtype=jnp.int32) == dense_seq).astype(jnp.int32)
    slot_number = jnp.arange(slot_count, dtype=jnp.int32)
    dense_widths = jnp.where(slot_number == 0, WIN_MAX, jnp.where(slot_number == 1, 2 * WIN_MIN - 1, WIN_MIN)).astype(jnp.int32)

    def one_sequence(seq_key, dense_flag):
        sizes_key, forced_key = jax.random.split(seq_key)
        widths = jax.random.randint(sizes_key, (slot_count,), WIN_MIN, WIN_MAX + 1)
        forced = jax.random.randint(forced_key, (), 0, 2)
        widths = jnp.where(slot_number == forced, WIN_MAX, widths).astype(jnp.int32)
        widths = jnp.where(dense_flag == 1, dense_widths, widths).astype(jnp.int32)
        window_ends = jnp.cumsum(widths).astype(jnp.int32)
        window_begins = window_ends - widths
        position = jnp.arange(LENGTH, dtype=jnp.int32)
        window_number = jnp.sum((window_ends[None, :] <= position[:, None]).astype(jnp.int32), axis=1)
        complete = (window_ends[window_number] <= LENGTH).astype(jnp.int32)
        return (window_number, window_begins[window_number], complete)
    window_number, window_start, complete = jax.vmap(one_sequence)(seq_keys, dense_flags)
    return (window_number.reshape(-1).astype(jnp.int32), window_start.reshape(-1).astype(jnp.int32), complete.reshape(-1).astype(jnp.int32))


def draw_segment_ids(key, part):
    return window_layout(key)[0]


def draw_segment_starts(key, part):
    return window_layout(key)[1]


def draw_padding_mask(key, part):
    return window_layout(key)[2]


def place_ends(values, stream_key, smallest, high):
    spot = [jax.random.randint(jax.random.fold_in(stream_key, axis), (), 0, length) for axis, length in enumerate(values.shape)]
    widest = values.shape.index(max(values.shape))
    next_to = spot[:widest] + [(spot[widest] + 1) % values.shape[widest]] + spot[widest + 1:]
    return values.at[tuple(spot)].set(smallest).at[tuple(next_to)].set(high)


def steps_of(stream_key, dims, pieces, least, largest):
    def one(dim, parts):
        steps = jax.random.uniform(jax.random.fold_in(jax.random.fold_in(stream_key, 6), dim), (parts,), jnp.float32, least / len(pieces), largest / len(pieces))
        return jnp.repeat(jnp.exp(steps), dims[dim] // parts).reshape((-1,) + (1,) * (len(dims) - dim - 1))

    gain = one(*pieces[0])
    for cut in pieces[1:]:
        gain = gain * one(*cut)
    return gain


def normal_values(own_key, dims, width, bound, cuts=(), kind=jnp.bfloat16):
    entries = jax.random.normal(own_key, dims, jnp.float32) * width
    if len(cuts) > 0:
        entries = steps_of(own_key, dims, cuts, -0.22, 0.18) * entries
    return jnp.clip(entries, min=-bound, max=bound).astype(kind)


def setup_inputs(seed: int = 0) -> dict:
    key_list = jax.random.split(jax.random.key(seed), 25)
    return {
        "tokens": normal_values(key_list[0], (TOKENS, D), 1.0, 6.0, ((0, 32),)),
        "cotangent": normal_values(key_list[1], (TOKENS, D), 1.0, 6.0, ((0, 32),)),
        "segment_ids": draw_segment_ids(jax.random.fold_in(key_list[24], 71), 0),
        "segment_starts": draw_segment_starts(jax.random.fold_in(key_list[24], 71), 0),
        "padding_mask": draw_padding_mask(jax.random.fold_in(key_list[24], 71), 0),
        "lead_index": place_ends(jax.random.randint(key_list[5], (SEQS,), 0, LEADS), jax.random.fold_in(key_list[5], 1), 0, LEADS - 1).astype(jnp.int32),
        "input_weights": normal_values(key_list[6], (LAYERS, D, 3 * D), D ** -0.5, 0.21875, ((1, 32),), jnp.float32),
        "input_moment": normal_values(key_list[7], (LAYERS, D, 3 * D), (0.3 * TOKENS ** 0.5), 224.0, ((1, 32),), jnp.float32),
        "input_square": jnp.clip(jnp.exp(math.log(11796.48) - 2.7725887 * jax.random.uniform(key_list[8], (LAYERS, D, 3 * D), jnp.float32) ** steps_of(key_list[8], (LAYERS, D, 3 * D), ((1, 32),), -0.2, 0.2)), 737.28, 11796.48),
        "output_weights": normal_values(key_list[9], (LAYERS, D, D), (D // 16) ** -0.5, 0.875, ((1, 32),), jnp.float32),
        "output_moment": normal_values(key_list[10], (LAYERS, D, D), (0.2 * TOKENS ** 0.5), 160.0, ((1, 32),), jnp.float32),
        "output_square": jnp.clip(jnp.exp(math.log(5242.88) - 2.7725887 * jax.random.uniform(key_list[11], (LAYERS, D, D), jnp.float32) ** steps_of(key_list[11], (LAYERS, D, D), ((1, 32),), -0.2, 0.2)), 327.68, 5242.88),
        "expand_weights": normal_values(key_list[12], (LAYERS, D, FF), D ** -0.5, 0.21875, ((1, 32),), jnp.float32),
        "expand_moment": normal_values(key_list[13], (LAYERS, D, FF), (0.25 * TOKENS ** 0.5), 192.0, ((1, 32),), jnp.float32),
        "expand_square": jnp.clip(jnp.exp(math.log(8192.0) - 2.8134107 * jax.random.uniform(key_list[14], (LAYERS, D, FF), jnp.float32) ** steps_of(key_list[14], (LAYERS, D, FF), ((1, 32),), -0.2, 0.2)), 491.52, 8192.0),
        "shrink_weights": normal_values(key_list[15], (LAYERS, FF, D), FF ** -0.5, 0.109375, ((1, 32),), jnp.float32),
        "shrink_moment": normal_values(key_list[16], (LAYERS, FF, D), (0.6 * TOKENS ** 0.5), 448.0, ((1, 32),), jnp.float32),
        "shrink_square": jnp.clip(jnp.exp(math.log(47185.92) - 2.7725887 * jax.random.uniform(key_list[17], (LAYERS, FF, D), jnp.float32) ** steps_of(key_list[17], (LAYERS, FF, D), ((1, 32),), -0.2, 0.2)), 2949.12, 47185.92),
        "bias_vector": normal_values(key_list[18], (LAYERS, BIAS_ROWS, D), 0.3, 4.0, ((2, 32),), jnp.float32),
        "bias_moment": normal_values(key_list[19], (LAYERS, BIAS_ROWS, D), (0.5 * TOKENS ** 0.5), 384.0, ((2, 32),), jnp.float32),
        "bias_square": jnp.clip(jnp.exp(math.log(32768.0) - 2.7725887 * jax.random.uniform(key_list[20], (LAYERS, BIAS_ROWS, D), jnp.float32) ** steps_of(key_list[20], (LAYERS, BIAS_ROWS, D), ((2, 32),), -0.2, 0.2)), 2048.0, 32768.0),
        "lead_table": normal_values(key_list[21], (LAYERS, LEADS, MOD_LEN), 0.3, 4.0, ((2, 32),), jnp.float32),
        "lead_moment": normal_values(key_list[22], (LAYERS, LEADS, MOD_LEN), (0.5 * (TOKENS // LEADS) ** 0.5), 80.0, ((2, 32),), jnp.float32),
        "lead_square": jnp.clip(jnp.exp(math.log(1638.0) - 2.7725887 * jax.random.uniform(key_list[23], (LAYERS, LEADS, MOD_LEN), jnp.float32) ** steps_of(key_list[23], (LAYERS, LEADS, MOD_LEN), ((2, 32),), -0.2, 0.2)), 102.375, 1638.0),
    }


EPSILON = 1e-06
NEGATIVE = -1e+30
BETA_ONE = 0.5
BETA_TWO = 0.5
RATE_MATRIX = 0.08
RATE_VECTOR = 0.3
DECAY = 0.1
ADAM_EPSILON = 1e-08
HIGHEST = lax.Precision.HIGHEST

@jax.custom_vjp
def low(v):
    return lax.optimization_barrier(v.astype(jnp.bfloat16)).astype(jnp.float32)

@jax.custom_vjp
def low_back(v):
    return v

def low_keep(v):
    return (low(v), None)

def low_pass(kept, grad):
    return (grad,)

def back_keep(v):
    return (v, None)

def back_low(kept, grad):
    return (low(grad),)
low.defvjp(low_keep, low_pass)
low_back.defvjp(back_keep, back_low)

def normalize(values):
    centred = values - lax.optimization_barrier(jnp.mean(values, axis=-1, keepdims=True))
    spread = lax.optimization_barrier(jnp.mean(centred * centred, axis=-1, keepdims=True))
    return centred * lax.rsqrt(spread + EPSILON)

def rotary_tables(relative):
    indices = jnp.arange(HEAD_DIM // 2).astype(jnp.float32)
    frequency = jnp.exp(indices * (-2.0 * math.log(10000.0) / HEAD_DIM))
    phase = relative.astype(jnp.float32)[:, None] * frequency[None, :]
    return (jnp.cos(phase)[:, None, :], jnp.sin(phase)[:, None, :])

def rotate(field, cosine_table, sine_table):
    half_dim = field.shape[-1] // 2
    first_half = field[..., :half_dim]
    second = field[..., half_dim:]
    return jnp.concatenate([first_half * cosine_table - second * sine_table, second * cosine_table + first_half * sine_table], axis=-1)

def attend_sequence(packed):
    queries, key_rows, values, segment, complete = packed
    length = queries.shape[0]
    block_size = min(512, length)
    block_count = length // block_size
    position = jnp.arange(length, dtype=jnp.int32)

    def one_block(piece):
        query_block, segment_block, position_block = piece
        raw_scores = low_back(jnp.einsum('qhd,khd->hqk', query_block, key_rows, precision=HIGHEST) * HEAD_DIM ** (-0.5))
        allowed = (segment_block[:, None] == segment[None, :]) & (complete[None, :] == 1) | (position_block[:, None] == position[None, :])
        scores = jnp.where(allowed[None, :, :], raw_scores, NEGATIVE)
        log_total = jax.nn.logsumexp(scores, axis=-1, keepdims=True)
        weights = low(jnp.exp(scores - log_total))
        return jnp.einsum('hqk,khd->qhd', weights, values, precision=HIGHEST)
    result = lax.map(jax.checkpoint(one_block), (queries.reshape(block_count, block_size, HEADS, HEAD_DIM), segment.reshape(block_count, block_size), position.reshape(block_count, block_size)))
    return result.reshape(length, HEADS, HEAD_DIM)

def forward(tokens, params, segment_ids, segment_starts, padding_mask, lead_index):
    input_weights, output_weights, expand_weights, shrink_weights, bias_vector, lead_table = params
    relative = jnp.arange(TOKENS, dtype=jnp.int32) % LENGTH - segment_starts.astype(jnp.int32)
    cosine_table, sine_table = rotary_tables(relative)
    lead_rows = jnp.repeat(lead_index.astype(jnp.int32), LENGTH)
    stream = tokens
    for layer_index in range(LAYERS):
        biases = bias_vector[layer_index].reshape(-1)
        modulation = lead_table[layer_index][lead_rows]
        shift_one = modulation[:, :D]
        scale_one = modulation[:, D:2 * D]
        shift_two = modulation[:, 2 * D:3 * D]
        scale_two = modulation[:, 3 * D:]
        normed = low(normalize(stream) * (1.0 + scale_one) + shift_one)
        projected = low_back(jnp.dot(normed, input_weights[layer_index], precision=HIGHEST, preferred_element_type=jnp.float32) + biases[:3 * D])
        queries = low(rotate(projected[:, :D].reshape(TOKENS, HEADS, HEAD_DIM), cosine_table, sine_table))
        key_rows = low(rotate(projected[:, D:2 * D].reshape(TOKENS, HEADS, HEAD_DIM), cosine_table, sine_table))
        values = low(projected[:, 2 * D:].reshape(TOKENS, HEADS, HEAD_DIM))
        attended = lax.map(attend_sequence, (queries.reshape(SEQS, LENGTH, HEADS, HEAD_DIM), key_rows.reshape(SEQS, LENGTH, HEADS, HEAD_DIM), values.reshape(SEQS, LENGTH, HEADS, HEAD_DIM), segment_ids.reshape(SEQS, LENGTH), padding_mask.reshape(SEQS, LENGTH)))
        attended = low(low_back(attended.reshape(TOKENS, D)))
        stream = stream + low_back(jnp.dot(attended, output_weights[layer_index], precision=HIGHEST, preferred_element_type=jnp.float32) + biases[3 * D:4 * D])
        normed = low(normalize(stream) * (1.0 + scale_two) + shift_two)
        hidden = low_back(jnp.dot(normed, expand_weights[layer_index], precision=HIGHEST, preferred_element_type=jnp.float32) + biases[4 * D:4 * D + FF])
        active = low(jax.nn.gelu(hidden, approximate=False))
        stream = stream + low_back(jnp.dot(active, shrink_weights[layer_index], precision=HIGHEST, preferred_element_type=jnp.float32) + biases[4 * D + FF:])
    return stream

def adam_update(weight, gradient, moment, square, step_rate, decay_rate):
    moment = BETA_ONE * moment + (1.0 - BETA_ONE) * gradient
    square = BETA_TWO * square + (1.0 - BETA_TWO) * gradient * gradient
    first_fix = 1.0 - BETA_ONE ** STEP
    second_fix = 1.0 - BETA_TWO ** STEP
    update = moment / first_fix / (jnp.sqrt(square / second_fix) + ADAM_EPSILON)
    weight = weight - step_rate * (update + decay_rate * weight)
    return (weight, moment, square, weight.astype(jnp.bfloat16))

def reference(tokens, cotangent, segment_ids, segment_starts, padding_mask, lead_index, input_weights, input_moment, input_square, output_weights, output_moment, output_square, expand_weights, expand_moment, expand_square, shrink_weights, shrink_moment, shrink_square, bias_vector, bias_moment, bias_square, lead_table, lead_moment, lead_square):
    copies = (low(input_weights), low(output_weights), low(expand_weights), low(shrink_weights), low(bias_vector), low(lead_table))

    def apply(stream, params):
        return forward(stream, params, segment_ids, segment_starts, padding_mask, lead_index)
    result, pullback = jax.vjp(apply, tokens.astype(jnp.float32), copies)
    in_grad, gradients = pullback(cotangent.astype(jnp.float32))
    first_set = adam_update(input_weights, gradients[0], input_moment, input_square, RATE_MATRIX, DECAY)
    second_set = adam_update(output_weights, gradients[1], output_moment, output_square, RATE_MATRIX, DECAY)
    third_set = adam_update(expand_weights, gradients[2], expand_moment, expand_square, RATE_MATRIX, DECAY)
    fourth_set = adam_update(shrink_weights, gradients[3], shrink_moment, shrink_square, RATE_MATRIX, DECAY)
    fifth_set = adam_update(bias_vector, gradients[4], bias_moment, bias_square, RATE_VECTOR, 0.0)
    sixth_set = adam_update(lead_table, gradients[5], lead_moment, lead_square, RATE_VECTOR, 0.0)
    return (result, in_grad, first_set[0], first_set[1], first_set[2], first_set[3], second_set[0], second_set[1], second_set[2], second_set[3], third_set[0], third_set[1], third_set[2], third_set[3], fourth_set[0], fourth_set[1], fourth_set[2], fourth_set[3], fifth_set[0], fifth_set[1], fifth_set[2], fifth_set[3], sixth_set[0], sixth_set[1], sixth_set[2], sixth_set[3])
```

```python
import functools
import math

import jax
import jax.numpy as jnp
from jax import lax
from jax.experimental import pallas as pl
from jax.experimental.pallas import tpu as pltpu
from jax.sharding import PartitionSpec as P

D = 768
FF = 3072
HEADS = 12
HEAD_DIM = 64
LEADS = 20
LAYERS = 2
WIN_MAX = 512
STEP = 10


EPSILON = 1e-06
NEGATIVE = -1e30
BETA_ONE = 0.5
BETA_TWO = 0.5
RATE_MATRIX = 0.08
RATE_VECTOR = 0.3
DECAY = 0.1
ADAM_EPSILON = 1e-08


MESH = pl.DeviceIdType.MESH
NZ, NY, NX = 4, 2, 2
CHIPS = NZ * NY * NX
SMALL = 256
PIECES = (
    (4, 48, 0, 48, 0, 128, "zxy"),
    (0, 48, 0, 48, 0, 1152, "xzy"),
    (1, 48, 0, 48, 0, 384, "yzx"),
    (2, 48, 0, 48, 0, 768, "yzx"),
    (2, 48, 0, 48, 768, 768, "zxy"),
    (3, 192, 0, 48, 0, 384, "zxy"),
    (3, 192, 48, 144, 0, 384, "zyx"),
)
WIDTHS = (2304, 768, 3072, 768, SMALL)
OWN_ROWS = (24, 24, 24, 96, 24)
AXIS = {"z": 0, "y": 1, "x": 2}


def place():
    dp, fs = lax.axis_index("dp"), lax.axis_index("fsdp")
    return lax.div(dp, NY), lax.rem(dp, NY), lax.div(fs, 2), lax.rem(fs, 2)


def device(z, y, x, core):
    return (z * NY + y, x * 2 + core)


def offsets():
    found = [
        (dz, dy, dx)
        for dz in range(1 - NZ, NZ)
        for dy in range(NY)
        for dx in range(NX)
    ]
    return sorted(found, key=lambda d: (abs(d[0]) + d[1] + d[2], abs(d[0])))


def last_axis(order, away):
    last = -1
    for number, axis in enumerate(order):
        if away[AXIS[axis]] != 0:
            last = number
    return last


def children(order, away):
    last = last_axis(order, away)
    found = []
    for number, axis in enumerate(order):
        if number < last:
            continue
        if axis == "z":
            if number > last:
                found += ["up", "down"]
            else:
                found += ["up"] if away[0] < 0 else ["down"]
        elif number > last:
            found.append(axis)
    return found


def exists(side, z):
    return {"up": z < NZ - 1, "down": z > 0}.get(side)


def neighbour(side, spot):
    z, y, x, core = spot
    return {
        "up": device(z + 1, y, x, core),
        "down": device(z - 1, y, x, core),
        "y": device(z, 1 - y, x, core),
        "x": device(z, y, 1 - x, core),
        "core": device(z, y, x, 1 - core),
    }[side]


def guarded(condition, action):
    if condition is None:
        action()
    else:
        pl.when(condition)(action)


def both(first, second):
    if first is None:
        return second
    if second is None:
        return first
    return first & second


def greet(spot):
    barrier = pltpu.get_barrier_semaphore()
    z = spot[0]
    for side in ("up", "down", "x", "y", "core"):

        def hello(side=side):
            pl.semaphore_signal(
                barrier, inc=1, device_id=neighbour(side, spot), device_id_type=MESH
            )

        guarded(exists(side, z), hello)
    count = 3 + jnp.where(z < NZ - 1, 1, 0) + jnp.where(z > 0, 1, 0)
    pl.semaphore_wait(barrier, count)


def source_of(spot, away):
    z, y, x, _ = spot
    sz = z + away[0]
    sy = 1 - y if away[1] else y
    sx = 1 - x if away[2] else x
    valid = None
    if away[0] > 0:
        valid = sz < NZ
    elif away[0] < 0:
        valid = sz >= 0
    return sz, sy, sx, valid


def chip_number(sz, sy, sx):
    return (sz * NY + sy) * NX + sx


def aligned(value, by):
    return value if isinstance(value, int) else pl.multiple_of(value, by)


def piece_view(ref, piece, chip, core):
    number, chip_rows, low, rows, column, columns, order = piece
    half = WIDTHS[number] // 2
    return ref.at[
        pl.ds(aligned(chip * chip_rows + low, 16), rows),
        pl.ds(aligned(core * half + column, 128), columns),
    ]


def gather_kernel(layer, *refs):
    masters = refs[:5]
    wholes = refs[5:10]
    mine = refs[10:15]
    theirs = refs[15:20]
    blocks = refs[20:25]
    local_sem, pair_send, pair_recv, store_sem, send_sem, recv_sem, core_send, core_recv = refs[25:]
    spot = place()
    z, y, x, core = spot
    me = chip_number(z, y, x)
    partner = neighbour("core", spot)
    loads = []
    for number in range(5):
        half = WIDTHS[number] // 2
        loads.append(
            pltpu.make_async_copy(
                masters[number].at[layer, :, pl.ds(aligned(core * half, 128), half)],
                mine[number],
                local_sem.at[number],
            )
        )
        loads[-1].start()
    greet(spot)
    swaps = []
    for number in (4, 0, 1, 2, 3):
        half = WIDTHS[number] // 2
        swap = pltpu.make_async_remote_copy(
            src_ref=masters[number].at[layer, :, pl.ds(aligned((1 - core) * half, 128), half)],
            dst_ref=theirs[number],
            send_sem=pair_send.at[number],
            recv_sem=pair_recv.at[number],
            device_id=partner,
            device_id_type=MESH,
        )
        swap.start()
        swaps.append((number, swap))

    def relay(index, away, source, view):
        piece = PIECES[index]
        for side in children(piece[6], away):

            def send(side=side):
                pltpu.make_async_remote_copy(
                    src_ref=view,
                    dst_ref=piece_view(wholes[piece[0]], piece, source, core),
                    send_sem=send_sem.at[index, ("up", "down", "x", "y").index(side)],
                    recv_sem=recv_sem.at[index, source],
                    device_id=neighbour(side, spot),
                    device_id_type=MESH,
                ).start()

            guarded(exists(side, z), send)
        pltpu.make_async_remote_copy(
            src_ref=view,
            dst_ref=piece_view(wholes[piece[0]], piece, source, core),
            send_sem=core_send.at[index],
            recv_sem=core_recv.at[index],
            device_id=partner,
            device_id_type=MESH,
        ).start()

    stores = []
    for number, swap in swaps:
        loads[number].wait()
        swap.wait_recv()
        rows = OWN_ROWS[number]
        own, other = mine[number][...], theirs[number][...]
        is_first = core == 0
        block = jnp.concatenate(
            [jnp.where(is_first, own, other), jnp.where(is_first, other, own)], axis=0
        )
        blocks[number][...] = block.astype(jnp.bfloat16)
        for index, piece in enumerate(PIECES):
            if piece[0] != number:
                continue
            view = blocks[number].at[pl.ds(piece[2], piece[3]), pl.ds(piece[4], piece[5])]
            store = pltpu.make_async_copy(
                view, piece_view(wholes[number], piece, me, core), store_sem.at[index]
            )
            store.start()
            stores.append(store)
            relay(index, (0, 0, 0), me, view)
    for away in offsets():
        if away == (0, 0, 0):
            continue
        for index, piece in enumerate(PIECES):
            sz, sy, sx, valid = source_of(spot, away)
            source = chip_number(sz, sy, sx)

            def arrival(index=index, piece=piece, source=source):
                view = piece_view(wholes[piece[0]], piece, source, core)
                pltpu.make_async_remote_copy(
                    src_ref=view,
                    dst_ref=view,
                    send_sem=send_sem.at[index, 0],
                    recv_sem=recv_sem.at[index, source],
                    device_id=partner,
                    device_id_type=MESH,
                ).wait_recv()
                relay(index, away, source, view)

            guarded(valid, arrival)
    for store in stores:
        store.wait()
    for _, swap in swaps:
        swap.wait_send()
    for index, piece in enumerate(PIECES):
        number, rows, columns = piece[0], piece[3], piece[5]

        def span(chunks, core_at):
            half = WIDTHS[number] // 2
            return wholes[number].at[
                pl.ds(0, chunks * rows), pl.ds(aligned(core_at * half + piece[4], 128), columns)
            ]

        def wait_send(chunks, sem):
            pltpu.make_async_remote_copy(
                src_ref=span(chunks, core),
                dst_ref=span(chunks, core),
                send_sem=sem,
                recv_sem=recv_sem.at[index, 0],
                device_id=partner,
                device_id_type=MESH,
            ).wait_send()

        order = piece[6]
        before = 1
        for axis in order:
            if axis == "z":
                for at in range(NZ):

                    @pl.when(z == at)
                    def _(at=at):
                        if at < NZ - 1:
                            wait_send(before * (at + 1), send_sem.at[index, 0])
                        if at > 0:
                            wait_send(before * (NZ - at), send_sem.at[index, 1])

                before *= NZ
            else:
                wait_send(before, send_sem.at[index, 2 if axis == "x" else 3])
                before *= 2
        wait_send(CHIPS, core_send.at[index])
        pltpu.make_async_remote_copy(
            src_ref=span(CHIPS, 1 - core),
            dst_ref=span(CHIPS, 1 - core),
            send_sem=core_send.at[index],
            recv_sem=core_recv.at[index],
            device_id=partner,
            device_id_type=MESH,
        ).wait_recv()


def gather_layer(layer, masters, ident):
    count = len(PIECES)
    return pl.pallas_call(
        functools.partial(gather_kernel, layer),
        out_shape=tuple(
            jax.ShapeDtypeStruct((32 * OWN_ROWS[n], WIDTHS[n]), jnp.bfloat16) for n in range(5)
        ),
        in_specs=[pl.BlockSpec(memory_space=pl.ANY)] * 5,
        out_specs=tuple([pl.BlockSpec(memory_space=pl.ANY)] * 5),
        scratch_shapes=(
            [pltpu.VMEM((OWN_ROWS[n], WIDTHS[n] // 2), jnp.float32) for n in range(5)]
            + [pltpu.VMEM((OWN_ROWS[n], WIDTHS[n] // 2), jnp.float32) for n in range(5)]
            + [pltpu.VMEM((2 * OWN_ROWS[n], WIDTHS[n] // 2), jnp.bfloat16) for n in range(5)]
            + [
                pltpu.SemaphoreType.DMA((5,)),
                pltpu.SemaphoreType.DMA((5,)),
                pltpu.SemaphoreType.DMA((5,)),
                pltpu.SemaphoreType.DMA((count,)),
                pltpu.SemaphoreType.DMA((count, 4)),
                pltpu.SemaphoreType.DMA((count, CHIPS)),
                pltpu.SemaphoreType.DMA((count,)),
                pltpu.SemaphoreType.DMA((count,)),
            ]
        ),
        name=f"gather_{layer}",
        compiler_params=pltpu.CompilerParams(
            collective_id=ident, has_side_effects=True, vmem_limit_bytes=40 << 20
        ),
    )(*masters)


def slot_of(order, side, source):
    sizes = {"z": NZ, "y": NY, "x": NX}
    base = 0
    ahead = 1
    number = 0
    for axis in order:
        at = source[AXIS[axis]]
        for here in ["up", "down"] if axis == "z" else [axis]:
            if axis == "z":
                if here == side:
                    return base + number * NZ + at
                base += ahead * NZ
            else:
                if here == side:
                    return base + number
                base += ahead
        number = number * sizes[axis] + at
        ahead *= sizes[axis]
    return base


def slot_count(order):
    return slot_of(order, None, (0, 0, 0))


def scatter_kernel(*refs):
    partials = refs[:5]
    outs = refs[5:10]
    count = len(PIECES)
    own = refs[10:15]
    pair = refs[15:20]
    total = refs[20:25]
    handed = refs[25:30]
    slots = refs[30 : 30 + count]
    (
        own_sem,
        pair_send,
        pair_recv,
        send_sem,
        recv_sem,
        end_send,
        end_recv,
        out_sem,
    ) = refs[30 + count :]
    spot = place()
    z, y, x, core = spot
    me = chip_number(z, y, x)
    partner = neighbour("core", spot)
    loads = []
    for index, piece in enumerate(PIECES):
        pass
    for number in (4, 0, 1, 2, 3):
        half = WIDTHS[number] // 2
        load = pltpu.make_async_copy(
            partials[number].at[:, pl.ds(aligned(core * half, 128), half)],
            own[number],
            own_sem.at[number],
        )
        load.start()
        loads.append(load)
    greet(spot)
    swaps = []
    for number in (4, 0, 1, 2, 3):
        half = WIDTHS[number] // 2
        swap = pltpu.make_async_remote_copy(
            src_ref=partials[number].at[:, pl.ds(aligned((1 - core) * half, 128), half)],
            dst_ref=pair[number],
            send_sem=pair_send.at[number],
            recv_sem=pair_recv.at[number],
            device_id=partner,
            device_id_type=MESH,
        )
        swap.start()
        swaps.append(swap)
    ready = set()
    sides = ("up", "down", "x", "y")
    for away in reversed(offsets()):
        for index, piece in enumerate(PIECES):
            number, chip_rows, low, rows, column, columns, order = piece
            if number not in ready:
                ready.add(number)
                at = (4, 0, 1, 2, 3).index(number)
                loads[at].wait()
                swaps[at].wait_recv()
            sz, sy, sx, valid = source_of(spot, away)
            source = chip_number(sz, sy, sx)
            last = last_axis(order, away)

            def event(
                index=index, number=number, chip_rows=chip_rows, low=low, rows=rows,
                column=column, columns=columns, order=order, source=source, last=last,
                where=(sz, sy, sx),
            ):
                kids = children(order, away)
                for side in kids:

                    def arrived(side=side):
                        slot = slot_of(order, side, where)
                        pltpu.make_async_remote_copy(
                            src_ref=slots[index].at[slot],
                            dst_ref=slots[index].at[slot],
                            send_sem=send_sem.at[index, 0],
                            recv_sem=recv_sem.at[index, slot],
                            device_id=partner,
                            device_id_type=MESH,
                        ).wait_recv()

                    guarded(exists(side, z), arrived)
                view = (pl.ds(aligned(source * chip_rows + low, 16), rows), pl.ds(column, columns))
                value = own[number][view].astype(jnp.float32) + pair[number][view].astype(jnp.float32)
                for side in kids:
                    landed = slots[index][slot_of(order, side, where)].astype(jnp.float32)
                    there = exists(side, z)
                    value = value + (landed if there is None else jnp.where(there, landed, 0.0))
                if last < 0:
                    total[number][pl.ds(low, rows), pl.ds(column, columns)] = value
                    return
                pair[number][view] = value.astype(jnp.bfloat16)
                axis = order[last]
                if axis == "z":
                    side = "up" if away[0] < 0 else "down"
                    parent = neighbour("down" if away[0] < 0 else "up", spot)
                else:
                    side = axis
                    parent = neighbour(axis, spot)
                slot = slot_of(order, side, where)
                pltpu.make_async_remote_copy(
                    src_ref=pair[number].at[view],
                    dst_ref=slots[index].at[slot],
                    send_sem=send_sem.at[index, source],
                    recv_sem=recv_sem.at[index, slot],
                    device_id=parent,
                    device_id_type=MESH,
                ).start()

            guarded(valid, event)
    ends = []
    for number in range(5):
        rows = OWN_ROWS[number]
        end = pltpu.make_async_remote_copy(
            src_ref=total[number].at[pl.ds(aligned((1 - core) * rows, 8), rows)],
            dst_ref=handed[number],
            send_sem=end_send.at[number],
            recv_sem=end_recv.at[number],
            device_id=partner,
            device_id_type=MESH,
        )
        end.start()
        ends.append(end)
    writes = []
    for number in range(5):
        rows = OWN_ROWS[number]
        half = WIDTHS[number] // 2
        write = pltpu.make_async_copy(
            total[number].at[pl.ds(aligned(core * rows, 8), rows)],
            outs[number].at[:, pl.ds(aligned(core * half, 128), half)],
            out_sem.at[number],
        )
        write.start()
        writes.append(write)
    for number in range(5):
        half = WIDTHS[number] // 2
        ends[number].wait_recv()
        write = pltpu.make_async_copy(
            handed[number],
            outs[number].at[:, pl.ds(aligned((1 - core) * half, 128), half)],
            out_sem.at[5 + number],
        )
        write.start()
        writes.append(write)
    for write in writes:
        write.wait()
    for end in ends:
        end.wait_send()
    for swap in swaps:
        swap.wait_send()
    for index, piece in enumerate(PIECES):
        number, chip_rows, low, rows, column, columns, order = piece
        for away in offsets():
            if away == (0, 0, 0):
                continue
            sz, sy, sx, valid = source_of(spot, away)
            source = chip_number(sz, sy, sx)

            def sent(index=index, source=source):
                view = (pl.ds(aligned(source * chip_rows + low, 16), rows), pl.ds(column, columns))
                pltpu.make_async_remote_copy(
                    src_ref=pair[number].at[view],
                    dst_ref=slots[index].at[0],
                    send_sem=send_sem.at[index, source],
                    recv_sem=recv_sem.at[index, 0],
                    device_id=partner,
                    device_id_type=MESH,
                ).wait_send()

            guarded(valid, sent)


def scatter_layer(layer, partials, ident):
    count = len(PIECES)
    most = max(slot_count(p[6]) for p in PIECES)
    return pl.pallas_call(
        scatter_kernel,
        out_shape=tuple(
            jax.ShapeDtypeStruct((OWN_ROWS[n], WIDTHS[n]), jnp.float32) for n in range(5)
        ),
        in_specs=[pl.BlockSpec(memory_space=pl.ANY)] * 5,
        out_specs=tuple([pl.BlockSpec(memory_space=pl.ANY)] * 5),
        scratch_shapes=(
            [pltpu.VMEM((32 * OWN_ROWS[n], WIDTHS[n] // 2), jnp.bfloat16) for n in range(5)]
            + [pltpu.VMEM((32 * OWN_ROWS[n], WIDTHS[n] // 2), jnp.bfloat16) for n in range(5)]
            + [pltpu.VMEM((2 * OWN_ROWS[n], WIDTHS[n] // 2), jnp.float32) for n in range(5)]
            + [pltpu.VMEM((OWN_ROWS[n], WIDTHS[n] // 2), jnp.float32) for n in range(5)]
            + [pltpu.VMEM((slot_count(p[6]), p[3], p[5]), jnp.bfloat16) for p in PIECES]
            + [
                pltpu.SemaphoreType.DMA((5,)),
                pltpu.SemaphoreType.DMA((5,)),
                pltpu.SemaphoreType.DMA((5,)),
                pltpu.SemaphoreType.DMA((count, CHIPS)),
                pltpu.SemaphoreType.DMA((count, most)),
                pltpu.SemaphoreType.DMA((5,)),
                pltpu.SemaphoreType.DMA((5,)),
                pltpu.SemaphoreType.DMA((10,)),
            ]
        ),
        name=f"scatter_{layer}",
        compiler_params=pltpu.CompilerParams(
            collective_id=ident, has_side_effects=True, vmem_limit_bytes=56 << 20
        ),
    )(*partials)


def with_halo(cells, sides, width):
    for axis, dim in sides:
        count = lax.axis_size(axis)
        ends = count - 1
        head = lax.slice_in_dim(cells, 0, width, axis=dim)
        tail = lax.slice_in_dim(cells, cells.shape[dim] - width, cells.shape[dim], axis=dim)
        cells = jnp.concatenate(
            [
                lax.ppermute(tail, axis, [(i, (i + 1) % count) for i in range(ends)]),
                cells,
                lax.ppermute(head, axis, [((i + 1) % count, i) for i in range(ends)]),
            ],
            axis=dim,
        )
    return cells


def passed_along(value, axis, by):
    size = lax.axis_size(axis)
    pairs = [(i, i + by) for i in range(size) if 0 <= i + by < size]
    return lax.ppermute(value, axis, pairs)


def normalize(values):
    centred = values - jnp.mean(values, axis=-1, keepdims=True)
    inverse = lax.rsqrt(jnp.mean(centred * centred, axis=-1, keepdims=True) + EPSILON)
    return (centred * inverse, inverse)


def normalize_back(grad_normed, normed, inverse):
    return inverse * (
        grad_normed
        - jnp.mean(grad_normed, axis=-1, keepdims=True)
        - normed * jnp.mean(grad_normed * normed, axis=-1, keepdims=True)
    )


def rotary_tables(relative):
    indices = jnp.arange(HEAD_DIM // 2).astype(jnp.float32)
    frequency = jnp.exp(indices * (-2.0 * math.log(10000.0) / HEAD_DIM))
    phase = relative.astype(jnp.float32)[:, None] * frequency[None, :]
    return (jnp.cos(phase)[:, None, :], jnp.sin(phase)[:, None, :])


def rotate(field, cosine_table, sine_table):
    half_dim = field.shape[-1] // 2
    first_half = field[..., :half_dim]
    second = field[..., half_dim:]
    return jnp.concatenate(
        [
            first_half * cosine_table - second * sine_table,
            second * cosine_table + first_half * sine_table,
        ],
        axis=-1,
    )


def rotate_back(field, cosine_table, sine_table):
    half_dim = field.shape[-1] // 2
    first_half = field[..., :half_dim]
    second = field[..., half_dim:]
    return jnp.concatenate(
        [
            first_half * cosine_table + second * sine_table,
            second * cosine_table - first_half * sine_table,
        ],
        axis=-1,
    )


def direct():
    return lax.axis_size("dp") == NZ * NY and lax.axis_size("fsdp") == NX * 2


def pack_small(bias, table):
    flat = jnp.concatenate([bias.reshape(LAYERS, -1), table.reshape(LAYERS, -1)], axis=1)
    flat = jnp.pad(flat, ((0, 0), (0, OWN_ROWS[4] * SMALL - flat.shape[1])))
    return flat.reshape(LAYERS, OWN_ROWS[4], SMALL)


def unpack_small(whole):
    count = lax.axis_size("dp") * lax.axis_size("fsdp")
    flat = whole.reshape(count, -1)
    wide = 9 * D // count
    bias = flat[:, :wide].reshape(count, 9, -1).transpose(1, 0, 2).reshape(9, D)
    table = flat[:, wide : wide + LEADS * 4 * D // count].reshape(count, LEADS, -1)
    return bias, table.transpose(1, 0, 2).reshape(LEADS, 4 * D)


def fetch_layers(masters):
    if direct():
        packed = tuple(masters[:4]) + (pack_small(masters[4], masters[5]),)
        layers = []
        for layer in range(LAYERS):
            whole = gather_layer(layer, packed, layer)
            layers.append(tuple(whole[:4]) + unpack_small(whole[4]))
        return layers
    both_axes = ("dp", "fsdp")
    layers = []
    for layer in range(LAYERS):
        low = [m[layer].astype(jnp.bfloat16) for m in masters]
        layers.append(
            tuple(lax.all_gather(low[n], both_axes, axis=0, tiled=True) for n in range(4))
            + tuple(lax.all_gather(low[n], both_axes, axis=1, tiled=True) for n in (4, 5))
        )
    return layers


def reduce_layer(layer, gradients):
    both_axes = ("dp", "fsdp")
    if direct():
        count = lax.axis_size("dp") * lax.axis_size("fsdp")
        bias, table = gradients[4], gradients[5]
        flat = jnp.concatenate(
            [
                bias.reshape(9, count, -1).transpose(1, 0, 2).reshape(count, -1),
                table.reshape(LEADS, count, -1).transpose(1, 0, 2).reshape(count, -1),
            ],
            axis=1,
        )
        used = flat.shape[1]
        small = jnp.pad(flat, ((0, 0), (0, OWN_ROWS[4] * SMALL - used))).reshape(-1, SMALL)
        partials = tuple(g.astype(jnp.bfloat16) for g in (*gradients[:4], small))
        summed = scatter_layer(layer, partials, LAYERS + layer)
        flat = summed[4].reshape(-1)
        wide = 9 * D // count
        return tuple(summed[:4]) + (
            flat[:wide].reshape(9, -1),
            flat[wide:used].reshape(LEADS, -1),
        )
    return tuple(
        lax.psum_scatter(gradients[n], both_axes, scatter_dimension=0 if n < 4 else 1, tiled=True)
        for n in range(6)
    )


def build_masks(segment_ids, padding_mask, offset, row_count):
    block_size = min(512, row_count)
    band_size = block_size + 2 * WIN_MAX
    filler = jnp.full((WIN_MAX,), -1, jnp.int32)
    nothing = jnp.zeros((WIN_MAX,), jnp.int32)
    segment_wide = lax.dynamic_slice_in_dim(
        jnp.concatenate([filler, segment_ids, filler]), offset, row_count + 2 * WIN_MAX
    )
    live_wide = lax.dynamic_slice_in_dim(
        jnp.concatenate([nothing, padding_mask, nothing]), offset, row_count + 2 * WIN_MAX
    )
    segment_own = lax.dynamic_slice_in_dim(segment_ids, offset, row_count)
    diagonal = jnp.arange(block_size)[:, None] + WIN_MAX == jnp.arange(band_size)[None, :]
    block_masks = [
        (segment_own[:, None] == segment_wide[None, :]) & (live_wide[None, :] == 1) | diagonal
    ]
    return block_masks


def block_scores(query_block, key_block, allowed):
    raw_scores = jnp.einsum(
        "qhd,khd->hqk", query_block, key_block, preferred_element_type=jnp.float32
    ) * HEAD_DIM ** (-0.5)
    return jnp.where(allowed[None, :, :], raw_scores, NEGATIVE)


def attend_forward(queries, extended, block_masks):
    block_size = block_masks[0].shape[0]
    band_size = block_masks[0].shape[1]
    outputs = []
    log_totals = []
    for block_index, allowed in enumerate(block_masks):
        low_edge = block_index * block_size
        key_block = extended[low_edge : low_edge + band_size, :D].reshape(
            band_size, HEADS, HEAD_DIM
        )
        value_block = extended[low_edge : low_edge + band_size, D:].reshape(
            band_size, HEADS, HEAD_DIM
        )
        masked = block_scores(queries, key_block, allowed)
        row_peak = jnp.max(masked, axis=-1, keepdims=True)
        log_total = row_peak + jnp.log(jnp.sum(jnp.exp(masked - row_peak), axis=-1, keepdims=True))
        weights = jnp.exp(masked - log_total).astype(jnp.bfloat16)
        outputs.append(
            jnp.einsum("hqk,khd->qhd", weights, value_block, preferred_element_type=jnp.float32)
        )
        log_totals.append(log_total)
    return (outputs[0], log_totals)


def attend_backward(queries, extended, log_totals, grad_attended, block_masks):
    block_size = block_masks[0].shape[0]
    band_size = block_masks[0].shape[1]
    grad_queries = []
    grad_extended = jnp.zeros((extended.shape[0], 2 * D), jnp.float32)
    for block_index, allowed in enumerate(block_masks):
        low_edge = block_index * block_size
        key_block = extended[low_edge : low_edge + band_size, :D].reshape(
            band_size, HEADS, HEAD_DIM
        )
        value_block = extended[low_edge : low_edge + band_size, D:].reshape(
            band_size, HEADS, HEAD_DIM
        )
        masked = block_scores(queries, key_block, allowed)
        probabilities = jnp.exp(masked - log_totals[block_index])
        weights = probabilities.astype(jnp.bfloat16)
        grad_weights = jnp.einsum(
            "qhd,khd->hqk", grad_attended, value_block, preferred_element_type=jnp.float32
        )
        row_delta = jnp.sum(probabilities * grad_weights, axis=-1, keepdims=True)
        grad_scores = (probabilities * (grad_weights - row_delta)).astype(jnp.bfloat16)
        grad_queries.append(
            jnp.einsum("hqk,khd->qhd", grad_scores, key_block, preferred_element_type=jnp.float32)
            * HEAD_DIM ** (-0.5)
        )
        grad_keys = jnp.einsum(
            "hqk,qhd->khd", grad_scores, queries, preferred_element_type=jnp.float32
        ) * HEAD_DIM ** (-0.5)
        grad_values = jnp.einsum(
            "hqk,qhd->khd", weights, grad_attended, preferred_element_type=jnp.float32
        )
        grad_extended = grad_extended.at[low_edge : low_edge + band_size].add(
            jnp.concatenate(
                [grad_keys.reshape(band_size, D), grad_values.reshape(band_size, D)], axis=1
            )
        )
    return (grad_queries[0], grad_extended)


def forward_layer(stream, gathered, context):
    in_full, out_full, expand_full, shrink_full, bias_full, table_full = gathered
    cosine_table, sine_table, block_masks, lead_row, lead_hot = context
    biases = bias_full.astype(jnp.float32).reshape(-1)
    modulation = lax.dynamic_index_in_dim(table_full, lead_row, 0, keepdims=False).astype(
        jnp.float32
    )
    shift_one = modulation[:D]
    scale_one = modulation[D : 2 * D]
    shift_two = modulation[2 * D : 3 * D]
    scale_two = modulation[3 * D :]
    normed_one, inverse_one = normalize(stream)
    input_one = (normed_one * (1.0 + scale_one) + shift_one).astype(jnp.bfloat16)
    projected = jnp.dot(input_one, in_full, preferred_element_type=jnp.float32) + biases[: 3 * D]
    queries = rotate(
        projected[:, :D].reshape(-1, HEADS, HEAD_DIM), cosine_table, sine_table
    ).astype(jnp.bfloat16)
    rotated_keys = rotate(
        projected[:, D : 2 * D].reshape(-1, HEADS, HEAD_DIM), cosine_table, sine_table
    ).astype(jnp.bfloat16)
    values = projected[:, 2 * D :].astype(jnp.bfloat16)
    extended = with_halo(
        jnp.concatenate([rotated_keys.reshape(-1, D), values], axis=1), (("fsdp", 0),), WIN_MAX
    )
    attended, log_totals = attend_forward(queries, extended, block_masks)
    attended = attended.reshape(-1, D).astype(jnp.bfloat16)
    middle = stream + (
        jnp.dot(attended, out_full, preferred_element_type=jnp.float32) + biases[3 * D : 4 * D]
    )
    normed_two, inverse_two = normalize(middle)
    input_two = (normed_two * (1.0 + scale_two) + shift_two).astype(jnp.bfloat16)
    hidden = (
        jnp.dot(input_two, expand_full, preferred_element_type=jnp.float32)
        + biases[4 * D : 4 * D + FF]
    )
    active = jax.nn.gelu(hidden, approximate=False).astype(jnp.bfloat16)
    result = middle + (
        jnp.dot(active, shrink_full, preferred_element_type=jnp.float32) + biases[4 * D + FF :]
    )
    saved_values = (
        normed_one,
        inverse_one,
        input_one,
        queries,
        extended,
        log_totals,
        attended,
        normed_two,
        inverse_two,
        input_two,
        hidden,
        active,
        modulation,
    )
    return (result, saved_values)


def backward_layer(grad_stream, gathered, saved_values, context):
    in_full, out_full, expand_full, shrink_full, bias_full, table_full = gathered
    cosine_table, sine_table, block_masks, lead_row, lead_hot = context
    (
        normed_one,
        inverse_one,
        input_one,
        queries,
        extended,
        log_totals,
        attended,
        normed_two,
        inverse_two,
        input_two,
        hidden,
        active,
        modulation,
    ) = saved_values
    row_count = grad_stream.shape[0]
    scale_one = modulation[D : 2 * D]
    scale_two = modulation[3 * D :]
    grad_low = grad_stream.astype(jnp.bfloat16)
    grad_shrink = jnp.einsum("tf,td->fd", active, grad_low, preferred_element_type=jnp.float32)
    bias_shrink = jnp.sum(grad_low.astype(jnp.float32), axis=0)
    grad_active = jnp.einsum("td,fd->tf", grad_low, shrink_full, preferred_element_type=jnp.float32)
    gelu_value, gelu_pull = jax.vjp(
        lambda hidden_in: jax.nn.gelu(hidden_in, approximate=False), hidden
    )
    grad_hidden = gelu_pull(grad_active)[0].astype(jnp.bfloat16)
    grad_expand = jnp.einsum(
        "tc,tf->cf", input_two, grad_hidden, preferred_element_type=jnp.float32
    )
    bias_expand = jnp.sum(grad_hidden.astype(jnp.float32), axis=0)
    grad_input_two = jnp.einsum(
        "tf,cf->tc", grad_hidden, expand_full, preferred_element_type=jnp.float32
    )
    shift_two_grad = jnp.sum(grad_input_two, axis=0)
    scale_two_grad = jnp.sum(grad_input_two * normed_two, axis=0)
    grad_middle = grad_stream + normalize_back(
        grad_input_two * (1.0 + scale_two), normed_two, inverse_two
    )
    middle_low = grad_middle.astype(jnp.bfloat16)
    grad_output = jnp.einsum("te,td->ed", attended, middle_low, preferred_element_type=jnp.float32)
    bias_output = jnp.sum(middle_low.astype(jnp.float32), axis=0)
    grad_attended = jnp.einsum(
        "td,ed->te", middle_low, out_full, preferred_element_type=jnp.float32
    )
    grad_attended = grad_attended.astype(jnp.bfloat16).reshape(row_count, HEADS, HEAD_DIM)
    grad_queries, grad_extended = attend_backward(
        queries, extended, log_totals, grad_attended, block_masks
    )
    lower_rim = grad_extended[:WIN_MAX]
    upper_rim = grad_extended[WIN_MAX + row_count :]
    from_above = passed_along(lower_rim.astype(jnp.bfloat16), "fsdp", -1).astype(lower_rim.dtype)
    from_below = passed_along(upper_rim.astype(jnp.bfloat16), "fsdp", 1).astype(upper_rim.dtype)
    own_rows = grad_extended[WIN_MAX : WIN_MAX + row_count]
    own_rows = own_rows.at[:WIN_MAX].add(from_below)
    own_rows = own_rows.at[row_count - WIN_MAX :].add(from_above)
    grad_query_pre = rotate_back(grad_queries, cosine_table, sine_table).reshape(row_count, D)
    grad_key_pre = rotate_back(
        own_rows[:, :D].reshape(row_count, HEADS, HEAD_DIM), cosine_table, sine_table
    ).reshape(row_count, D)
    grad_projected = jnp.concatenate(
        [grad_query_pre, grad_key_pre, own_rows[:, D:]], axis=1
    ).astype(jnp.bfloat16)
    grad_input = jnp.einsum(
        "tc,te->ce", input_one, grad_projected, preferred_element_type=jnp.float32
    )
    bias_input = jnp.sum(grad_projected.astype(jnp.float32), axis=0)
    grad_input_one = jnp.einsum(
        "te,ce->tc", grad_projected, in_full, preferred_element_type=jnp.float32
    )
    shift_one_grad = jnp.sum(grad_input_one, axis=0)
    scale_one_grad = jnp.sum(grad_input_one * normed_one, axis=0)
    grad_before = grad_middle + normalize_back(
        grad_input_one * (1.0 + scale_one), normed_one, inverse_one
    )
    grad_bias = jnp.concatenate([bias_input, bias_output, bias_expand, bias_shrink]).reshape(-1, D)
    grad_table = (
        lead_hot[:, None]
        * jnp.concatenate([shift_one_grad, scale_one_grad, shift_two_grad, scale_two_grad])[None, :]
    )
    return (grad_before, (grad_input, grad_output, grad_expand, grad_shrink, grad_bias, grad_table))


def adam_update(weight, gradient, moment, square, step_rate, decay_rate):
    moment = BETA_ONE * moment + (1.0 - BETA_ONE) * gradient
    square = BETA_TWO * square + (1.0 - BETA_TWO) * gradient * gradient
    first_fix = 1.0 - BETA_ONE**STEP
    second_fix = 1.0 - BETA_TWO**STEP
    update = moment / first_fix / (jnp.sqrt(square / second_fix) + ADAM_EPSILON)
    weight = weight - step_rate * (update + decay_rate * weight)
    return (weight, moment, square, weight.astype(jnp.bfloat16))


def shards(
    tokens,
    cotangent,
    segment_ids,
    segment_starts,
    padding_mask,
    lead_index,
    input_weights,
    input_moment,
    input_square,
    output_weights,
    output_moment,
    output_square,
    expand_weights,
    expand_moment,
    expand_square,
    shrink_weights,
    shrink_moment,
    shrink_square,
    bias_vector,
    bias_moment,
    bias_square,
    lead_table,
    lead_moment,
    lead_square,
):
    row_count = tokens.shape[0]
    offset = lax.axis_index("fsdp") * row_count
    block_masks = build_masks(segment_ids, padding_mask, offset, row_count)
    own_starts = lax.dynamic_slice_in_dim(segment_starts, offset, row_count)
    relative = offset + jnp.arange(row_count, dtype=jnp.int32) - own_starts
    cosine_table, sine_table = rotary_tables(relative)
    lead_row = lead_index[0]
    lead_hot = (jnp.arange(LEADS, dtype=jnp.int32) == lead_row).astype(jnp.float32)
    context = (cosine_table, sine_table, block_masks, lead_row, lead_hot)
    masters = (
        input_weights,
        output_weights,
        expand_weights,
        shrink_weights,
        bias_vector,
        lead_table,
    )
    stream = tokens.astype(jnp.float32)
    saved_layers = []
    gathered_layers = fetch_layers(masters)
    for layer_index in range(LAYERS):
        gathered = gathered_layers[layer_index]
        stream, saved_values = forward_layer(stream, gathered, context)
        saved_layers.append(saved_values)
    grad_stream = cotangent.astype(jnp.float32)
    reduced_layers = [None] * LAYERS
    for layer_index in reversed(range(LAYERS)):
        gathered = gathered_layers[layer_index]
        grad_stream, layer_grads = backward_layer(
            grad_stream, gathered, saved_layers[layer_index], context
        )
        reduced_layers[layer_index] = reduce_layer(layer_index, layer_grads)
    moments = (input_moment, output_moment, expand_moment, shrink_moment, bias_moment, lead_moment)
    squares = (input_square, output_square, expand_square, shrink_square, bias_square, lead_square)
    results = []
    for number in range(6):
        stacked = jnp.stack([reduced_layers[layer_index][number] for layer_index in range(LAYERS)])
        step_rate = RATE_MATRIX if number < 4 else RATE_VECTOR
        decay_rate = DECAY if number < 4 else 0.0
        results.append(
            adam_update(
                masters[number], stacked, moments[number], squares[number], step_rate, decay_rate
            )
        )
    return (
        stream,
        grad_stream,
        results[0][0],
        results[0][1],
        results[0][2],
        results[0][3],
        results[1][0],
        results[1][1],
        results[1][2],
        results[1][3],
        results[2][0],
        results[2][1],
        results[2][2],
        results[2][3],
        results[3][0],
        results[3][1],
        results[3][2],
        results[3][3],
        results[4][0],
        results[4][1],
        results[4][2],
        results[4][3],
        results[5][0],
        results[5][1],
        results[5][2],
        results[5][3],
    )


def solution(mesh):
    return jax.shard_map(
        shards,
        mesh=mesh,
        in_specs=(
            P(("dp", "fsdp"), None),
            P(("dp", "fsdp"), None),
            P("dp"),
            P("dp"),
            P("dp"),
            P("dp"),
            P(None, ("dp", "fsdp"), None),
            P(None, ("dp", "fsdp"), None),
            P(None, ("dp", "fsdp"), None),
            P(None, ("dp", "fsdp"), None),
            P(None, ("dp", "fsdp"), None),
            P(None, ("dp", "fsdp"), None),
            P(None, ("dp", "fsdp"), None),
            P(None, ("dp", "fsdp"), None),
            P(None, ("dp", "fsdp"), None),
            P(None, ("dp", "fsdp"), None),
            P(None, ("dp", "fsdp"), None),
            P(None, ("dp", "fsdp"), None),
            P(None, None, ("dp", "fsdp")),
            P(None, None, ("dp", "fsdp")),
            P(None, None, ("dp", "fsdp")),
            P(None, None, ("dp", "fsdp")),
            P(None, None, ("dp", "fsdp")),
            P(None, None, ("dp", "fsdp")),
        ),
        out_specs=(
            P(("dp", "fsdp"), None),
            P(("dp", "fsdp"), None),
            P(None, ("dp", "fsdp"), None),
            P(None, ("dp", "fsdp"), None),
            P(None, ("dp", "fsdp"), None),
            P(None, ("dp", "fsdp"), None),
            P(None, ("dp", "fsdp"), None),
            P(None, ("dp", "fsdp"), None),
            P(None, ("dp", "fsdp"), None),
            P(None, ("dp", "fsdp"), None),
            P(None, ("dp", "fsdp"), None),
            P(None, ("dp", "fsdp"), None),
            P(None, ("dp", "fsdp"), None),
            P(None, ("dp", "fsdp"), None),
            P(None, ("dp", "fsdp"), None),
            P(None, ("dp", "fsdp"), None),
            P(None, ("dp", "fsdp"), None),
            P(None, ("dp", "fsdp"), None),
            P(None, None, ("dp", "fsdp")),
            P(None, None, ("dp", "fsdp")),
            P(None, None, ("dp", "fsdp")),
            P(None, None, ("dp", "fsdp")),
            P(None, None, ("dp", "fsdp")),
            P(None, None, ("dp", "fsdp")),
            P(None, None, ("dp", "fsdp")),
            P(None, None, ("dp", "fsdp")),
        ),
        check_vma=False,
    )
```

```python
import functools
import math

import jax
import jax.numpy as jnp
from jax import lax
from jax.experimental import pallas as pl
from jax.experimental.pallas import tpu as pltpu
from jax.sharding import PartitionSpec as P

D = 768
FF = 3072
HEADS = 12
HEAD_DIM = 64
LEADS = 20
LAYERS = 2
WIN_MAX = 512
STEP = 10
LATER_OFFLOADED = True

EPSILON = 1e-06
NEGATIVE = -1e30
BETA_ONE = 0.5
BETA_TWO = 0.5
RATE_MATRIX = 0.08
RATE_VECTOR = 0.3
DECAY = 0.1
ADAM_EPSILON = 1e-08

MESH = pl.DeviceIdType.MESH
NZ, NY, NX = 4, 2, 2
CHIPS = NZ * NY * NX
SMALL = 256
PIECES = (
    (4, 2, 0, 48, 0, 48, 0, 128, "zxy"),
    (0, 0, 0, 48, 0, 48, 0, 1152, "xzy"),
    (1, 0, 2304, 48, 0, 48, 0, 384, "yzx"),
    (2, 0, 3072, 48, 0, 48, 0, 768, "yzx"),
    (2, 0, 3072, 48, 0, 48, 768, 768, "zxy"),
    (3, 1, 0, 192, 0, 48, 0, 384, "zxy"),
    (3, 1, 0, 192, 48, 144, 0, 384, "zyx"),
)
WIDTHS = (2304, 768, 3072, 768, SMALL)
OWN_ROWS = (24, 24, 24, 96, 24)
WHOLES = ((768, 6144), (3072, 768), (768, SMALL))
AXIS = {"z": 0, "y": 1, "x": 2}


def place():
    dp, fs = lax.axis_index("dp"), lax.axis_index("fsdp")
    return lax.div(dp, NY), lax.rem(dp, NY), lax.div(fs, 2), lax.rem(fs, 2)


def device(z, y, x, core):
    return (z * NY + y, x * 2 + core)


def offsets():
    found = [
        (dz, dy, dx)
        for dz in range(1 - NZ, NZ)
        for dy in range(NY)
        for dx in range(NX)
    ]
    return sorted(found, key=lambda d: (abs(d[0]) + d[1] + d[2], abs(d[0])))


def last_axis(order, away):
    last = -1
    for number, axis in enumerate(order):
        if away[AXIS[axis]] != 0:
            last = number
    return last


def children(order, away):
    last = last_axis(order, away)
    found = []
    for number, axis in enumerate(order):
        if number < last:
            continue
        if axis == "z":
            if number > last:
                found += ["up", "down"]
            else:
                found += ["up"] if away[0] < 0 else ["down"]
        elif number > last:
            found.append(axis)
    return found


def exists(side, z):
    return {"up": z < NZ - 1, "down": z > 0}.get(side)


def neighbour(side, spot):
    z, y, x, core = spot
    return {
        "up": device(z + 1, y, x, core),
        "down": device(z - 1, y, x, core),
        "y": device(z, 1 - y, x, core),
        "x": device(z, y, 1 - x, core),
        "core": device(z, y, x, 1 - core),
    }[side]


def guarded(condition, action):
    if condition is None:
        action()
    else:
        pl.when(condition)(action)


def both(first, second):
    if first is None:
        return second
    if second is None:
        return first
    return first & second


def greet(spot):
    barrier = pltpu.get_barrier_semaphore()
    z = spot[0]
    for side in ("up", "down", "x", "y", "core"):

        def hello(side=side):
            pl.semaphore_signal(
                barrier, inc=1, device_id=neighbour(side, spot), device_id_type=MESH
            )

        guarded(exists(side, z), hello)
    count = 3 + jnp.where(z < NZ - 1, 1, 0) + jnp.where(z > 0, 1, 0)
    pl.semaphore_wait(barrier, count)


def source_of(spot, away):
    z, y, x, _ = spot
    sz = z + away[0]
    sy = 1 - y if away[1] else y
    sx = 1 - x if away[2] else x
    valid = None
    if away[0] > 0:
        valid = sz < NZ
    elif away[0] < 0:
        valid = sz >= 0
    return sz, sy, sx, valid


def chip_number(sz, sy, sx):
    return (sz * NY + sy) * NX + sx


def aligned(value, by):
    return value if isinstance(value, int) else pl.multiple_of(value, by)


def piece_view(ref, piece, chip, core):
    number, _, base, chip_rows, low, rows, column, columns, _ = piece
    half = WIDTHS[number] // 2
    return ref.at[
        pl.ds(aligned(chip * chip_rows + low, 16), rows),
        pl.ds(aligned(base + core * half + column, 128), columns),
    ]


def gather_kernel(layer, numbers, pieces, *refs):
    count = len(numbers)
    arrays = 3 if 4 in numbers else 2
    take = iter(refs)
    masters = dict(zip(numbers, [next(take) for _ in range(count)]))
    wholes = [next(take) for _ in range(arrays)]
    mine = dict(zip(numbers, [next(take) for _ in range(count)]))
    theirs = dict(zip(numbers, [next(take) for _ in range(count)]))
    blocks = dict(zip(numbers, [next(take) for _ in range(count)]))
    local_sem, pair_send, pair_recv, store_sem, send_sem, recv_sem, core_send, core_recv = take
    spot = place()
    z, y, x, core = spot
    me = chip_number(z, y, x)
    partner = neighbour("core", spot)
    loads = {}
    for number in numbers:
        half = WIDTHS[number] // 2
        loads[number] = pltpu.make_async_copy(
            masters[number].at[0 if number == 4 else layer, :, pl.ds(aligned(core * half, 128), half)],
            mine[number],
            local_sem.at[number],
        )
        loads[number].start()
    greet(spot)
    swaps = []
    for number in numbers:
        half = WIDTHS[number] // 2
        swap = pltpu.make_async_remote_copy(
            src_ref=masters[number].at[0 if number == 4 else layer, :, pl.ds(aligned((1 - core) * half, 128), half)],
            dst_ref=theirs[number],
            send_sem=pair_send.at[number],
            recv_sem=pair_recv.at[number],
            device_id=partner,
            device_id_type=MESH,
        )
        swap.start()
        swaps.append((number, swap))

    def relay(index, away, source, view):
        piece = pieces[index]
        for side in children(piece[8], away):

            def send(side=side):
                pltpu.make_async_remote_copy(
                    src_ref=view,
                    dst_ref=piece_view(wholes[piece[1]], piece, source, core),
                    send_sem=send_sem.at[index, ("up", "down", "x", "y").index(side)],
                    recv_sem=recv_sem.at[index, source],
                    device_id=neighbour(side, spot),
                    device_id_type=MESH,
                ).start()

            guarded(exists(side, z), send)
        pltpu.make_async_remote_copy(
            src_ref=view,
            dst_ref=piece_view(wholes[piece[1]], piece, source, core),
            send_sem=core_send.at[index],
            recv_sem=core_recv.at[index],
            device_id=partner,
            device_id_type=MESH,
        ).start()

    stores = []
    for number, swap in swaps:
        loads[number].wait()
        swap.wait_recv()
        rows = OWN_ROWS[number]
        own, other = mine[number][...], theirs[number][...]
        is_first = core == 0
        block = jnp.concatenate(
            [jnp.where(is_first, own, other), jnp.where(is_first, other, own)], axis=0
        )
        blocks[number][...] = block.astype(jnp.bfloat16)
        for index, piece in enumerate(pieces):
            if piece[0] != number:
                continue
            view = blocks[number].at[pl.ds(piece[4], piece[5]), pl.ds(piece[6], piece[7])]
            store = pltpu.make_async_copy(
                view, piece_view(wholes[piece[1]], piece, me, core), store_sem.at[index]
            )
            store.start()
            stores.append(store)
            relay(index, (0, 0, 0), me, view)
    for away in offsets():
        if away == (0, 0, 0):
            continue
        for index, piece in enumerate(pieces):
            sz, sy, sx, valid = source_of(spot, away)
            source = chip_number(sz, sy, sx)

            def arrival(index=index, piece=piece, source=source):
                view = piece_view(wholes[piece[1]], piece, source, core)
                pltpu.make_async_remote_copy(
                    src_ref=view,
                    dst_ref=view,
                    send_sem=send_sem.at[index, 0],
                    recv_sem=recv_sem.at[index, source],
                    device_id=partner,
                    device_id_type=MESH,
                ).wait_recv()
                relay(index, away, source, view)

            guarded(valid, arrival)
    for store in stores:
        store.wait()
    for _, swap in swaps:
        swap.wait_send()
    for index, piece in enumerate(pieces):
        number, rows, columns = piece[0], piece[5], piece[7]

        def span(chunks, core_at):
            half = WIDTHS[number] // 2
            start = aligned(piece[2] + core_at * half + piece[6], 128)
            return wholes[piece[1]].at[pl.ds(0, chunks * rows), pl.ds(start, columns)]

        def wait_send(chunks, sem):
            pltpu.make_async_remote_copy(
                src_ref=span(chunks, core),
                dst_ref=span(chunks, core),
                send_sem=sem,
                recv_sem=recv_sem.at[index, 0],
                device_id=partner,
                device_id_type=MESH,
            ).wait_send()

        order = piece[8]
        before = 1
        for axis in order:
            if axis == "z":
                for at in range(NZ):

                    @pl.when(z == at)
                    def _(at=at):
                        if at < NZ - 1:
                            wait_send(before * (at + 1), send_sem.at[index, 0])
                        if at > 0:
                            wait_send(before * (NZ - at), send_sem.at[index, 1])

                before *= NZ
            else:
                wait_send(before, send_sem.at[index, 2 if axis == "x" else 3])
                before *= 2
        wait_send(CHIPS, core_send.at[index])
        pltpu.make_async_remote_copy(
            src_ref=span(CHIPS, 1 - core),
            dst_ref=span(CHIPS, 1 - core),
            send_sem=core_send.at[index],
            recv_sem=core_recv.at[index],
            device_id=partner,
            device_id_type=MESH,
        ).wait_recv()


def gather_layer(layer, masters, ident):
    numbers = (4, 0, 1, 2, 3) if len(masters) == 5 else (0, 1, 2, 3)
    pieces = tuple(p for p in PIECES if p[0] in numbers)
    count = len(pieces)
    arrays = 3 if 4 in numbers else 2
    scratch = lambda rows, dtype: [
        pltpu.VMEM((rows * OWN_ROWS[n], WIDTHS[n] // 2), dtype) for n in numbers
    ]
    return pl.pallas_call(
        functools.partial(gather_kernel, layer, numbers, pieces),
        out_shape=tuple(jax.ShapeDtypeStruct(WHOLES[n], jnp.bfloat16) for n in range(arrays)),
        in_specs=[pl.BlockSpec(memory_space=pl.ANY)] * len(numbers),
        out_specs=tuple([pl.BlockSpec(memory_space=pl.ANY)] * arrays),
        scratch_shapes=(
            scratch(1, jnp.float32)
            + scratch(1, jnp.float32)
            + scratch(2, jnp.bfloat16)
            + [
                pltpu.SemaphoreType.DMA((5,)),
                pltpu.SemaphoreType.DMA((5,)),
                pltpu.SemaphoreType.DMA((5,)),
                pltpu.SemaphoreType.DMA((count,)),
                pltpu.SemaphoreType.DMA((count, 4)),
                pltpu.SemaphoreType.DMA((count, CHIPS)),
                pltpu.SemaphoreType.DMA((count,)),
                pltpu.SemaphoreType.DMA((count,)),
            ]
        ),
        name=f"gather_{layer}",
        compiler_params=pltpu.CompilerParams(
            collective_id=ident, has_side_effects=True, vmem_limit_bytes=40 << 20
        ),
        cost_estimate=pl.CostEstimate(flops=0, bytes_accessed=int(2e8), transcendentals=0),
    )(*[masters[n] for n in numbers])


def slot_of(order, side, source):
    sizes = {"z": NZ, "y": NY, "x": NX}
    base = 0
    ahead = 1
    number = 0
    for axis in order:
        at = source[AXIS[axis]]
        for here in ["up", "down"] if axis == "z" else [axis]:
            if axis == "z":
                if here == side:
                    return base + number * NZ + at
                base += ahead * NZ
            else:
                if here == side:
                    return base + number
                base += ahead
        number = number * sizes[axis] + at
        ahead *= sizes[axis]
    return base


def slot_count(order):
    return slot_of(order, None, (0, 0, 0))


def scatter_kernel(numbers, pieces, *refs):
    many = len(numbers)
    count = len(pieces)
    take = iter(refs)
    partials = [next(take) for _ in range(3 if 4 in numbers else 2)]
    named = lambda: dict(zip(numbers, [next(take) for _ in range(many)]))
    outs, own, pair, total, handed = named(), named(), named(), named(), named()
    slots = [next(take) for _ in range(count)]
    base = {p[0]: p[2] for p in pieces}
    array = {p[0]: p[1] for p in pieces}
    (
        own_sem,
        pair_send,
        pair_recv,
        send_sem,
        recv_sem,
        end_send,
        end_recv,
        out_sem,
    ) = take
    spot = place()
    z, y, x, core = spot
    me = chip_number(z, y, x)
    partner = neighbour("core", spot)
    loads = {}
    for number in numbers:
        half = WIDTHS[number] // 2
        load = pltpu.make_async_copy(
            partials[array[number]].at[:, pl.ds(aligned(base[number] + core * half, 128), half)],
            own[number],
            own_sem.at[number],
        )
        load.start()
        loads[number] = load
    greet(spot)
    swaps = {}
    for number in numbers:
        half = WIDTHS[number] // 2
        swap = pltpu.make_async_remote_copy(
            src_ref=partials[array[number]].at[
                :, pl.ds(aligned(base[number] + (1 - core) * half, 128), half)
            ],
            dst_ref=pair[number],
            send_sem=pair_send.at[number],
            recv_sem=pair_recv.at[number],
            device_id=partner,
            device_id_type=MESH,
        )
        swap.start()
        swaps[number] = swap
    ready = set()
    for away in reversed(offsets()):
        for index, piece in enumerate(pieces):
            number, _, _, chip_rows, low, rows, column, columns, order = piece
            if number not in ready:
                ready.add(number)
                loads[number].wait()
                swaps[number].wait_recv()
            sz, sy, sx, valid = source_of(spot, away)
            source = chip_number(sz, sy, sx)
            last = last_axis(order, away)

            def event(
                index=index, number=number, chip_rows=chip_rows, low=low, rows=rows,
                column=column, columns=columns, order=order, source=source, last=last,
                where=(sz, sy, sx),
            ):
                kids = children(order, away)
                for side in kids:

                    def arrived(side=side):
                        slot = slot_of(order, side, where)
                        pltpu.make_async_remote_copy(
                            src_ref=slots[index].at[slot],
                            dst_ref=slots[index].at[slot],
                            send_sem=send_sem.at[index, 0],
                            recv_sem=recv_sem.at[index, slot],
                            device_id=partner,
                            device_id_type=MESH,
                        ).wait_recv()

                    guarded(exists(side, z), arrived)
                view = (pl.ds(aligned(source * chip_rows + low, 16), rows), pl.ds(column, columns))
                value = own[number][view].astype(jnp.float32) + pair[number][view].astype(jnp.float32)
                for side in kids:
                    landed = slots[index][slot_of(order, side, where)].astype(jnp.float32)
                    there = exists(side, z)
                    value = value + (landed if there is None else jnp.where(there, landed, 0.0))
                if last < 0:
                    total[number][pl.ds(low, rows), pl.ds(column, columns)] = value
                    return
                pair[number][view] = value.astype(jnp.bfloat16)
                axis = order[last]
                if axis == "z":
                    side = "up" if away[0] < 0 else "down"
                    parent = neighbour("down" if away[0] < 0 else "up", spot)
                else:
                    side = axis
                    parent = neighbour(axis, spot)
                slot = slot_of(order, side, where)
                pltpu.make_async_remote_copy(
                    src_ref=pair[number].at[view],
                    dst_ref=slots[index].at[slot],
                    send_sem=send_sem.at[index, source],
                    recv_sem=recv_sem.at[index, slot],
                    device_id=parent,
                    device_id_type=MESH,
                ).start()

            guarded(valid, event)
    ends = {}
    for number in numbers:
        rows = OWN_ROWS[number]
        end = pltpu.make_async_remote_copy(
            src_ref=total[number].at[pl.ds(aligned((1 - core) * rows, 8), rows)],
            dst_ref=handed[number],
            send_sem=end_send.at[number],
            recv_sem=end_recv.at[number],
            device_id=partner,
            device_id_type=MESH,
        )
        end.start()
        ends[number] = end
    writes = []
    for number in numbers:
        rows = OWN_ROWS[number]
        half = WIDTHS[number] // 2
        write = pltpu.make_async_copy(
            total[number].at[pl.ds(aligned(core * rows, 8), rows)],
            outs[number].at[:, pl.ds(aligned(core * half, 128), half)],
            out_sem.at[number],
        )
        write.start()
        writes.append(write)
    for number in numbers:
        half = WIDTHS[number] // 2
        ends[number].wait_recv()
        write = pltpu.make_async_copy(
            handed[number],
            outs[number].at[:, pl.ds(aligned((1 - core) * half, 128), half)],
            out_sem.at[5 + number],
        )
        write.start()
        writes.append(write)
    for write in writes:
        write.wait()
    for end in ends.values():
        end.wait_send()
    for swap in swaps.values():
        swap.wait_send()
    for index, piece in enumerate(pieces):
        number, _, _, chip_rows, low, rows, column, columns, order = piece
        for away in offsets():
            if away == (0, 0, 0):
                continue
            sz, sy, sx, valid = source_of(spot, away)
            source = chip_number(sz, sy, sx)

            def sent(index=index, source=source):
                view = (pl.ds(aligned(source * chip_rows + low, 16), rows), pl.ds(column, columns))
                pltpu.make_async_remote_copy(
                    src_ref=pair[number].at[view],
                    dst_ref=slots[index].at[0],
                    send_sem=send_sem.at[index, source],
                    recv_sem=recv_sem.at[index, 0],
                    device_id=partner,
                    device_id_type=MESH,
                ).wait_send()

            guarded(valid, sent)


def scatter_layer(layer, partials, ident):
    numbers = (4, 0, 1, 2, 3) if len(partials) == 3 else (0, 1, 2, 3)
    pieces = tuple(p for p in PIECES if p[0] in numbers)
    count = len(pieces)
    most = max(slot_count(p[8]) for p in pieces)
    scratch = lambda rows, dtype: [
        pltpu.VMEM((rows * OWN_ROWS[n], WIDTHS[n] // 2), dtype) for n in numbers
    ]
    return dict(
        zip(
            numbers,
            pl.pallas_call(
                functools.partial(scatter_kernel, numbers, pieces),
                out_shape=tuple(
                    jax.ShapeDtypeStruct((OWN_ROWS[n], WIDTHS[n]), jnp.float32) for n in numbers
                ),
                in_specs=[pl.BlockSpec(memory_space=pl.ANY)] * len(partials),
                out_specs=tuple([pl.BlockSpec(memory_space=pl.ANY)] * len(numbers)),
                scratch_shapes=(
                    scratch(32, jnp.bfloat16)
                    + scratch(32, jnp.bfloat16)
                    + scratch(2, jnp.float32)
                    + scratch(1, jnp.float32)
                    + [pltpu.VMEM((slot_count(p[8]), p[5], p[7]), jnp.bfloat16) for p in pieces]
                    + [
                        pltpu.SemaphoreType.DMA((5,)),
                        pltpu.SemaphoreType.DMA((5,)),
                        pltpu.SemaphoreType.DMA((5,)),
                        pltpu.SemaphoreType.DMA((count, CHIPS)),
                        pltpu.SemaphoreType.DMA((count, most)),
                        pltpu.SemaphoreType.DMA((5,)),
                        pltpu.SemaphoreType.DMA((5,)),
                        pltpu.SemaphoreType.DMA((10,)),
                    ]
                ),
                name=f"scatter_{layer}",
                compiler_params=pltpu.CompilerParams(
                    collective_id=ident, has_side_effects=True, vmem_limit_bytes=56 << 20
                ),
                cost_estimate=pl.CostEstimate(flops=0, bytes_accessed=int(2e8), transcendentals=0),
            )(*partials),
        )
    )


def passed_along(value, axis, by):
    size = lax.axis_size(axis)
    pairs = [(i, i + by) for i in range(size) if 0 <= i + by < size]
    return lax.ppermute(value, axis, pairs)


def normalize(values):
    centred = values - jnp.mean(values, axis=-1, keepdims=True)
    inverse = lax.rsqrt(jnp.mean(centred * centred, axis=-1, keepdims=True) + EPSILON)
    return (centred * inverse, inverse)


def normalize_back(grad_normed, normed, inverse):
    return inverse * (
        grad_normed
        - jnp.mean(grad_normed, axis=-1, keepdims=True)
        - normed * jnp.mean(grad_normed * normed, axis=-1, keepdims=True)
    )


def rotary_tables(relative):
    indices = jnp.arange(HEAD_DIM // 2).astype(jnp.float32)
    frequency = jnp.exp(indices * (-2.0 * math.log(10000.0) / HEAD_DIM))
    phase = relative.astype(jnp.float32)[:, None] * frequency[None, :]
    cosine, sine = jnp.cos(phase), jnp.sin(phase)
    return (
        jnp.concatenate([cosine] * 4, axis=1),
        jnp.concatenate([-sine, sine, -sine, sine], axis=1),
    )


BAND = 128
VARIANTS = (3, 4, 5, 6, 7, 9)
STEP_COLUMNS = 384
BLOCK = 512
F32 = jnp.float32
BF16 = jnp.bfloat16
MATMUL = (((1,), (0,)), ((), ()))
MATMUL_RIGHT = (((1,), (1,)), ((), ()))
MATMUL_LEFT = (((0,), (0,)), ((), ()))


def product(left, right, dims=MATMUL):
    return lax.dot_general(left, right, dims, preferred_element_type=F32)


def vmem(limit=56):
    return pltpu.CompilerParams(vmem_limit_bytes=limit << 20)


def cost(flops, moved):
    return pl.CostEstimate(flops=int(flops), bytes_accessed=int(moved), transcendentals=0)


def swap_halves(values):
    lane = lax.broadcasted_iota(jnp.int32, values.shape, 1)
    low = lax.rem(lane, HEAD_DIM) < HEAD_DIM // 2
    return jnp.where(
        low,
        pltpu.roll(values, 2 * HEAD_DIM - HEAD_DIM // 2, 1),
        pltpu.roll(values, HEAD_DIM // 2, 1),
    )


def turn(values, cosine, sine):
    parts = []
    for at in range(0, values.shape[1], 128):
        part = values[:, at : at + 128]
        parts.append(part * cosine + swap_halves(part) * sine)
    return jnp.concatenate(parts, axis=1)


def project_kernel(x_ref, w_ref, bias_ref, mod_ref, cos_ref, sin_ref, q_ref, kv_ref, h_ref):
    step = pl.program_id(0)

    @pl.when(step == 0)
    def _():
        normed, _ = normalize(x_ref[...].astype(F32))
        h_ref[...] = (normed * (1.0 + mod_ref[1:2]) + mod_ref[0:1]).astype(BF16)

    y = product(h_ref[...], w_ref[...]) + bias_ref[...]

    @pl.when(step < 2)
    def _():
        q_ref[...] = turn(y, cos_ref[...], sin_ref[...]).astype(BF16)

    @pl.when((step >= 2) & (step < 4))
    def _():
        kv_ref[0] = turn(y, cos_ref[...], sin_ref[...]).astype(BF16)

    @pl.when(step >= 4)
    def _():
        kv_ref[0] = y.astype(BF16)


def project(stream, square, bias, modulation, cosine, sine):
    rows = stream.shape[0]
    whole = lambda shape: pl.BlockSpec(shape, lambda c: (0,) * len(shape))
    return pl.pallas_call(
        project_kernel,
        grid=(6,),
        in_specs=[
            whole((rows, D)),
            pl.BlockSpec((D, STEP_COLUMNS), lambda c: (0, c)),
            pl.BlockSpec((1, STEP_COLUMNS), lambda c: (0, c)),
            whole((4, D)),
            whole((rows, 128)),
            whole((rows, 128)),
        ],
        out_specs=(
            pl.BlockSpec((rows, STEP_COLUMNS), lambda c: (0, jnp.minimum(c, 1))),
            pl.BlockSpec(
                (1, rows, STEP_COLUMNS),
                lambda c: (jnp.maximum(c - 2, 0) // 2, 0, jnp.maximum(c - 2, 0) % 2),
            ),
            whole((rows, D)),
        ),
        out_shape=(
            jax.ShapeDtypeStruct((rows, D), BF16),
            jax.ShapeDtypeStruct((2, rows, D), BF16),
            jax.ShapeDtypeStruct((rows, D), BF16),
        ),
        compiler_params=vmem(),
        cost_estimate=cost(2 * rows * D * 3 * D, 8e6),
        name="project",
    )(stream, square, bias, modulation, cosine, sine)


def stack_heads(pair):
    lane = lax.broadcasted_iota(jnp.int32, pair.shape, 1)
    zero = jnp.zeros_like(pair)
    return jnp.concatenate(
        [jnp.where(lane < HEAD_DIM, pair, zero), jnp.where(lane < HEAD_DIM, zero, pair)], axis=0
    )


def merge_heads(stacked):
    rows = stacked.shape[0] // 2
    lane = lax.broadcasted_iota(jnp.int32, (rows, stacked.shape[1]), 1)
    return jnp.where(lane < HEAD_DIM, stacked[:rows], stacked[rows:])


def over_bands(bounds_ref, count, action):
    def one(number, carry):
        low, need = bounds_ref[0, number], bounds_ref[1, number]
        before = 0
        for size in VARIANTS:

            @pl.when((need > before) & (need <= size))
            def _(size=size):
                start = jnp.minimum(low, count - size) * BAND
                action(pl.multiple_of(number * BAND, BAND), pl.multiple_of(start, BAND), size * BAND)

            before = size
        return carry

    lax.fori_loop(0, bounds_ref.shape[1], one, 0)


def attend_kernel(bounds_ref, q_ref, low_ref, own_ref, high_ref, idq_ref, idk_ref, o_ref, lse_ref, ext):
    rows = own_ref.shape[1]
    for at in range(2):
        ext[at, :WIN_MAX] = low_ref[at]
        ext[at, WIN_MAX : WIN_MAX + rows] = own_ref[at]
        ext[at, WIN_MAX + rows :] = high_ref[at]

    def block(first, start, size):
        mine = pl.ds(first, BAND)
        queries = stack_heads(q_ref[mine, :]) * jnp.asarray(HEAD_DIM**-0.5, BF16)
        keys = ext[0, pl.ds(start, size), :]
        scores = product(queries, keys, MATMUL_RIGHT)
        ids = idq_ref[mine, :]
        allowed = jnp.concatenate([ids] * (size // BAND), axis=1) == idk_ref[0:1, pl.ds(start, size)]
        scores = jnp.where(jnp.concatenate([allowed, allowed], axis=0), scores, NEGATIVE)
        peak = jnp.max(scores, axis=1, keepdims=True)
        weights = jnp.exp(scores - peak)
        total = jnp.sum(weights, axis=1, keepdims=True)
        values = ext[1, pl.ds(start, size), :]
        mixed = product(weights.astype(BF16), values) * (1.0 / total)
        o_ref[mine, :] = merge_heads(mixed).astype(BF16)
        wide = jnp.broadcast_to(peak + jnp.log(total), (2 * BAND, BAND))
        lse_ref[0, 0:1, mine] = wide[:BAND].T[0:1]
        lse_ref[0, 1:2, mine] = wide[BAND:].T[0:1]

    over_bands(bounds_ref, (rows + 2 * WIN_MAX) // BAND, block)


def pair_spec(rows):
    return pl.BlockSpec((2, rows, 128), lambda j, b: (0, 0, j))


def attend(bounds, queries, low, own, high, ids_query, ids_key):
    rows = queries.shape[0]
    wide = rows + 2 * WIN_MAX
    column = pl.BlockSpec((rows, 128), lambda j, b: (0, j))
    return pl.pallas_call(
        attend_kernel,
        grid_spec=pltpu.PrefetchScalarGridSpec(
            num_scalar_prefetch=1,
            grid=(HEADS // 2,),
            in_specs=[
                column,
                pair_spec(WIN_MAX),
                pair_spec(rows),
                pair_spec(WIN_MAX),
                pl.BlockSpec((rows, 128), lambda j, b: (0, 0)),
                pl.BlockSpec((8, wide), lambda j, b: (0, 0)),
            ],
            out_specs=(column, pl.BlockSpec((1, 8, rows), lambda j, b: (j, 0, 0))),
            scratch_shapes=[pltpu.VMEM((2, wide, 128), BF16)],
        ),
        out_shape=(
            jax.ShapeDtypeStruct((rows, D), BF16),
            jax.ShapeDtypeStruct((HEADS // 2, 8, rows), F32),
        ),
        compiler_params=vmem(),
        cost_estimate=cost(5e9, 8e6),
        name="attend",
    )(bounds, queries, low, own, high, ids_query, ids_key)


def attend_back_kernel(
    bounds_ref, q_ref, g_ref, o_ref, lse_ref, low_ref, own_ref, high_ref, idq_ref, idk_ref,
    cos_ref, sin_ref, dq_ref, dlow_ref, down_ref, dhigh_ref, ext, dext,
):
    rows = own_ref.shape[1]
    for at in range(2):
        ext[at, :WIN_MAX] = low_ref[at]
        ext[at, WIN_MAX : WIN_MAX + rows] = own_ref[at]
        ext[at, WIN_MAX + rows :] = high_ref[at]
    dext[...] = jnp.zeros_like(dext)

    def block(first, start, size):
        mine = pl.ds(first, BAND)
        band = pl.ds(start, size)
        queries = stack_heads(q_ref[mine, :]) * jnp.asarray(HEAD_DIM**-0.5, BF16)
        grads = stack_heads(g_ref[mine, :])
        keys = ext[0, band, :]
        scores = product(keys, queries, MATMUL_RIGHT)
        ids = idk_ref[band, :] == idq_ref[0:1, mine]
        allowed = jnp.concatenate([ids, ids], axis=1)
        lse = jnp.concatenate([lse_ref[0, 0:1, mine], lse_ref[0, 1:2, mine]], axis=1)
        weights = jnp.where(allowed, jnp.exp(scores - lse), 0.0)
        both_heads = (g_ref[mine, :].astype(F32) * o_ref[mine, :].astype(F32)).T
        delta = jnp.concatenate(
            [
                jnp.sum(both_heads[:HEAD_DIM], axis=0, keepdims=True),
                jnp.sum(both_heads[HEAD_DIM:], axis=0, keepdims=True),
            ],
            axis=1,
        )
        values = ext[1, band, :]
        grad_weights = product(values, grads, MATMUL_RIGHT)
        grad_scores = (weights * (grad_weights - delta)).astype(BF16)
        dext[0, band, :] += product(grad_scores, queries)
        dext[1, band, :] += product(weights.astype(BF16), grads)
        grad_queries = merge_heads(product(grad_scores, keys, MATMUL_LEFT)) * HEAD_DIM**-0.5
        dq_ref[mine, :] = turn(grad_queries, cos_ref[mine, :], -sin_ref[mine, :]).astype(BF16)

    over_bands(bounds_ref, (rows + 2 * WIN_MAX) // BAND, block)
    dlow_ref[...] = dext[:, :WIN_MAX].astype(BF16)
    down_ref[...] = dext[:, WIN_MAX : WIN_MAX + rows]
    dhigh_ref[...] = dext[:, WIN_MAX + rows :].astype(BF16)


def attend_back(bounds, queries, grads, attended, lse, low, own, high, ids_query, ids_key, cosine, sine):
    rows = queries.shape[0]
    wide = rows + 2 * WIN_MAX
    column = pl.BlockSpec((rows, 128), lambda j, b: (0, j))
    fixed = lambda shape: pl.BlockSpec(shape, lambda j, b: (0,) * len(shape))
    return pl.pallas_call(
        attend_back_kernel,
        grid_spec=pltpu.PrefetchScalarGridSpec(
            num_scalar_prefetch=1,
            grid=(HEADS // 2,),
            in_specs=[
                column,
                column,
                column,
                pl.BlockSpec((1, 8, rows), lambda j, b: (j, 0, 0)),
                pair_spec(WIN_MAX),
                pair_spec(rows),
                pair_spec(WIN_MAX),
                fixed((8, rows)),
                fixed((wide, 128)),
                fixed((rows, 128)),
                fixed((rows, 128)),
            ],
            out_specs=(column, pair_spec(WIN_MAX), pair_spec(rows), pair_spec(WIN_MAX)),
            scratch_shapes=[pltpu.VMEM((2, wide, 128), BF16), pltpu.VMEM((2, wide, 128), F32)],
        ),
        out_shape=(
            jax.ShapeDtypeStruct((rows, D), BF16),
            jax.ShapeDtypeStruct((2, WIN_MAX, D), BF16),
            jax.ShapeDtypeStruct((2, rows, D), F32),
            jax.ShapeDtypeStruct((2, WIN_MAX, D), BF16),
        ),
        compiler_params=vmem(),
        cost_estimate=cost(12e9, 16e6),
        name="attend_back",
    )(bounds, queries, grads, attended, lse, low, own, high, ids_query, ids_key, cosine, sine)


def feed_kernel(
    o_ref, x_ref, wo_ref, we_ref, ws_ref, bo_ref, be_ref, bs_ref, mod_ref,
    mid_ref, h_ref, z_ref, slope_ref, out_ref,
):
    step = pl.program_id(0)

    @pl.when(step == 0)
    def _():
        middle = x_ref[...].astype(F32) + (product(o_ref[...], wo_ref[...]) + bo_ref[...])
        mid_ref[...] = middle
        normed, _ = normalize(middle)
        h_ref[...] = (normed * (1.0 + mod_ref[3:4]) + mod_ref[2:3]).astype(BF16)
        out_ref[...] = middle + bs_ref[...]

    u = product(h_ref[...], we_ref[...]) + be_ref[...]
    share = 0.5 + 0.5 * lax.erf(u * (0.5**0.5))
    active = (u * share).astype(BF16)
    z_ref[...] = active
    slope_ref[...] = (share + u * (jnp.exp(-0.5 * u * u) * (2.0 * math.pi) ** -0.5)).astype(BF16)
    out_ref[...] += product(active, ws_ref[...])


def feed(attended, stream, square, shrink, bias, modulation):
    rows = stream.shape[0]
    whole = lambda shape: pl.BlockSpec(shape, lambda c: (0,) * len(shape))
    width = STEP_COLUMNS
    return pl.pallas_call(
        feed_kernel,
        grid=(FF // width,),
        in_specs=[
            whole((rows, D)),
            whole((rows, D)),
            pl.BlockSpec((D, D), lambda c: (0, 3)),
            pl.BlockSpec((D, width), lambda c: (0, 4 * D // width + c)),
            pl.BlockSpec((width, D), lambda c: (c, 0)),
            pl.BlockSpec((1, D), lambda c: (0, 3)),
            pl.BlockSpec((1, width), lambda c: (0, 4 * D // width + c)),
            pl.BlockSpec((1, D), lambda c: (0, 8)),
            whole((4, D)),
        ],
        out_specs=(
            whole((rows, D)),
            whole((rows, D)),
            pl.BlockSpec((rows, width), lambda c: (0, c)),
            pl.BlockSpec((rows, width), lambda c: (0, c)),
            whole((rows, D)),
        ),
        out_shape=(
            jax.ShapeDtypeStruct((rows, D), F32),
            jax.ShapeDtypeStruct((rows, D), BF16),
            jax.ShapeDtypeStruct((rows, FF), BF16),
            jax.ShapeDtypeStruct((rows, FF), BF16),
            jax.ShapeDtypeStruct((rows, D), F32),
        ),
        compiler_params=vmem(),
        cost_estimate=cost(2 * rows * D * (D + 2 * FF), 24e6),
        name="feed",
    )(attended, stream, square, square, shrink, bias, bias, bias, modulation)


def feed_back_kernel(
    g_ref, z_ref, slope_ref, h_ref, mid_ref, o_ref, we_ref, ws_ref, wo_ref, mod_ref,
    square_ref, dshr_ref, mid_grad_ref, do_ref, dbe_ref, sums_ref,
    low, turned, total,
):
    step = pl.program_id(0)
    chunks = FF // STEP_COLUMNS

    @pl.when(step == 0)
    def _():
        low[...] = g_ref[...].astype(BF16)
        turned[...] = h_ref[...].T
        total[...] = jnp.zeros_like(total)
        sums_ref[3:4] = jnp.sum(low[...].astype(F32), axis=0, keepdims=True)

    @pl.when(step < chunks)
    def _():
        grad_active = product(low[...], ws_ref[...], MATMUL_RIGHT)
        grad_hidden = (grad_active * slope_ref[...].astype(F32)).astype(BF16)
        dbe_ref[...] = jnp.sum(grad_hidden.astype(F32), axis=0, keepdims=True)
        dshr_ref[...] = product(z_ref[...], low[...], MATMUL_LEFT).astype(BF16)
        square_ref[...] = product(turned[...], grad_hidden).astype(BF16)
        total[...] += product(grad_hidden, we_ref[...], MATMUL_RIGHT)

    @pl.when(step == chunks)
    def _():
        normed, inverse = normalize(mid_ref[...])
        grad = total[...]
        sums_ref[0:1] = jnp.sum(grad, axis=0, keepdims=True)
        sums_ref[1:2] = jnp.sum(grad * normed, axis=0, keepdims=True)
        middle = g_ref[...].astype(F32) + normalize_back(grad * (1.0 + mod_ref[3:4]), normed, inverse)
        mid_grad_ref[...] = middle
        low[...] = middle.astype(BF16)
        sums_ref[2:3] = jnp.sum(low[...].astype(F32), axis=0, keepdims=True)
        do_ref[...] = product(low[...], wo_ref[...], MATMUL_RIGHT).astype(BF16)
        turned[...] = o_ref[...].T
        square_ref[...] = product(turned[...], low[:, :STEP_COLUMNS]).astype(BF16)

    @pl.when(step == chunks + 1)
    def _():
        square_ref[...] = product(turned[...], low[:, STEP_COLUMNS:]).astype(BF16)


def feed_back(grad, active, slope, hidden_in, middle, attended, square, shrink, modulation):
    rows = grad.shape[0]
    whole = lambda shape: pl.BlockSpec(shape, lambda c: (0,) * len(shape))
    width = STEP_COLUMNS
    chunks = FF // width
    upto = lambda c: jnp.minimum(c, chunks - 1)
    return pl.pallas_call(
        feed_back_kernel,
        grid=(chunks + 2,),
        in_specs=[
            whole((rows, D)),
            pl.BlockSpec((rows, width), lambda c: (0, upto(c))),
            pl.BlockSpec((rows, width), lambda c: (0, upto(c))),
            whole((rows, D)),
            whole((rows, D)),
            whole((rows, D)),
            pl.BlockSpec((D, width), lambda c: (0, 4 * D // width + upto(c))),
            pl.BlockSpec((width, D), lambda c: (upto(c), 0)),
            pl.BlockSpec((D, D), lambda c: (0, 3)),
            whole((4, D)),
        ],
        out_specs=(
            pl.BlockSpec(
                (D, width),
                lambda c: (0, jnp.where(c < chunks, 4 * D // width + c, 3 * D // width + c - chunks)),
            ),
            pl.BlockSpec((width, D), lambda c: (upto(c), 0)),
            whole((rows, D)),
            whole((rows, D)),
            pl.BlockSpec((1, width), lambda c: (0, upto(c))),
            whole((4, D)),
        ),
        out_shape=(
            jax.ShapeDtypeStruct((D, 4 * D + FF), BF16),
            jax.ShapeDtypeStruct((FF, D), BF16),
            jax.ShapeDtypeStruct((rows, D), F32),
            jax.ShapeDtypeStruct((rows, D), BF16),
            jax.ShapeDtypeStruct((1, FF), F32),
            jax.ShapeDtypeStruct((4, D), F32),
        ),
        scratch_shapes=[
            pltpu.VMEM((rows, D), BF16),
            pltpu.VMEM((D, rows), BF16),
            pltpu.VMEM((rows, D), F32),
        ],
        compiler_params=vmem(),
        cost_estimate=cost(4 * rows * D * (D + 2 * FF), 40e6),
        name="feed_back",
    )(grad, active, slope, hidden_in, middle, attended, square, shrink, square, modulation)


def project_back_kernel(
    dq_ref, own_ref, below_ref, above_ref, cos_ref, sin_ref, h_ref, x_ref, mid_grad_ref, w_ref, mod_ref,
    square_in, square_ref, out_ref, db_ref, sums_ref, turned, total,
):
    step = pl.program_id(0)

    @pl.when(step == 0)
    def _():
        turned[...] = h_ref[...].T
        total[...] = jnp.zeros_like(total)

    def chunk(grad):
        db_ref[...] = jnp.sum(grad.astype(F32), axis=0, keepdims=True)
        square_ref[...] = product(turned[...], grad).astype(BF16)
        total[...] += product(grad, w_ref[...], MATMUL_RIGHT)

    def summed():
        return own_ref[0] + below_ref[0].astype(F32) + above_ref[0].astype(F32)

    @pl.when(step < 2)
    def _():
        chunk(dq_ref[...])

    @pl.when((step >= 2) & (step < 4))
    def _():
        chunk(turn(summed(), cos_ref[...], -sin_ref[...]).astype(BF16))

    @pl.when(step >= 4)
    def _():
        chunk(summed().astype(BF16))

    @pl.when(step == 5)
    def _():
        normed, inverse = normalize(x_ref[...].astype(F32))
        grad = total[...]
        sums_ref[0:1] = jnp.sum(grad, axis=0, keepdims=True)
        sums_ref[1:2] = jnp.sum(grad * normed, axis=0, keepdims=True)
        out_ref[...] = mid_grad_ref[...] + normalize_back(
            grad * (1.0 + mod_ref[1:2]), normed, inverse
        )


def project_back(dq, own, below, above, cosine, sine, hidden_in, stream, mid_grad, square, modulation, square_grad):
    rows = dq.shape[0]
    width = STEP_COLUMNS
    whole = lambda shape: pl.BlockSpec(shape, lambda c: (0,) * len(shape))
    later = pl.BlockSpec(
        (1, rows, width), lambda c: (jnp.maximum(c - 2, 0) // 2, 0, jnp.maximum(c - 2, 0) % 2)
    )
    return pl.pallas_call(
        project_back_kernel,
        grid=(6,),
        in_specs=[
            pl.BlockSpec((rows, width), lambda c: (0, jnp.minimum(c, 1))),
            later,
            later,
            later,
            whole((rows, 128)),
            whole((rows, 128)),
            whole((rows, D)),
            whole((rows, D)),
            whole((rows, D)),
            pl.BlockSpec((D, width), lambda c: (0, c)),
            whole((4, D)),
            pl.BlockSpec(memory_space=pl.ANY),
        ],
        out_specs=(
            pl.BlockSpec((D, width), lambda c: (0, c)),
            whole((rows, D)),
            pl.BlockSpec((1, width), lambda c: (0, c)),
            whole((2, D)),
        ),
        out_shape=(
            jax.ShapeDtypeStruct((D, 4 * D + FF), BF16),
            jax.ShapeDtypeStruct((rows, D), F32),
            jax.ShapeDtypeStruct((1, 3 * D), F32),
            jax.ShapeDtypeStruct((2, D), F32),
        ),
        scratch_shapes=[pltpu.VMEM((D, rows), BF16), pltpu.VMEM((rows, D), F32)],
        input_output_aliases={11: 0},
        compiler_params=vmem(),
        cost_estimate=cost(4 * rows * D * 3 * D, 20e6),
        name="project_back",
    )(dq, own, below, above, cosine, sine, hidden_in, stream, mid_grad, square, modulation, square_grad)


def direct():
    return lax.axis_size("dp") == NZ * NY and lax.axis_size("fsdp") == NX * 2


BOTH = ("dp", "fsdp")


def pack_small(bias, table):
    flat = jnp.concatenate([bias.reshape(-1), table.reshape(-1)])
    flat = jnp.pad(flat, (0, OWN_ROWS[4] * SMALL - flat.shape[0]))
    return flat.reshape(1, OWN_ROWS[4], SMALL)


def unpack_small(whole, lead_row):
    count = lax.axis_size("dp") * lax.axis_size("fsdp")
    flat = whole.reshape(count, -1).astype(F32)
    wide = LAYERS * 9 * D // count
    bias = flat[:, :wide].reshape(count, LAYERS, 9, -1).transpose(1, 2, 0, 3).reshape(LAYERS, 9 * D)
    table = flat[:, wide : wide + LAYERS * LEADS * 4 * D // count].reshape(count, LAYERS, LEADS, -1)
    rows = lax.dynamic_index_in_dim(table, lead_row, 2, keepdims=False)
    return bias, rows.transpose(1, 0, 2).reshape(LAYERS, 4, D)


def plain_fetch(masters, layer):
    square = jnp.concatenate([masters[n][layer].astype(BF16) for n in range(3)], axis=1)
    shrink = masters[3][layer].astype(BF16)
    return (
        lax.all_gather(square, BOTH, axis=0, tiled=True),
        lax.all_gather(shrink, BOTH, axis=0, tiled=True),
    )


def fetch_layers(masters, lead_row):
    if direct():
        small = pack_small(masters[4], masters[5])
        *first, whole = gather_layer(0, (*masters[:4], small), 0)
        bias, modulation = unpack_small(whole, lead_row)
        layers = [tuple(first)]
    else:
        bias = lax.all_gather(masters[4].astype(BF16), BOTH, axis=2, tiled=True)
        bias = bias.astype(F32).reshape(LAYERS, 9 * D)
        table = lax.all_gather(masters[5].astype(BF16), BOTH, axis=2, tiled=True)
        modulation = lax.dynamic_index_in_dim(table, lead_row, 1, keepdims=False)
        modulation = modulation.astype(F32).reshape(LAYERS, 4, D)
        layers = [plain_fetch(masters, 0)]
    for layer in range(1, LAYERS):
        if direct() and not LATER_OFFLOADED:
            layers.append(tuple(gather_layer(layer, masters[:4], layer)))
        else:
            layers.append(plain_fetch(masters, layer))
    return layers, bias, modulation


def plain_reduce(square, shrink):
    square = lax.psum_scatter(square, BOTH, scatter_dimension=0, tiled=True).astype(F32)
    shrink = lax.psum_scatter(shrink, BOTH, scatter_dimension=0, tiled=True).astype(F32)
    return [square[:, : 3 * D], square[:, 3 * D : 4 * D], square[:, 4 * D :], shrink]


def reduce_small_inputs(bias_grads, rows_grads, lead_hot):
    count = lax.axis_size("dp") * lax.axis_size("fsdp")
    bias = bias_grads.reshape(LAYERS * 9, count, -1).transpose(1, 0, 2).reshape(count, -1)
    rows = rows_grads.reshape(LAYERS, 1, count, -1) * lead_hot[None, :, None, None]
    rows = rows.transpose(2, 0, 1, 3).reshape(count, -1)
    flat = jnp.concatenate([bias, rows], axis=1)
    used = flat.shape[1]
    flat = jnp.pad(flat, ((0, 0), (0, OWN_ROWS[4] * SMALL - used)))
    return flat.reshape(-1, SMALL).astype(BF16)


def split_small(own):
    count = lax.axis_size("dp") * lax.axis_size("fsdp")
    flat = own.reshape(-1)
    wide = LAYERS * 9 * D // count
    used = wide + LAYERS * LEADS * 4 * D // count
    return flat[:wide].reshape(LAYERS, 9, -1), flat[wide:used].reshape(LAYERS, LEADS, -1)


def bands(segment_ids, segment_starts, padding_mask, offset, rows):
    length = segment_ids.shape[0]
    position = jnp.arange(length, dtype=jnp.int32)
    real = padding_mask == 1
    names = jnp.where(real, segment_ids, length + position)
    fill = jnp.full((WIN_MAX,), -1, jnp.int32)
    wide = lax.dynamic_slice_in_dim(
        jnp.concatenate([fill, names, fill - 1]), offset, rows + 2 * WIN_MAX
    )
    own = lax.dynamic_slice_in_dim(names, offset, rows)
    at = offset + jnp.arange(rows // BAND, dtype=jnp.int32) * BAND
    last = at + BAND - 1
    begins = jnp.where(real, segment_starts, position)[at]
    ends = jnp.sum((segment_ids[None, :] <= segment_ids[last][:, None]).astype(jnp.int32), axis=1)
    ends = jnp.where(real[last], ends, last + 1)
    low = (begins - offset + WIN_MAX) // BAND
    need = (ends - offset + WIN_MAX + BAND - 1) // BAND - low
    return jnp.stack([low, need]), own, wide


def exchange(pair):
    return passed_along(pair, "fsdp", 1), pair, passed_along(pair, "fsdp", -1)


def adam_update(weight, gradient, moment, square, step_rate, decay_rate):
    moment = BETA_ONE * moment + (1.0 - BETA_ONE) * gradient
    square = BETA_TWO * square + (1.0 - BETA_TWO) * gradient * gradient
    first_fix = 1.0 - BETA_ONE**STEP
    second_fix = 1.0 - BETA_TWO**STEP
    update = moment / first_fix / (jnp.sqrt(square / second_fix) + ADAM_EPSILON)
    weight = weight - step_rate * (update + decay_rate * weight)
    return (weight, moment, square, weight.astype(jnp.bfloat16))


def shards(
    tokens,
    cotangent,
    segment_ids,
    segment_starts,
    padding_mask,
    lead_index,
    input_weights,
    input_moment,
    input_square,
    output_weights,
    output_moment,
    output_square,
    expand_weights,
    expand_moment,
    expand_square,
    shrink_weights,
    shrink_moment,
    shrink_square,
    bias_vector,
    bias_moment,
    bias_square,
    lead_table,
    lead_moment,
    lead_square,
):
    rows = tokens.shape[0]
    offset = lax.axis_index("fsdp") * rows
    bounds, own_names, wide_names = bands(segment_ids, segment_starts, padding_mask, offset, rows)
    ids_query = jnp.broadcast_to(own_names[:, None], (rows, 128))
    ids_key = jnp.broadcast_to(wide_names[None, :], (8, wide_names.shape[0]))
    ids_query_row = jnp.broadcast_to(own_names[None, :], (8, rows))
    ids_key_column = jnp.broadcast_to(wide_names[:, None], (wide_names.shape[0], 128))
    own_starts = lax.dynamic_slice_in_dim(segment_starts, offset, rows)
    relative = offset + jnp.arange(rows, dtype=jnp.int32) - own_starts
    cosine, sine = rotary_tables(relative)
    lead_row = lead_index[0]
    lead_hot = (jnp.arange(LEADS, dtype=jnp.int32) == lead_row).astype(F32)
    masters = (input_weights, output_weights, expand_weights, shrink_weights, bias_vector, lead_table)
    layers, bias, modulation = fetch_layers(masters, lead_row)
    stream = tokens
    saved = []
    for layer in range(LAYERS):
        square, shrink = layers[layer]
        own_bias, own_mod = bias[layer][None], modulation[layer]
        queries, pair, first_in = project(stream, square, own_bias, own_mod, cosine, sine)
        low, own, high = exchange(pair)
        attended, lse = attend(bounds, queries, low, own, high, ids_query, ids_key)
        middle, second_in, active, slope, result = feed(
            attended, stream, square, shrink, own_bias, own_mod
        )
        saved.append(
            (stream, queries, low, own, high, first_in, attended, lse, middle, second_in, active, slope)
        )
        stream = result
    grad = cotangent
    reduced = [None] * LAYERS
    bias_grads = [None] * LAYERS
    rows_grads = [None] * LAYERS
    for layer in reversed(range(LAYERS)):
        square, shrink = layers[layer]
        own_mod = modulation[layer]
        before, queries, low, own, high, first_in, attended, lse, middle, second_in, active, slope = saved[
            layer
        ]
        square_grad, shrink_grad, mid_grad, attended_grad, expand_bias, sums = feed_back(
            grad, active, slope, second_in, middle, attended, square, shrink, own_mod
        )
        dq, to_below, own_grad, to_above = attend_back(
            bounds, queries, attended_grad, attended, lse, low, own, high, ids_query_row,
            ids_key_column, cosine, sine,
        )
        below = passed_along(to_above, "fsdp", 1)
        above = passed_along(to_below, "fsdp", -1)
        square_grad, grad, input_bias, more = project_back(
            dq, own_grad, below, above, cosine, sine, first_in, before, mid_grad, square, own_mod,
            square_grad,
        )
        bias_grads[layer] = jnp.concatenate([input_bias[0], sums[2], expand_bias[0], sums[3]])
        rows_grads[layer] = jnp.concatenate([more[0], more[1], sums[0], sums[1]])
        if direct() and layer == 0:
            small = reduce_small_inputs(jnp.stack(bias_grads), jnp.stack(rows_grads), lead_hot)
            summed = scatter_layer(layer, (square_grad, shrink_grad, small), LAYERS + layer)
            reduced[layer] = [summed[n] for n in range(4)]
            bias_grad, lead_grad = split_small(summed[4])
        elif direct() and not LATER_OFFLOADED:
            summed = scatter_layer(layer, (square_grad, shrink_grad), LAYERS + layer)
            reduced[layer] = [summed[n] for n in range(4)]
        else:
            reduced[layer] = plain_reduce(square_grad, shrink_grad)
    if not direct():
        bias_grad = lax.psum_scatter(
            jnp.stack(bias_grads).reshape(LAYERS, 9, D), BOTH, scatter_dimension=2, tiled=True
        )
        lead_grad = lax.psum_scatter(
            jnp.stack(rows_grads)[:, None, :] * lead_hot[None, :, None], BOTH, scatter_dimension=2,
            tiled=True,
        )
    moments = (input_moment, output_moment, expand_moment, shrink_moment, bias_moment, lead_moment)
    squares = (input_square, output_square, expand_square, shrink_square, bias_square, lead_square)
    results = []
    for number in range(6):
        if number < 4:
            gradient = jnp.stack([reduced[layer][number] for layer in range(LAYERS)])
        else:
            gradient = (bias_grad, lead_grad)[number - 4]
        results.append(
            adam_update(
                masters[number],
                gradient,
                moments[number],
                squares[number],
                RATE_MATRIX if number < 4 else RATE_VECTOR,
                DECAY if number < 4 else 0.0,
            )
        )
    return (stream, grad, *(array for four in results for array in four))


def solution(mesh):
    rows = P(("dp", "fsdp"), None)
    matrix = P(None, ("dp", "fsdp"), None)
    vector = P(None, None, ("dp", "fsdp"))
    return jax.shard_map(
        shards,
        mesh=mesh,
        in_specs=(rows,) * 2 + (P("dp"),) * 4 + (matrix,) * 12 + (vector,) * 6,
        out_specs=(rows,) * 2 + (matrix,) * 16 + (vector,) * 8,
        check_vma=False,
    )
```

```python
import functools
import math

import jax
import jax.numpy as jnp
from jax import lax
from jax.experimental import pallas as pl
from jax.experimental.pallas import tpu as pltpu
from jax.sharding import PartitionSpec as P

D = 768
FF = 3072
HEADS = 12
HEAD_DIM = 64
LEADS = 20
LAYERS = 2
WIN_MAX = 512
STEP = 10

EPSILON = 1e-06
NEGATIVE = -1e30
BETA_ONE = 0.5
BETA_TWO = 0.5
RATE_MATRIX = 0.08
RATE_VECTOR = 0.3
DECAY = 0.1
ADAM_EPSILON = 1e-08

MESH = pl.DeviceIdType.MESH
NZ, NY, NX = 4, 2, 2
CHIPS = NZ * NY * NX
SMALL = 256
PIECES = (
    (4, 2, 0, 48, 0, 48, 0, 128, "zxy"),
    (0, 0, 0, 48, 0, 48, 0, 1152, "xzy"),
    (1, 0, 2304, 48, 0, 48, 0, 384, "yzx"),
    (2, 0, 3072, 48, 0, 48, 0, 768, "yzx"),
    (2, 0, 3072, 48, 0, 48, 768, 768, "zxy"),
    (3, 1, 0, 192, 0, 48, 0, 384, "zxy"),
    (3, 1, 0, 192, 48, 144, 0, 384, "zyx"),
)
LATER_PIECES = (
    (5, 3, 0, 48, 0, 48, 0, 768, "xzy"),
    (5, 3, 0, 48, 0, 48, 768, 384, "yzx"),
    (6, 3, 2304, 48, 0, 48, 0, 384, "yzx"),
    (7, 3, 3072, 48, 0, 48, 0, 768, "zxy"),
    (7, 3, 3072, 48, 0, 48, 768, 768, "zyx"),
)
WIDTHS = (2304, 768, 3072, 768, SMALL, 2304, 768, 3072)
OWN_ROWS = (24, 24, 24, 96, 24, 24, 24, 24)
WHOLES = ((768, 6144), (3072, 768), (768, SMALL))
AXIS = {"z": 0, "y": 1, "x": 2}


def place():
    dp, fs = lax.axis_index("dp"), lax.axis_index("fsdp")
    return lax.div(dp, NY), lax.rem(dp, NY), lax.div(fs, 2), lax.rem(fs, 2)


def device(z, y, x, core):
    return (z * NY + y, x * 2 + core)


def offsets():
    found = [
        (dz, dy, dx)
        for dz in range(1 - NZ, NZ)
        for dy in range(NY)
        for dx in range(NX)
    ]
    return sorted(found, key=lambda d: (abs(d[0]) + d[1] + d[2], abs(d[0])))


def last_axis(order, away):
    last = -1
    for number, axis in enumerate(order):
        if away[AXIS[axis]] != 0:
            last = number
    return last


def children(order, away):
    last = last_axis(order, away)
    found = []
    for number, axis in enumerate(order):
        if number < last:
            continue
        if axis == "z":
            if number > last:
                found += ["up", "down"]
            else:
                found += ["up"] if away[0] < 0 else ["down"]
        elif number > last:
            found.append(axis)
    return found


def exists(side, z):
    return {"up": z < NZ - 1, "down": z > 0}.get(side)


def neighbour(side, spot):
    z, y, x, core = spot
    return {
        "up": device(z + 1, y, x, core),
        "down": device(z - 1, y, x, core),
        "y": device(z, 1 - y, x, core),
        "x": device(z, y, 1 - x, core),
        "core": device(z, y, x, 1 - core),
    }[side]


def guarded(condition, action):
    if condition is None:
        action()
    else:
        pl.when(condition)(action)


def both(first, second):
    if first is None:
        return second
    if second is None:
        return first
    return first & second


def greet(spot):
    barrier = pltpu.get_barrier_semaphore()
    z = spot[0]
    for side in ("up", "down", "x", "y", "core"):

        def hello(side=side):
            pl.semaphore_signal(
                barrier, inc=1, device_id=neighbour(side, spot), device_id_type=MESH
            )

        guarded(exists(side, z), hello)
    count = 3 + jnp.where(z < NZ - 1, 1, 0) + jnp.where(z > 0, 1, 0)
    pl.semaphore_wait(barrier, count)


def source_of(spot, away):
    z, y, x, _ = spot
    sz = z + away[0]
    sy = 1 - y if away[1] else y
    sx = 1 - x if away[2] else x
    valid = None
    if away[0] > 0:
        valid = sz < NZ
    elif away[0] < 0:
        valid = sz >= 0
    return sz, sy, sx, valid


def chip_number(sz, sy, sx):
    return (sz * NY + sy) * NX + sx


def aligned(value, by):
    return value if isinstance(value, int) else pl.multiple_of(value, by)


def piece_view(ref, piece, chip, core):
    number, _, base, chip_rows, low, rows, column, columns, _ = piece
    half = WIDTHS[number] // 2
    return ref.at[
        pl.ds(aligned(chip * chip_rows + low, 16), rows),
        pl.ds(aligned(base + core * half + column, 128), columns),
    ]


def gather_kernel(layer, numbers, pieces, *refs):
    count = len(numbers)
    arrays = 3 if 4 in numbers else 2
    take = iter(refs)
    masters = dict(zip(numbers, [next(take) for _ in range(count)]))
    wholes = [next(take) for _ in range(arrays)]
    mine = dict(zip(numbers, [next(take) for _ in range(count)]))
    theirs = dict(zip(numbers, [next(take) for _ in range(count)]))
    blocks = dict(zip(numbers, [next(take) for _ in range(count)]))
    local_sem, pair_send, pair_recv, store_sem, send_sem, recv_sem, core_send, core_recv = take
    spot = place()
    z, y, x, core = spot
    me = chip_number(z, y, x)
    partner = neighbour("core", spot)
    loads = {}
    for number in numbers:
        half = WIDTHS[number] // 2
        loads[number] = pltpu.make_async_copy(
            masters[number].at[0 if number == 4 else layer, :, pl.ds(aligned(core * half, 128), half)],
            mine[number],
            local_sem.at[number],
        )
        loads[number].start()
    greet(spot)
    swaps = []
    for number in numbers:
        half = WIDTHS[number] // 2
        swap = pltpu.make_async_remote_copy(
            src_ref=masters[number].at[0 if number == 4 else layer, :, pl.ds(aligned((1 - core) * half, 128), half)],
            dst_ref=theirs[number],
            send_sem=pair_send.at[number],
            recv_sem=pair_recv.at[number],
            device_id=partner,
            device_id_type=MESH,
        )
        swap.start()
        swaps.append((number, swap))

    def relay(index, away, source, view):
        piece = pieces[index]
        for side in children(piece[8], away):

            def send(side=side):
                pltpu.make_async_remote_copy(
                    src_ref=view,
                    dst_ref=piece_view(wholes[piece[1]], piece, source, core),
                    send_sem=send_sem.at[index, ("up", "down", "x", "y").index(side)],
                    recv_sem=recv_sem.at[index, source],
                    device_id=neighbour(side, spot),
                    device_id_type=MESH,
                ).start()

            guarded(exists(side, z), send)
        pltpu.make_async_remote_copy(
            src_ref=view,
            dst_ref=piece_view(wholes[piece[1]], piece, source, core),
            send_sem=core_send.at[index],
            recv_sem=core_recv.at[index],
            device_id=partner,
            device_id_type=MESH,
        ).start()

    stores = []
    for number, swap in swaps:
        loads[number].wait()
        swap.wait_recv()
        rows = OWN_ROWS[number]
        own, other = mine[number][...], theirs[number][...]
        is_first = core == 0
        block = jnp.concatenate(
            [jnp.where(is_first, own, other), jnp.where(is_first, other, own)], axis=0
        )
        blocks[number][...] = block.astype(jnp.bfloat16)
        for index, piece in enumerate(pieces):
            if piece[0] != number:
                continue
            view = blocks[number].at[pl.ds(piece[4], piece[5]), pl.ds(piece[6], piece[7])]
            store = pltpu.make_async_copy(
                view, piece_view(wholes[piece[1]], piece, me, core), store_sem.at[index]
            )
            store.start()
            stores.append(store)
            relay(index, (0, 0, 0), me, view)
    for away in offsets():
        if away == (0, 0, 0):
            continue
        for index, piece in enumerate(pieces):
            sz, sy, sx, valid = source_of(spot, away)
            source = chip_number(sz, sy, sx)

            def arrival(index=index, piece=piece, source=source):
                view = piece_view(wholes[piece[1]], piece, source, core)
                pltpu.make_async_remote_copy(
                    src_ref=view,
                    dst_ref=view,
                    send_sem=send_sem.at[index, 0],
                    recv_sem=recv_sem.at[index, source],
                    device_id=partner,
                    device_id_type=MESH,
                ).wait_recv()
                relay(index, away, source, view)

            guarded(valid, arrival)
    for store in stores:
        store.wait()
    for _, swap in swaps:
        swap.wait_send()
    for index, piece in enumerate(pieces):
        number, rows, columns = piece[0], piece[5], piece[7]

        def span(chunks, core_at):
            half = WIDTHS[number] // 2
            start = aligned(piece[2] + core_at * half + piece[6], 128)
            return wholes[piece[1]].at[pl.ds(0, chunks * rows), pl.ds(start, columns)]

        def wait_send(chunks, sem):
            pltpu.make_async_remote_copy(
                src_ref=span(chunks, core),
                dst_ref=span(chunks, core),
                send_sem=sem,
                recv_sem=recv_sem.at[index, 0],
                device_id=partner,
                device_id_type=MESH,
            ).wait_send()

        order = piece[8]
        before = 1
        for axis in order:
            if axis == "z":
                for at in range(NZ):

                    @pl.when(z == at)
                    def _(at=at):
                        if at < NZ - 1:
                            wait_send(before * (at + 1), send_sem.at[index, 0])
                        if at > 0:
                            wait_send(before * (NZ - at), send_sem.at[index, 1])

                before *= NZ
            else:
                wait_send(before, send_sem.at[index, 2 if axis == "x" else 3])
                before *= 2
        wait_send(CHIPS, core_send.at[index])
        pltpu.make_async_remote_copy(
            src_ref=span(CHIPS, 1 - core),
            dst_ref=span(CHIPS, 1 - core),
            send_sem=core_send.at[index],
            recv_sem=core_recv.at[index],
            device_id=partner,
            device_id_type=MESH,
        ).wait_recv()


def gather_layer(layer, masters, ident):
    numbers = (4, 0, 1, 2, 3) if len(masters) == 5 else (0, 1, 2, 3)
    pieces = tuple(p for p in PIECES if p[0] in numbers)
    count = len(pieces)
    arrays = 3 if 4 in numbers else 2
    scratch = lambda rows, dtype: [
        pltpu.VMEM((rows * OWN_ROWS[n], WIDTHS[n] // 2), dtype) for n in numbers
    ]
    return pl.pallas_call(
        functools.partial(gather_kernel, layer, numbers, pieces),
        out_shape=tuple(jax.ShapeDtypeStruct(WHOLES[n], jnp.bfloat16) for n in range(arrays)),
        in_specs=[pl.BlockSpec(memory_space=pl.ANY)] * len(numbers),
        out_specs=tuple([pl.BlockSpec(memory_space=pl.ANY)] * arrays),
        scratch_shapes=(
            scratch(1, jnp.float32)
            + scratch(1, jnp.float32)
            + scratch(2, jnp.bfloat16)
            + [
                pltpu.SemaphoreType.DMA((5,)),
                pltpu.SemaphoreType.DMA((5,)),
                pltpu.SemaphoreType.DMA((5,)),
                pltpu.SemaphoreType.DMA((count,)),
                pltpu.SemaphoreType.DMA((count, 4)),
                pltpu.SemaphoreType.DMA((count, CHIPS)),
                pltpu.SemaphoreType.DMA((count,)),
                pltpu.SemaphoreType.DMA((count,)),
            ]
        ),
        name=f"gather_{layer}",
        compiler_params=pltpu.CompilerParams(
            collective_id=ident, has_side_effects=True, vmem_limit_bytes=40 << 20
        ),
        cost_estimate=pl.CostEstimate(flops=0, bytes_accessed=int(2e8), transcendentals=0),
    )(*[masters[n] for n in numbers])


def slot_of(order, side, source):
    sizes = {"z": NZ, "y": NY, "x": NX}
    base = 0
    ahead = 1
    number = 0
    for axis in order:
        at = source[AXIS[axis]]
        for here in ["up", "down"] if axis == "z" else [axis]:
            if axis == "z":
                if here == side:
                    return base + number * NZ + at
                base += ahead * NZ
            else:
                if here == side:
                    return base + number
                base += ahead
        number = number * sizes[axis] + at
        ahead *= sizes[axis]
    return base


def slot_count(order):
    return slot_of(order, None, (0, 0, 0))


def scatter_kernel(numbers, pieces, *refs):
    many = len(numbers)
    count = len(pieces)
    take = iter(refs)
    partials = [next(take) for _ in range(1 + max(p[1] for p in pieces))]
    named = lambda: dict(zip(numbers, [next(take) for _ in range(many)]))
    outs, own, pair, total, handed = named(), named(), named(), named(), named()
    slots = [next(take) for _ in range(count)]
    base = {p[0]: p[2] for p in pieces}
    array = {p[0]: p[1] for p in pieces}
    (
        own_sem,
        pair_send,
        pair_recv,
        send_sem,
        recv_sem,
        end_send,
        end_recv,
        out_sem,
    ) = take
    spot = place()
    z, y, x, core = spot
    me = chip_number(z, y, x)
    partner = neighbour("core", spot)
    loads = {}
    for number in numbers:
        half = WIDTHS[number] // 2
        load = pltpu.make_async_copy(
            partials[array[number]].at[:, pl.ds(aligned(base[number] + core * half, 128), half)],
            own[number],
            own_sem.at[number],
        )
        load.start()
        loads[number] = load
    greet(spot)
    swaps = {}
    for number in numbers:
        half = WIDTHS[number] // 2
        swap = pltpu.make_async_remote_copy(
            src_ref=partials[array[number]].at[
                :, pl.ds(aligned(base[number] + (1 - core) * half, 128), half)
            ],
            dst_ref=pair[number],
            send_sem=pair_send.at[number],
            recv_sem=pair_recv.at[number],
            device_id=partner,
            device_id_type=MESH,
        )
        swap.start()
        swaps[number] = swap
    ready = set()
    for away in reversed(offsets()):
        for index, piece in enumerate(pieces):
            number, _, _, chip_rows, low, rows, column, columns, order = piece
            if number not in ready:
                ready.add(number)
                loads[number].wait()
                swaps[number].wait_recv()
            sz, sy, sx, valid = source_of(spot, away)
            source = chip_number(sz, sy, sx)
            last = last_axis(order, away)

            def event(
                index=index, number=number, chip_rows=chip_rows, low=low, rows=rows,
                column=column, columns=columns, order=order, source=source, last=last,
                where=(sz, sy, sx),
            ):
                kids = children(order, away)
                for side in kids:

                    def arrived(side=side):
                        slot = slot_of(order, side, where)
                        pltpu.make_async_remote_copy(
                            src_ref=slots[index].at[slot],
                            dst_ref=slots[index].at[slot],
                            send_sem=send_sem.at[index, 0],
                            recv_sem=recv_sem.at[index, slot],
                            device_id=partner,
                            device_id_type=MESH,
                        ).wait_recv()

                    guarded(exists(side, z), arrived)
                view = (pl.ds(aligned(source * chip_rows + low, 16), rows), pl.ds(column, columns))
                value = own[number][view].astype(jnp.float32) + pair[number][view].astype(jnp.float32)
                for side in kids:
                    landed = slots[index][slot_of(order, side, where)].astype(jnp.float32)
                    there = exists(side, z)
                    value = value + (landed if there is None else jnp.where(there, landed, 0.0))
                if last < 0:
                    total[number][pl.ds(low, rows), pl.ds(column, columns)] = value
                    return
                pair[number][view] = value.astype(jnp.bfloat16)
                axis = order[last]
                if axis == "z":
                    side = "up" if away[0] < 0 else "down"
                    parent = neighbour("down" if away[0] < 0 else "up", spot)
                else:
                    side = axis
                    parent = neighbour(axis, spot)
                slot = slot_of(order, side, where)
                pltpu.make_async_remote_copy(
                    src_ref=pair[number].at[view],
                    dst_ref=slots[index].at[slot],
                    send_sem=send_sem.at[index, source],
                    recv_sem=recv_sem.at[index, slot],
                    device_id=parent,
                    device_id_type=MESH,
                ).start()

            guarded(valid, event)
    ends = {}
    for number in numbers:
        rows = OWN_ROWS[number]
        end = pltpu.make_async_remote_copy(
            src_ref=total[number].at[pl.ds(aligned((1 - core) * rows, 8), rows)],
            dst_ref=handed[number],
            send_sem=end_send.at[number],
            recv_sem=end_recv.at[number],
            device_id=partner,
            device_id_type=MESH,
        )
        end.start()
        ends[number] = end
    writes = []
    for number in numbers:
        rows = OWN_ROWS[number]
        half = WIDTHS[number] // 2
        write = pltpu.make_async_copy(
            total[number].at[pl.ds(aligned(core * rows, 8), rows)],
            outs[number].at[:, pl.ds(aligned(core * half, 128), half)],
            out_sem.at[number],
        )
        write.start()
        writes.append(write)
    for number in numbers:
        half = WIDTHS[number] // 2
        ends[number].wait_recv()
        write = pltpu.make_async_copy(
            handed[number],
            outs[number].at[:, pl.ds(aligned((1 - core) * half, 128), half)],
            out_sem.at[8 + number],
        )
        write.start()
        writes.append(write)
    for write in writes:
        write.wait()
    for end in ends.values():
        end.wait_send()
    for swap in swaps.values():
        swap.wait_send()
    for index, piece in enumerate(pieces):
        number, _, _, chip_rows, low, rows, column, columns, order = piece
        for away in offsets():
            if away == (0, 0, 0):
                continue
            sz, sy, sx, valid = source_of(spot, away)
            source = chip_number(sz, sy, sx)

            def sent(index=index, source=source):
                view = (pl.ds(aligned(source * chip_rows + low, 16), rows), pl.ds(column, columns))
                pltpu.make_async_remote_copy(
                    src_ref=pair[number].at[view],
                    dst_ref=slots[index].at[0],
                    send_sem=send_sem.at[index, source],
                    recv_sem=recv_sem.at[index, 0],
                    device_id=partner,
                    device_id_type=MESH,
                ).wait_send()

            guarded(valid, sent)


def scatter_layers(partials, ident):
    numbers = (5, 6, 7, 4, 0, 1, 2, 3)
    pieces = LATER_PIECES + PIECES
    count = len(pieces)
    most = max(slot_count(p[8]) for p in pieces)
    scratch = lambda rows, dtype: [
        pltpu.VMEM((rows * OWN_ROWS[n], WIDTHS[n] // 2), dtype) for n in numbers
    ]
    return dict(
        zip(
            numbers,
            pl.pallas_call(
                functools.partial(scatter_kernel, numbers, pieces),
                out_shape=tuple(
                    jax.ShapeDtypeStruct((OWN_ROWS[n], WIDTHS[n]), jnp.float32) for n in numbers
                ),
                in_specs=[pl.BlockSpec(memory_space=pl.ANY)] * len(partials),
                out_specs=tuple([pl.BlockSpec(memory_space=pl.ANY)] * len(numbers)),
                scratch_shapes=(
                    scratch(32, jnp.bfloat16)
                    + scratch(32, jnp.bfloat16)
                    + scratch(2, jnp.float32)
                    + scratch(1, jnp.float32)
                    + [pltpu.VMEM((slot_count(p[8]), p[5], p[7]), jnp.bfloat16) for p in pieces]
                    + [
                        pltpu.SemaphoreType.DMA((8,)),
                        pltpu.SemaphoreType.DMA((8,)),
                        pltpu.SemaphoreType.DMA((8,)),
                        pltpu.SemaphoreType.DMA((count, CHIPS)),
                        pltpu.SemaphoreType.DMA((count, most)),
                        pltpu.SemaphoreType.DMA((8,)),
                        pltpu.SemaphoreType.DMA((8,)),
                        pltpu.SemaphoreType.DMA((16,)),
                    ]
                ),
                name="scatter",
                compiler_params=pltpu.CompilerParams(
                    collective_id=ident, has_side_effects=True, vmem_limit_bytes=60 << 20
                ),
                cost_estimate=pl.CostEstimate(flops=0, bytes_accessed=int(2e8), transcendentals=0),
            )(*partials),
        )
    )


def normalize(values):
    centred = values - jnp.mean(values, axis=-1, keepdims=True)
    inverse = lax.rsqrt(jnp.mean(centred * centred, axis=-1, keepdims=True) + EPSILON)
    return (centred * inverse, inverse)


def normalize_back(grad_normed, normed, inverse):
    return inverse * (
        grad_normed
        - jnp.mean(grad_normed, axis=-1, keepdims=True)
        - normed * jnp.mean(grad_normed * normed, axis=-1, keepdims=True)
    )


def rotary_tables(relative):
    indices = jnp.arange(HEAD_DIM // 2).astype(jnp.float32)
    frequency = jnp.exp(indices * (-2.0 * math.log(10000.0) / HEAD_DIM))
    phase = relative.astype(jnp.float32)[:, None] * frequency[None, :]
    cosine, sine = jnp.cos(phase), jnp.sin(phase)
    return (
        jnp.concatenate([cosine] * 4, axis=1),
        jnp.concatenate([-sine, sine, -sine, sine], axis=1),
    )


BAND = 128
VARIANTS = (3, 4, 5, 6, 7, 9)
STEP_COLUMNS = 384
BLOCK = 512
F32 = jnp.float32
BF16 = jnp.bfloat16
MATMUL = (((1,), (0,)), ((), ()))
MATMUL_RIGHT = (((1,), (1,)), ((), ()))
MATMUL_LEFT = (((0,), (0,)), ((), ()))


def product(left, right, dims=MATMUL):
    return lax.dot_general(left, right, dims, preferred_element_type=F32)


def vmem(limit=56):
    return pltpu.CompilerParams(vmem_limit_bytes=limit << 20)


def cost(flops, moved):
    return pl.CostEstimate(flops=int(flops), bytes_accessed=int(moved), transcendentals=0)


def swap_halves(values):
    lane = lax.broadcasted_iota(jnp.int32, values.shape, 1)
    low = lax.rem(lane, HEAD_DIM) < HEAD_DIM // 2
    return jnp.where(
        low,
        pltpu.roll(values, 2 * HEAD_DIM - HEAD_DIM // 2, 1),
        pltpu.roll(values, HEAD_DIM // 2, 1),
    )


def turn(values, cosine, sine):
    parts = []
    for at in range(0, values.shape[1], 128):
        part = values[:, at : at + 128]
        parts.append(part * cosine + swap_halves(part) * sine)
    return jnp.concatenate(parts, axis=1)


def beside():
    dp, fs = lax.axis_index("dp"), lax.axis_index("fsdp")
    return ((dp, fs - 1), fs > 0), ((dp, fs + 1), fs < lax.axis_size("fsdp") - 1)


def greet_beside():
    barrier = pltpu.get_barrier_semaphore()
    count = 0
    for device_at, there in beside():

        @pl.when(there)
        def _(device_at=device_at):
            pl.semaphore_signal(barrier, inc=1, device_id=device_at, device_id_type=MESH)

        count = count + jnp.where(there, 1, 0)
    pl.semaphore_wait(barrier, count)


def halo_copies(sources, landing, send_sem, recv_sem):
    return [
        (
            there,
            pltpu.make_async_remote_copy(
                src_ref=sources[side],
                dst_ref=landing.at[1 - side],
                send_sem=send_sem.at[side],
                recv_sem=recv_sem.at[1 - side],
                device_id=device_at,
                device_id_type=MESH,
            ),
        )
        for side, (device_at, there) in enumerate(beside())
    ]


def halo_start(sources, landing, send_sem, recv_sem):
    for there, copy in halo_copies(sources, landing, send_sem, recv_sem):
        pl.when(there)(copy.start)


def halo_wait(sources, landing, send_sem, recv_sem):
    sides = beside()
    for side, (there, copy) in enumerate(halo_copies(sources, landing, send_sem, recv_sem)):
        pl.when(there)(copy.wait_send)
        device_at, _ = sides[side]

        @pl.when(there)
        def _(side=side, device_at=device_at):
            pltpu.make_async_remote_copy(
                src_ref=sources[side],
                dst_ref=landing.at[side],
                send_sem=send_sem.at[side],
                recv_sem=recv_sem.at[side],
                device_id=device_at,
                device_id_type=MESH,
            ).wait_recv()

        @pl.when(jnp.logical_not(there))
        def _(side=side):
            landing[side] = jnp.zeros(landing.shape[1:], landing.dtype)


def project_kernel(
    x_ref, w_ref, bias_ref, mod_ref, cos_ref, sin_ref, q_ref, own_ref, low_ref, high_ref, h_ref, halo_ref,
    mine, landing, send_sem, recv_sem,
):
    step = pl.program_id(0)
    rows = x_ref.shape[0]

    @pl.when(step == 0)
    def _():
        normed, _ = normalize(x_ref[...].astype(F32))
        hidden_in = (normed * (1.0 + mod_ref[1:2]) + mod_ref[0:1]).astype(BF16)
        mine[...] = hidden_in
        h_ref[...] = hidden_in
        greet_beside()
        halo_start((mine, mine), landing, send_sem, recv_sem)

    def own_turned(y):
        return turn(y, cos_ref[WIN_MAX : WIN_MAX + rows], sin_ref[WIN_MAX : WIN_MAX + rows]).astype(BF16)

    @pl.when(step < 6)
    def _():
        y = product(mine[...], w_ref[...]) + bias_ref[...]

        @pl.when(step < 2)
        def _():
            q_ref[...] = own_turned(y)

        @pl.when((step >= 2) & (step < 4))
        def _():
            own_ref[0] = own_turned(y)

        @pl.when(step >= 4)
        def _():
            own_ref[0] = y.astype(BF16)

    @pl.when(step == 6)
    def _():
        halo_wait((mine, mine), landing, send_sem, recv_sem)
        halo_ref[...] = landing[...]

    @pl.when(step >= 6)
    def _():
        for side, out_ref, first in ((0, low_ref, 0), (1, high_ref, WIN_MAX + rows)):
            y = product(landing[side], w_ref[...]) + bias_ref[...]

            @pl.when(step < 8)
            def _(y=y, out_ref=out_ref, first=first):
                table = slice(first, first + WIN_MAX)
                out_ref[0] = turn(y, cos_ref[table], sin_ref[table]).astype(BF16)

            @pl.when(step >= 8)
            def _(y=y, out_ref=out_ref):
                out_ref[0] = y.astype(BF16)


def project(stream, square, bias, modulation, cosine, sine, ident):
    rows = stream.shape[0]
    whole = lambda shape: pl.BlockSpec(shape, lambda c: (0,) * len(shape))

    def halves(first):
        def index(c):
            at = jnp.clip(c - first, 0, 3)
            return (at // 2, 0, at % 2)

        return pl.BlockSpec((1, rows, STEP_COLUMNS), index)

    column = lambda c: (0, jnp.where(c < 6, c, c - 4))
    pair = jax.ShapeDtypeStruct((2, rows, D), BF16)
    single = jax.ShapeDtypeStruct((rows, D), BF16)
    return pl.pallas_call(
        project_kernel,
        grid=(10,),
        in_specs=[
            whole((rows, D)),
            pl.BlockSpec((D, STEP_COLUMNS), column),
            pl.BlockSpec((1, STEP_COLUMNS), column),
            whole((4, D)),
            whole((rows + 2 * WIN_MAX, 128)),
            whole((rows + 2 * WIN_MAX, 128)),
        ],
        out_specs=(
            pl.BlockSpec((rows, STEP_COLUMNS), lambda c: (0, jnp.minimum(c, 1))),
            halves(2),
            halves(6),
            halves(6),
            whole((rows, D)),
            whole((2, rows, D)),
        ),
        out_shape=(single, pair, pair, pair, single, pair),
        scratch_shapes=[
            pltpu.VMEM((rows, D), BF16),
            pltpu.VMEM((2, rows, D), BF16),
            pltpu.SemaphoreType.DMA((2,)),
            pltpu.SemaphoreType.DMA((2,)),
        ],
        compiler_params=pltpu.CompilerParams(
            vmem_limit_bytes=56 << 20, collective_id=ident, has_side_effects=True
        ),
        cost_estimate=cost(2 * rows * D * 7 * D, 8e6),
        name="project",
    )(stream, square, bias, modulation, cosine, sine)


def stack_heads(pair):
    lane = lax.broadcasted_iota(jnp.int32, pair.shape, 1)
    zero = jnp.zeros_like(pair)
    return jnp.concatenate(
        [jnp.where(lane < HEAD_DIM, pair, zero), jnp.where(lane < HEAD_DIM, zero, pair)], axis=0
    )


def merge_heads(stacked):
    rows = stacked.shape[0] // 2
    lane = lax.broadcasted_iota(jnp.int32, (rows, stacked.shape[1]), 1)
    return jnp.where(lane < HEAD_DIM, stacked[:rows], stacked[rows:])


def over_bands(bounds_ref, count, action):
    def one(number, carry):
        low, need = bounds_ref[0, number], bounds_ref[1, number]
        before = 0
        for size in VARIANTS:

            @pl.when((need > before) & (need <= size))
            def _(size=size):
                start = jnp.minimum(low, count - size) * BAND
                action(pl.multiple_of(number * BAND, BAND), pl.multiple_of(start, BAND), size * BAND)

            before = size
        return carry

    lax.fori_loop(0, bounds_ref.shape[1], one, 0)


def attend_kernel(bounds_ref, q_ref, low_ref, own_ref, high_ref, idq_ref, idk_ref, o_ref, lse_ref, ext):
    rows = own_ref.shape[1]
    for at in range(2):
        ext[at, :WIN_MAX] = low_ref[at]
        ext[at, WIN_MAX : WIN_MAX + rows] = own_ref[at]
        ext[at, WIN_MAX + rows :] = high_ref[at]

    def block(first, start, size):
        mine = pl.ds(first, BAND)
        queries = stack_heads(q_ref[mine, :]) * jnp.asarray(HEAD_DIM**-0.5, BF16)
        keys = ext[0, pl.ds(start, size), :]
        scores = product(queries, keys, MATMUL_RIGHT)
        ids = idq_ref[mine, :]
        allowed = jnp.concatenate([ids] * (size // BAND), axis=1) == idk_ref[0:1, pl.ds(start, size)]
        scores = jnp.where(jnp.concatenate([allowed, allowed], axis=0), scores, NEGATIVE)
        peak = jnp.max(scores, axis=1, keepdims=True)
        weights = jnp.exp(scores - peak)
        total = jnp.sum(weights, axis=1, keepdims=True)
        values = ext[1, pl.ds(start, size), :]
        mixed = product(weights.astype(BF16), values) * (1.0 / total)
        o_ref[mine, :] = merge_heads(mixed).astype(BF16)
        wide = jnp.broadcast_to(peak + jnp.log(total), (2 * BAND, BAND))
        lse_ref[0, 0:1, mine] = wide[:BAND].T[0:1]
        lse_ref[0, 1:2, mine] = wide[BAND:].T[0:1]

    over_bands(bounds_ref, (rows + 2 * WIN_MAX) // BAND, block)


def pair_spec(rows):
    return pl.BlockSpec((2, rows, 128), lambda j, b: (0, 0, j))


def attend(bounds, queries, low, own, high, ids_query, ids_key):
    rows = queries.shape[0]
    wide = rows + 2 * WIN_MAX
    column = pl.BlockSpec((rows, 128), lambda j, b: (0, j))
    return pl.pallas_call(
        attend_kernel,
        grid_spec=pltpu.PrefetchScalarGridSpec(
            num_scalar_prefetch=1,
            grid=(HEADS // 2,),
            in_specs=[
                column,
                pair_spec(WIN_MAX),
                pair_spec(rows),
                pair_spec(WIN_MAX),
                pl.BlockSpec((rows, 128), lambda j, b: (0, 0)),
                pl.BlockSpec((8, wide), lambda j, b: (0, 0)),
            ],
            out_specs=(column, pl.BlockSpec((1, 8, rows), lambda j, b: (j, 0, 0))),
            scratch_shapes=[pltpu.VMEM((2, wide, 128), BF16)],
        ),
        out_shape=(
            jax.ShapeDtypeStruct((rows, D), BF16),
            jax.ShapeDtypeStruct((HEADS // 2, 8, rows), F32),
        ),
        compiler_params=vmem(),
        cost_estimate=cost(5e9, 8e6),
        name="attend",
    )(bounds, queries, low, own, high, ids_query, ids_key)


def attend_back_kernel(
    bounds_ref, q_ref, g_ref, o_ref, lse_ref, low_ref, own_ref, high_ref, idq_ref, idk_ref,
    cos_ref, sin_ref, dq_ref, dlow_ref, down_ref, dhigh_ref, ext, dext,
):
    rows = own_ref.shape[1]
    for at in range(2):
        ext[at, :WIN_MAX] = low_ref[at]
        ext[at, WIN_MAX : WIN_MAX + rows] = own_ref[at]
        ext[at, WIN_MAX + rows :] = high_ref[at]
    dext[...] = jnp.zeros_like(dext)

    def block(first, start, size):
        mine = pl.ds(first, BAND)
        band = pl.ds(start, size)
        queries = stack_heads(q_ref[mine, :]) * jnp.asarray(HEAD_DIM**-0.5, BF16)
        grads = stack_heads(g_ref[mine, :])
        keys = ext[0, band, :]
        scores = product(keys, queries, MATMUL_RIGHT)
        ids = idk_ref[band, :] == idq_ref[0:1, mine]
        allowed = jnp.concatenate([ids, ids], axis=1)
        lse = jnp.concatenate([lse_ref[0, 0:1, mine], lse_ref[0, 1:2, mine]], axis=1)
        weights = jnp.where(allowed, jnp.exp(scores - lse), 0.0)
        both_heads = (g_ref[mine, :].astype(F32) * o_ref[mine, :].astype(F32)).T
        delta = jnp.concatenate(
            [
                jnp.sum(both_heads[:HEAD_DIM], axis=0, keepdims=True),
                jnp.sum(both_heads[HEAD_DIM:], axis=0, keepdims=True),
            ],
            axis=1,
        )
        values = ext[1, band, :]
        grad_weights = product(values, grads, MATMUL_RIGHT)
        grad_scores = (weights * (grad_weights - delta)).astype(BF16)
        dext[0, band, :] += product(grad_scores, queries)
        dext[1, band, :] += product(weights.astype(BF16), grads)
        grad_queries = merge_heads(product(grad_scores, keys, MATMUL_LEFT)) * HEAD_DIM**-0.5
        table = pl.ds(pl.multiple_of(first + WIN_MAX, BAND), BAND)
        dq_ref[mine, :] = turn(grad_queries, cos_ref[table, :], -sin_ref[table, :]).astype(BF16)

    over_bands(bounds_ref, (rows + 2 * WIN_MAX) // BAND, block)
    for out_ref, part in (
        (dlow_ref, slice(0, WIN_MAX)),
        (down_ref, slice(WIN_MAX, WIN_MAX + rows)),
        (dhigh_ref, slice(WIN_MAX + rows, 2 * WIN_MAX + rows)),
    ):
        out_ref[0] = turn(dext[0, part], cos_ref[part], -sin_ref[part]).astype(BF16)
        out_ref[1] = dext[1, part].astype(BF16)


def attend_back(bounds, queries, grads, attended, lse, low, own, high, ids_query, ids_key, cosine, sine):
    rows = queries.shape[0]
    wide = rows + 2 * WIN_MAX
    column = pl.BlockSpec((rows, 128), lambda j, b: (0, j))
    fixed = lambda shape: pl.BlockSpec(shape, lambda j, b: (0,) * len(shape))
    return pl.pallas_call(
        attend_back_kernel,
        grid_spec=pltpu.PrefetchScalarGridSpec(
            num_scalar_prefetch=1,
            grid=(HEADS // 2,),
            in_specs=[
                column,
                column,
                column,
                pl.BlockSpec((1, 8, rows), lambda j, b: (j, 0, 0)),
                pair_spec(WIN_MAX),
                pair_spec(rows),
                pair_spec(WIN_MAX),
                fixed((8, rows)),
                fixed((wide, 128)),
                fixed((wide, 128)),
                fixed((wide, 128)),
            ],
            out_specs=(column, pair_spec(WIN_MAX), pair_spec(rows), pair_spec(WIN_MAX)),
            scratch_shapes=[pltpu.VMEM((2, wide, 128), BF16), pltpu.VMEM((2, wide, 128), F32)],
        ),
        out_shape=(
            jax.ShapeDtypeStruct((rows, D), BF16),
            jax.ShapeDtypeStruct((2, WIN_MAX, D), BF16),
            jax.ShapeDtypeStruct((2, rows, D), BF16),
            jax.ShapeDtypeStruct((2, WIN_MAX, D), BF16),
        ),
        compiler_params=vmem(),
        cost_estimate=cost(12e9, 16e6),
        name="attend_back",
    )(bounds, queries, grads, attended, lse, low, own, high, ids_query, ids_key, cosine, sine)


def feed_kernel(
    o_ref, x_ref, wo_ref, we_ref, ws_ref, bo_ref, be_ref, bs_ref, mod_ref,
    mid_ref, h_ref, z_ref, slope_ref, out_ref,
):
    step = pl.program_id(0)

    @pl.when(step == 0)
    def _():
        middle = x_ref[...].astype(F32) + (product(o_ref[...], wo_ref[...]) + bo_ref[...])
        mid_ref[...] = middle
        normed, _ = normalize(middle)
        h_ref[...] = (normed * (1.0 + mod_ref[3:4]) + mod_ref[2:3]).astype(BF16)
        out_ref[...] = middle + bs_ref[...]

    u = product(h_ref[...], we_ref[...]) + be_ref[...]
    share = 0.5 + 0.5 * lax.erf(u * (0.5**0.5))
    active = (u * share).astype(BF16)
    z_ref[...] = active
    slope_ref[...] = (share + u * (jnp.exp(-0.5 * u * u) * (2.0 * math.pi) ** -0.5)).astype(BF16)
    out_ref[...] += product(active, ws_ref[...])


def feed(attended, stream, square, shrink, bias, modulation):
    rows = stream.shape[0]
    whole = lambda shape: pl.BlockSpec(shape, lambda c: (0,) * len(shape))
    width = STEP_COLUMNS
    return pl.pallas_call(
        feed_kernel,
        grid=(FF // width,),
        in_specs=[
            whole((rows, D)),
            whole((rows, D)),
            pl.BlockSpec((D, D), lambda c: (0, 3)),
            pl.BlockSpec((D, width), lambda c: (0, 4 * D // width + c)),
            pl.BlockSpec((width, D), lambda c: (c, 0)),
            pl.BlockSpec((1, D), lambda c: (0, 3)),
            pl.BlockSpec((1, width), lambda c: (0, 4 * D // width + c)),
            pl.BlockSpec((1, D), lambda c: (0, 8)),
            whole((4, D)),
        ],
        out_specs=(
            whole((rows, D)),
            whole((rows, D)),
            pl.BlockSpec((rows, width), lambda c: (0, c)),
            pl.BlockSpec((rows, width), lambda c: (0, c)),
            whole((rows, D)),
        ),
        out_shape=(
            jax.ShapeDtypeStruct((rows, D), F32),
            jax.ShapeDtypeStruct((rows, D), BF16),
            jax.ShapeDtypeStruct((rows, FF), BF16),
            jax.ShapeDtypeStruct((rows, FF), BF16),
            jax.ShapeDtypeStruct((rows, D), F32),
        ),
        compiler_params=vmem(),
        cost_estimate=cost(2 * rows * D * (D + 2 * FF), 24e6),
        name="feed",
    )(attended, stream, square, square, shrink, bias, bias, bias, modulation)


def feed_back_kernel(
    g_ref, z_ref, slope_ref, h_ref, mid_ref, o_ref, we_ref, ws_ref, wo_ref, mod_ref,
    square_ref, dshr_ref, mid_grad_ref, do_ref, dbe_ref, sums_ref,
    low, turned, total,
):
    step = pl.program_id(0)
    chunks = FF // STEP_COLUMNS

    @pl.when(step == 0)
    def _():
        low[...] = g_ref[...].astype(BF16)
        turned[...] = h_ref[...].T
        total[...] = jnp.zeros_like(total)
        sums_ref[3:4] = jnp.sum(low[...].astype(F32), axis=0, keepdims=True)

    @pl.when(step < chunks)
    def _():
        grad_active = product(low[...], ws_ref[...], MATMUL_RIGHT)
        grad_hidden = (grad_active * slope_ref[...].astype(F32)).astype(BF16)
        dbe_ref[...] = jnp.sum(grad_hidden.astype(F32), axis=0, keepdims=True)
        dshr_ref[...] = product(z_ref[...], low[...], MATMUL_LEFT).astype(BF16)
        square_ref[...] = product(turned[...], grad_hidden).astype(BF16)
        total[...] += product(grad_hidden, we_ref[...], MATMUL_RIGHT)

    @pl.when(step == chunks)
    def _():
        normed, inverse = normalize(mid_ref[...])
        grad = total[...]
        sums_ref[0:1] = jnp.sum(grad, axis=0, keepdims=True)
        sums_ref[1:2] = jnp.sum(grad * normed, axis=0, keepdims=True)
        middle = g_ref[...].astype(F32) + normalize_back(grad * (1.0 + mod_ref[3:4]), normed, inverse)
        mid_grad_ref[...] = middle
        low[...] = middle.astype(BF16)
        sums_ref[2:3] = jnp.sum(low[...].astype(F32), axis=0, keepdims=True)
        do_ref[...] = product(low[...], wo_ref[...], MATMUL_RIGHT).astype(BF16)
        turned[...] = o_ref[...].T
        square_ref[...] = product(turned[...], low[:, :STEP_COLUMNS]).astype(BF16)

    @pl.when(step == chunks + 1)
    def _():
        square_ref[...] = product(turned[...], low[:, STEP_COLUMNS:]).astype(BF16)


def feed_back(grad, active, slope, hidden_in, middle, attended, square, shrink, modulation):
    rows = grad.shape[0]
    whole = lambda shape: pl.BlockSpec(shape, lambda c: (0,) * len(shape))
    width = STEP_COLUMNS
    chunks = FF // width
    upto = lambda c: jnp.minimum(c, chunks - 1)
    return pl.pallas_call(
        feed_back_kernel,
        grid=(chunks + 2,),
        in_specs=[
            whole((rows, D)),
            pl.BlockSpec((rows, width), lambda c: (0, upto(c))),
            pl.BlockSpec((rows, width), lambda c: (0, upto(c))),
            whole((rows, D)),
            whole((rows, D)),
            whole((rows, D)),
            pl.BlockSpec((D, width), lambda c: (0, 4 * D // width + upto(c))),
            pl.BlockSpec((width, D), lambda c: (upto(c), 0)),
            pl.BlockSpec((D, D), lambda c: (0, 3)),
            whole((4, D)),
        ],
        out_specs=(
            pl.BlockSpec(
                (D, width),
                lambda c: (0, jnp.where(c < chunks, 4 * D // width + c, 3 * D // width + c - chunks)),
            ),
            pl.BlockSpec((width, D), lambda c: (upto(c), 0)),
            whole((rows, D)),
            whole((rows, D)),
            pl.BlockSpec((1, width), lambda c: (0, upto(c))),
            whole((4, D)),
        ),
        out_shape=(
            jax.ShapeDtypeStruct((D, 4 * D + FF), BF16),
            jax.ShapeDtypeStruct((FF, D), BF16),
            jax.ShapeDtypeStruct((rows, D), F32),
            jax.ShapeDtypeStruct((rows, D), BF16),
            jax.ShapeDtypeStruct((1, FF), F32),
            jax.ShapeDtypeStruct((4, D), F32),
        ),
        scratch_shapes=[
            pltpu.VMEM((rows, D), BF16),
            pltpu.VMEM((D, rows), BF16),
            pltpu.VMEM((rows, D), F32),
        ],
        compiler_params=vmem(),
        cost_estimate=cost(4 * rows * D * (D + 2 * FF), 40e6),
        name="feed_back",
    )(grad, active, slope, hidden_in, middle, attended, square, shrink, square, modulation)


def project_back_kernel(
    dq_ref, low_ref, own_ref, high_ref, h_ref, halo_ref, x_ref, mid_grad_ref, w_ref, mod_ref,
    square_in, square_ref, out_ref, db_ref, sums_ref,
    turned, total, around, sending, landing, send_sem, recv_sem,
):
    step = pl.program_id(0)
    rows = x_ref.shape[0]
    middle = slice(WIN_MAX, WIN_MAX + rows)
    sources = (sending.at[0], sending.at[1])

    @pl.when(step == 0)
    def _():
        around[...] = jnp.zeros_like(around)
        total[...] = jnp.zeros_like(total)
        greet_beside()

    @pl.when(step < 4)
    def _():
        around[0] += product(low_ref[0], w_ref[...], MATMUL_RIGHT)
        around[1] += product(high_ref[0], w_ref[...], MATMUL_RIGHT)

    @pl.when(step == 3)
    def _():
        sending[...] = around[...].astype(BF16)
        halo_start(sources, landing, send_sem, recv_sem)
        turned[:, :WIN_MAX] = halo_ref[0].T
        turned[:, middle] = h_ref[...].T
        turned[:, WIN_MAX + rows :] = halo_ref[1].T

    @pl.when((step >= 4) & (step < 6))
    def _():
        grad = dq_ref[...]
        db_ref[...] = jnp.sum(grad.astype(F32), axis=0, keepdims=True)
        square_ref[...] = product(turned[:, middle], grad).astype(BF16)
        total[...] += product(grad, w_ref[...], MATMUL_RIGHT)

    @pl.when(step >= 6)
    def _():
        grad = jnp.concatenate([low_ref[0], own_ref[0], high_ref[0]], axis=0)
        db_ref[...] = jnp.sum(grad.astype(F32), axis=0, keepdims=True)
        square_ref[...] = product(turned[...], grad).astype(BF16)
        total[...] += product(own_ref[0], w_ref[...], MATMUL_RIGHT)

    @pl.when(step == 9)
    def _():
        halo_wait(sources, landing, send_sem, recv_sem)
        normed, inverse = normalize(x_ref[...].astype(F32))
        grad = total[...] + landing[0].astype(F32) + landing[1].astype(F32)
        sums_ref[0:1] = jnp.sum(grad, axis=0, keepdims=True)
        sums_ref[1:2] = jnp.sum(grad * normed, axis=0, keepdims=True)
        out_ref[...] = mid_grad_ref[...] + normalize_back(
            grad * (1.0 + mod_ref[1:2]), normed, inverse
        )


def project_back(dq, low, own, high, hidden_in, halo, stream, mid_grad, square, modulation, square_grad, ident):
    rows = dq.shape[0]
    width = STEP_COLUMNS
    whole = lambda shape: pl.BlockSpec(shape, lambda c: (0,) * len(shape))

    def halves(c):
        at = jnp.where(c < 4, c, jnp.clip(c - 6, 0, 3))
        return (at // 2, 0, at % 2)

    later = pl.BlockSpec((1, rows, width), halves)
    own_columns = lambda c: (0, jnp.clip(c - 4, 0, 5))
    return pl.pallas_call(
        project_back_kernel,
        grid=(10,),
        in_specs=[
            pl.BlockSpec((rows, width), lambda c: (0, jnp.clip(c - 4, 0, 1))),
            later,
            later,
            later,
            whole((rows, D)),
            whole((2, rows, D)),
            whole((rows, D)),
            whole((rows, D)),
            pl.BlockSpec((D, width), lambda c: (0, jnp.where(c < 4, c + 2, c - 4))),
            whole((4, D)),
            pl.BlockSpec(memory_space=pl.ANY),
        ],
        out_specs=(
            pl.BlockSpec((D, width), own_columns),
            whole((rows, D)),
            pl.BlockSpec((1, width), own_columns),
            whole((2, D)),
        ),
        out_shape=(
            jax.ShapeDtypeStruct((D, 4 * D + FF), BF16),
            jax.ShapeDtypeStruct((rows, D), F32),
            jax.ShapeDtypeStruct((1, 3 * D), F32),
            jax.ShapeDtypeStruct((2, D), F32),
        ),
        scratch_shapes=[
            pltpu.VMEM((D, rows + 2 * WIN_MAX), BF16),
            pltpu.VMEM((rows, D), F32),
            pltpu.VMEM((2, rows, D), F32),
            pltpu.VMEM((2, rows, D), BF16),
            pltpu.VMEM((2, rows, D), BF16),
            pltpu.SemaphoreType.DMA((2,)),
            pltpu.SemaphoreType.DMA((2,)),
        ],
        input_output_aliases={10: 0},
        compiler_params=pltpu.CompilerParams(
            vmem_limit_bytes=56 << 20, collective_id=ident, has_side_effects=True
        ),
        cost_estimate=cost(4 * rows * D * 6 * D, 20e6),
        name="project_back",
    )(dq, low, own, high, hidden_in, halo, stream, mid_grad, square, modulation, square_grad)


def direct():
    return lax.axis_size("dp") == NZ * NY and lax.axis_size("fsdp") == NX * 2


BOTH = ("dp", "fsdp")


def pack_small(bias, table):
    flat = jnp.concatenate([bias.reshape(-1), table.reshape(-1)])
    flat = jnp.pad(flat, (0, OWN_ROWS[4] * SMALL - flat.shape[0]))
    return flat.reshape(1, OWN_ROWS[4], SMALL)


def unpack_small(whole, lead_row):
    count = lax.axis_size("dp") * lax.axis_size("fsdp")
    flat = whole.reshape(count, -1).astype(F32)
    wide = LAYERS * 9 * D // count
    bias = flat[:, :wide].reshape(count, LAYERS, 9, -1).transpose(1, 2, 0, 3).reshape(LAYERS, 9 * D)
    table = flat[:, wide : wide + LAYERS * LEADS * 4 * D // count].reshape(count, LAYERS, LEADS, -1)
    rows = lax.dynamic_index_in_dim(table, lead_row, 2, keepdims=False)
    return bias, rows.transpose(1, 0, 2).reshape(LAYERS, 4, D)


def plain_fetch(masters, layer):
    square = jnp.concatenate([masters[n][layer].astype(BF16) for n in range(3)], axis=1)
    shrink = masters[3][layer].astype(BF16)
    return (
        lax.all_gather(square, BOTH, axis=0, tiled=True),
        lax.all_gather(shrink, BOTH, axis=0, tiled=True),
    )


def fetch_layers(masters, lead_row):
    if direct():
        small = pack_small(masters[4], masters[5])
        *first, whole = gather_layer(0, (*masters[:4], small), 0)
        bias, modulation = unpack_small(whole, lead_row)
        layers = [tuple(first)]
    else:
        bias = lax.all_gather(masters[4].astype(BF16), BOTH, axis=2, tiled=True)
        bias = bias.astype(F32).reshape(LAYERS, 9 * D)
        table = lax.all_gather(masters[5].astype(BF16), BOTH, axis=2, tiled=True)
        modulation = lax.dynamic_index_in_dim(table, lead_row, 1, keepdims=False)
        modulation = modulation.astype(F32).reshape(LAYERS, 4, D)
        layers = [plain_fetch(masters, 0)]
    for layer in range(1, LAYERS):
        layers.append(plain_fetch(masters, layer))
    return layers, bias, modulation


def plain_reduce(square, shrink):
    square = lax.psum_scatter(square, BOTH, scatter_dimension=0, tiled=True).astype(F32)
    shrink = lax.psum_scatter(shrink, BOTH, scatter_dimension=0, tiled=True).astype(F32)
    return [square[:, : 3 * D], square[:, 3 * D : 4 * D], square[:, 4 * D :], shrink]


def reduce_small_inputs(bias_grads, rows_grads, lead_hot):
    count = lax.axis_size("dp") * lax.axis_size("fsdp")
    bias = bias_grads.reshape(LAYERS * 9, count, -1).transpose(1, 0, 2).reshape(count, -1)
    rows = rows_grads.reshape(LAYERS, 1, count, -1) * lead_hot[None, :, None, None]
    rows = rows.transpose(2, 0, 1, 3).reshape(count, -1)
    flat = jnp.concatenate([bias, rows], axis=1)
    used = flat.shape[1]
    flat = jnp.pad(flat, ((0, 0), (0, OWN_ROWS[4] * SMALL - used)))
    return flat.reshape(-1, SMALL).astype(BF16)


def split_small(own):
    count = lax.axis_size("dp") * lax.axis_size("fsdp")
    flat = own.reshape(-1)
    wide = LAYERS * 9 * D // count
    used = wide + LAYERS * LEADS * 4 * D // count
    return flat[:wide].reshape(LAYERS, 9, -1), flat[wide:used].reshape(LAYERS, LEADS, -1)


def bands(segment_ids, segment_starts, padding_mask, offset, rows):
    length = segment_ids.shape[0]
    position = jnp.arange(length, dtype=jnp.int32)
    real = padding_mask == 1
    names = jnp.where(real, segment_ids, length + position)
    fill = jnp.full((WIN_MAX,), -1, jnp.int32)
    wide = lax.dynamic_slice_in_dim(
        jnp.concatenate([fill, names, fill - 1]), offset, rows + 2 * WIN_MAX
    )
    own = lax.dynamic_slice_in_dim(names, offset, rows)
    at = offset + jnp.arange(rows // BAND, dtype=jnp.int32) * BAND
    last = at + BAND - 1
    begins = jnp.where(real, segment_starts, position)[at]
    ends = jnp.sum((segment_ids[None, :] <= segment_ids[last][:, None]).astype(jnp.int32), axis=1)
    ends = jnp.where(real[last], ends, last + 1)
    low = (begins - offset + WIN_MAX) // BAND
    need = (ends - offset + WIN_MAX + BAND - 1) // BAND - low
    return jnp.stack([low, need]), own, wide


def adam_update(weight, gradient, moment, square, step_rate, decay_rate):
    moment = BETA_ONE * moment + (1.0 - BETA_ONE) * gradient
    square = BETA_TWO * square + (1.0 - BETA_TWO) * gradient * gradient
    first_fix = 1.0 - BETA_ONE**STEP
    second_fix = 1.0 - BETA_TWO**STEP
    update = moment / first_fix / (jnp.sqrt(square / second_fix) + ADAM_EPSILON)
    weight = weight - step_rate * (update + decay_rate * weight)
    return (weight, moment, square, weight.astype(jnp.bfloat16))


def shards(
    tokens,
    cotangent,
    segment_ids,
    segment_starts,
    padding_mask,
    lead_index,
    input_weights,
    input_moment,
    input_square,
    output_weights,
    output_moment,
    output_square,
    expand_weights,
    expand_moment,
    expand_square,
    shrink_weights,
    shrink_moment,
    shrink_square,
    bias_vector,
    bias_moment,
    bias_square,
    lead_table,
    lead_moment,
    lead_square,
):
    rows = tokens.shape[0]
    offset = lax.axis_index("fsdp") * rows
    bounds, own_names, wide_names = bands(segment_ids, segment_starts, padding_mask, offset, rows)
    ids_query = jnp.broadcast_to(own_names[:, None], (rows, 128))
    ids_key = jnp.broadcast_to(wide_names[None, :], (8, wide_names.shape[0]))
    ids_query_row = jnp.broadcast_to(own_names[None, :], (8, rows))
    ids_key_column = jnp.broadcast_to(wide_names[:, None], (wide_names.shape[0], 128))
    fill = jnp.zeros((WIN_MAX,), jnp.int32)
    relative = jnp.arange(segment_starts.shape[0], dtype=jnp.int32) - segment_starts
    relative = jnp.concatenate([fill, relative, fill])
    cosine, sine = rotary_tables(
        lax.dynamic_slice_in_dim(relative, offset, rows + 2 * WIN_MAX)
    )
    lead_row = lead_index[0]
    lead_hot = (jnp.arange(LEADS, dtype=jnp.int32) == lead_row).astype(F32)
    masters = (input_weights, output_weights, expand_weights, shrink_weights, bias_vector, lead_table)
    layers, bias, modulation = fetch_layers(masters, lead_row)
    stream = tokens
    saved = []
    for layer in range(LAYERS):
        square, shrink = layers[layer]
        own_bias, own_mod = bias[layer][None], modulation[layer]
        queries, own, low, high, first_in, halo = project(
            stream, square, own_bias, own_mod, cosine, sine, 2 * LAYERS + layer
        )
        attended, lse = attend(bounds, queries, low, own, high, ids_query, ids_key)
        middle, second_in, active, slope, result = feed(
            attended, stream, square, shrink, own_bias, own_mod
        )
        saved.append(
            (stream, queries, low, own, high, first_in, halo, attended, lse, middle, second_in, active, slope)
        )
        stream = result
    grad = cotangent
    reduced = [None] * LAYERS
    bias_grads = [None] * LAYERS
    rows_grads = [None] * LAYERS
    for layer in reversed(range(LAYERS)):
        square, shrink = layers[layer]
        own_mod = modulation[layer]
        (
            before, queries, low, own, high, first_in, halo, attended, lse, middle, second_in, active, slope,
        ) = saved[layer]
        square_grad, shrink_grad, mid_grad, attended_grad, expand_bias, sums = feed_back(
            grad, active, slope, second_in, middle, attended, square, shrink, own_mod
        )
        dq, low_grad, own_grad, high_grad = attend_back(
            bounds, queries, attended_grad, attended, lse, low, own, high, ids_query_row,
            ids_key_column, cosine, sine,
        )
        square_grad, grad, input_bias, more = project_back(
            dq, low_grad, own_grad, high_grad, first_in, halo, before, mid_grad, square, own_mod,
            square_grad, 3 * LAYERS + layer,
        )
        bias_grads[layer] = jnp.concatenate([input_bias[0], sums[2], expand_bias[0], sums[3]])
        rows_grads[layer] = jnp.concatenate([more[0], more[1], sums[0], sums[1]])
        if not direct():
            reduced[layer] = plain_reduce(square_grad, shrink_grad)
        elif layer > 0:
            later_square = square_grad
            shrink_sum = lax.psum_scatter(shrink_grad, BOTH, scatter_dimension=0, tiled=True)
        else:
            small = reduce_small_inputs(jnp.stack(bias_grads), jnp.stack(rows_grads), lead_hot)
            summed = scatter_layers((square_grad, shrink_grad, small, later_square), LAYERS)
            reduced = [
                [summed[n] for n in range(4)],
                [summed[n] for n in (5, 6, 7)] + [shrink_sum.astype(F32)],
            ]
            bias_grad, lead_grad = split_small(summed[4])
    if not direct():
        bias_grad = lax.psum_scatter(
            jnp.stack(bias_grads).reshape(LAYERS, 9, D), BOTH, scatter_dimension=2, tiled=True
        )
        lead_grad = lax.psum_scatter(
            jnp.stack(rows_grads)[:, None, :] * lead_hot[None, :, None], BOTH, scatter_dimension=2,
            tiled=True,
        )
    moments = (input_moment, output_moment, expand_moment, shrink_moment, bias_moment, lead_moment)
    squares = (input_square, output_square, expand_square, shrink_square, bias_square, lead_square)
    results = []
    for number in range(6):
        if number < 4:
            gradient = jnp.stack([reduced[layer][number] for layer in range(LAYERS)])
        else:
            gradient = (bias_grad, lead_grad)[number - 4]
        results.append(
            adam_update(
                masters[number],
                gradient,
                moments[number],
                squares[number],
                RATE_MATRIX if number < 4 else RATE_VECTOR,
                DECAY if number < 4 else 0.0,
            )
        )
    return (stream, grad, *(array for four in results for array in four))


def solution(mesh):
    rows = P(("dp", "fsdp"), None)
    matrix = P(None, ("dp", "fsdp"), None)
    vector = P(None, None, ("dp", "fsdp"))
    return jax.shard_map(
        shards,
        mesh=mesh,
        in_specs=(rows,) * 2 + (P("dp"),) * 4 + (matrix,) * 12 + (vector,) * 6,
        out_specs=(rows,) * 2 + (matrix,) * 16 + (vector,) * 8,
        check_vma=False,
    )
```

```python
import functools
import math

import jax
import jax.numpy as jnp
from jax import lax
from jax.experimental import pallas as pl
from jax.experimental.pallas import tpu as pltpu
from jax.sharding import PartitionSpec as P

D = 768
FF = 3072
HEADS = 12
HEAD_DIM = 64
LEADS = 20
LAYERS = 2
WIN_MAX = 512
STEP = 10

EPSILON = 1e-06
NEGATIVE = -1e30
BETA_ONE = 0.5
BETA_TWO = 0.5
RATE_MATRIX = 0.08
RATE_VECTOR = 0.3
DECAY = 0.1
ADAM_EPSILON = 1e-08

MESH = pl.DeviceIdType.MESH
NZ, NY, NX = 4, 2, 2
CHIPS = NZ * NY * NX
SMALL = 256
GATHERED = (
    (4, "small", 0, 48, 0, 48, 0, 128, "zxy"),
    (0, "square", 0, 48, 0, 48, 0, 1152, "xzy"),
    (1, "square", 2304, 48, 0, 48, 0, 384, "yzx"),
    (2, "square", 3072, 48, 0, 48, 0, 768, "yzx"),
    (2, "square", 3072, 48, 0, 48, 768, 768, "zxy"),
    (3, "shrink", 0, 192, 0, 48, 0, 384, "zxy"),
    (3, "shrink", 0, 192, 48, 144, 0, 384, "zyx"),
)
SCATTERED = (
    (5, "later_in", 0, 48, 0, 48, 0, 384, "xzy"),
    (5, "later_in", 0, 48, 0, 48, 384, 384, "yzx"),
    (5, "later_in", 0, 48, 0, 48, 768, 384, "zxy"),
    (6, "later_out", 0, 48, 0, 48, 0, 384, "zyx"),
    (7, "later_expand", 0, 48, 0, 48, 0, 384, "xzy"),
    (7, "later_expand", 0, 48, 0, 48, 384, 384, "yzx"),
    (7, "later_expand", 0, 48, 0, 48, 768, 384, "zxy"),
    (7, "later_expand", 0, 48, 0, 48, 1152, 384, "zyx"),
    (2, "expand", 0, 48, 0, 48, 0, 768, "xzy"),
    (2, "expand", 0, 48, 0, 48, 768, 768, "yzx"),
    (3, "shrink", 0, 192, 0, 96, 0, 384, "zxy"),
    (3, "shrink", 0, 192, 96, 96, 0, 384, "zyx"),
    (0, "in", 0, 48, 0, 48, 0, 384, "xzy"),
    (0, "in", 0, 48, 0, 48, 384, 384, "yzx"),
    (0, "in", 0, 48, 0, 48, 768, 384, "zxy"),
    (1, "out", 0, 48, 0, 48, 0, 384, "zyx"),
    (4, "small", 0, 48, 0, 48, 0, 128, "zyx"),
)
LAG = (0.0,) * 4 + (0.5,) * 4 + (1.0,) * 2 + (1.5,) * 2 + (2.0,) * 5
WIDTHS = (2304, 768, 3072, 768, SMALL, 2304, 768, 3072)
OWN_ROWS = (24, 24, 24, 96, 24, 24, 24, 24)
WHOLES = {"square": (768, 6144), "shrink": (3072, 768), "small": (768, SMALL)}
AXIS = {"z": 0, "y": 1, "x": 2}


def place():
    dp, fs = lax.axis_index("dp"), lax.axis_index("fsdp")
    return lax.div(dp, NY), lax.rem(dp, NY), lax.div(fs, 2), lax.rem(fs, 2)


def device(z, y, x, core):
    return (z * NY + y, x * 2 + core)


def offsets():
    found = [
        (dz, dy, dx)
        for dz in range(1 - NZ, NZ)
        for dy in range(NY)
        for dx in range(NX)
    ]
    return sorted(found, key=lambda d: (abs(d[0]) + d[1] + d[2], abs(d[0])))


def last_axis(order, away):
    last = -1
    for number, axis in enumerate(order):
        if away[AXIS[axis]] != 0:
            last = number
    return last


def children(order, away):
    last = last_axis(order, away)
    found = []
    for number, axis in enumerate(order):
        if number < last:
            continue
        if axis == "z":
            if number > last:
                found += ["up", "down"]
            else:
                found += ["up"] if away[0] < 0 else ["down"]
        elif number > last:
            found.append(axis)
    return found


def exists(side, z):
    return {"up": z < NZ - 1, "down": z > 0}.get(side)


def neighbour(side, spot):
    z, y, x, core = spot
    return {
        "up": device(z + 1, y, x, core),
        "down": device(z - 1, y, x, core),
        "y": device(z, 1 - y, x, core),
        "x": device(z, y, 1 - x, core),
        "core": device(z, y, x, 1 - core),
    }[side]


def guarded(condition, action):
    if condition is None:
        action()
    else:
        pl.when(condition)(action)


def both(first, second):
    if first is None:
        return second
    if second is None:
        return first
    return first & second


def greet(spot):
    barrier = pltpu.get_barrier_semaphore()
    z, y, x, core = spot
    sides = [(neighbour(side, spot), exists(side, z)) for side in ("up", "down", "x", "y", "core")]
    count = 3
    for target, there in sides:

        def hello(target=target):
            pl.semaphore_signal(barrier, inc=1, device_id=target, device_id_type=MESH)

        guarded(there, hello)
        if there is not None:
            count = count + jnp.where(there, 1, 0)
    pl.semaphore_wait(barrier, count)


def source_of(spot, away):
    z, y, x, _ = spot
    sz = z + away[0]
    sy = 1 - y if away[1] else y
    sx = 1 - x if away[2] else x
    valid = None
    if away[0] > 0:
        valid = sz < NZ
    elif away[0] < 0:
        valid = sz >= 0
    return sz, sy, sx, valid


def chip_number(sz, sy, sx):
    return (sz * NY + sy) * NX + sx


def aligned(value, by):
    return value if isinstance(value, int) else pl.multiple_of(value, by)


def piece_view(ref, piece, chip, core):
    number, _, base, chip_rows, low, rows, column, columns, _ = piece
    half = WIDTHS[number] // 2
    return ref.at[
        pl.ds(aligned(chip * chip_rows + low, 16), rows),
        pl.ds(aligned(base + core * half + column, 128), columns),
    ]


class Job:
    def __init__(self, pieces):
        self.pieces = pieces
        self.numbers = tuple(dict.fromkeys(p[0] for p in pieces))
        self.arrays = tuple(dict.fromkeys(p[1] for p in pieces))

    def scratch_of(self, rows, dtype):
        return [pltpu.VMEM((rows * OWN_ROWS[n], WIDTHS[n] // 2), dtype) for n in self.numbers]


class GatherJob(Job):
    def __init__(self, pieces, layer):
        super().__init__(pieces)
        self.layer = layer
        self.inputs = len(self.numbers)
        self.outputs = tuple(jax.ShapeDtypeStruct(WHOLES[a], jnp.bfloat16) for a in self.arrays)
        count = len(pieces)
        self.scratch = (
            self.scratch_of(1, jnp.float32)
            + self.scratch_of(1, jnp.float32)
            + self.scratch_of(2, jnp.bfloat16)
            + [
                pltpu.SemaphoreType.DMA((8,)),
                pltpu.SemaphoreType.DMA((8,)),
                pltpu.SemaphoreType.DMA((8,)),
                pltpu.SemaphoreType.DMA((count,)),
                pltpu.SemaphoreType.DMA((count, 4)),
                pltpu.SemaphoreType.DMA((count, CHIPS)),
                pltpu.SemaphoreType.DMA((count,)),
                pltpu.SemaphoreType.DMA((count,)),
            ]
        )

    def bind(self, inputs, outputs, scratch):
        pieces, numbers, layer = self.pieces, self.numbers, self.layer
        many = len(numbers)
        take = iter(scratch)
        named = lambda: dict(zip(numbers, [next(take) for _ in range(many)]))
        masters = dict(zip(numbers, inputs))
        wholes = dict(zip(self.arrays, outputs))
        mine, theirs, blocks = named(), named(), named()
        local_sem, pair_send, pair_recv, store_sem, send_sem, recv_sem, core_send, core_recv = take
        spot = place()
        z, y, x, core = spot
        me = chip_number(z, y, x)
        partner = neighbour("core", spot)

        def columns_of(number, side):
            half = WIDTHS[number] // 2
            which = 0 if number == 4 else layer
            return masters[number].at[which, :, pl.ds(aligned(side * half, 128), half)]

        def load(number):
            return pltpu.make_async_copy(columns_of(number, core), mine[number], local_sem.at[number])

        def swap(number):
            return pltpu.make_async_remote_copy(
                src_ref=columns_of(number, 1 - core),
                dst_ref=theirs[number],
                send_sem=pair_send.at[number],
                recv_sem=pair_recv.at[number],
                device_id=partner,
                device_id_type=MESH,
            )

        def relay(index, away, source, view):
            piece = pieces[index]
            for side in children(piece[8], away):

                def send(side=side):
                    pltpu.make_async_remote_copy(
                        src_ref=view,
                        dst_ref=piece_view(wholes[piece[1]], piece, source, core),
                        send_sem=send_sem.at[index, ("up", "down", "x", "y").index(side)],
                        recv_sem=recv_sem.at[index, source],
                        device_id=neighbour(side, spot),
                        device_id_type=MESH,
                    ).start()

                guarded(exists(side, z), send)
            pltpu.make_async_remote_copy(
                src_ref=view,
                dst_ref=piece_view(wholes[piece[1]], piece, source, core),
                send_sem=core_send.at[index],
                recv_sem=core_recv.at[index],
                device_id=partner,
                device_id_type=MESH,
            ).start()

        def own_view(index):
            piece = pieces[index]
            return blocks[piece[0]].at[pl.ds(piece[4], piece[5]), pl.ds(piece[6], piece[7])]

        def store(index):
            piece = pieces[index]
            return pltpu.make_async_copy(
                own_view(index), piece_view(wholes[piece[1]], piece, me, core), store_sem.at[index]
            )

        def start():
            for number in numbers:
                load(number).start()
            for number in numbers:
                swap(number).start()

        def own(number):
            load(number).wait()
            swap(number).wait_recv()
            own_rows, other_rows = mine[number][...], theirs[number][...]
            is_first = core == 0
            block = jnp.concatenate(
                [jnp.where(is_first, own_rows, other_rows), jnp.where(is_first, other_rows, own_rows)],
                axis=0,
            )
            blocks[number][...] = block.astype(jnp.bfloat16)
            for index, piece in enumerate(pieces):
                if piece[0] == number:
                    store(index).start()
                    relay(index, (0, 0, 0), me, own_view(index))

        def event(away, index):
            piece = pieces[index]
            sz, sy, sx, valid = source_of(spot, away)
            source = chip_number(sz, sy, sx)

            def arrival():
                view = piece_view(wholes[piece[1]], piece, source, core)
                pltpu.make_async_remote_copy(
                    src_ref=view,
                    dst_ref=view,
                    send_sem=send_sem.at[index, 0],
                    recv_sem=recv_sem.at[index, source],
                    device_id=partner,
                    device_id_type=MESH,
                ).wait_recv()
                relay(index, away, source, view)

            guarded(valid, arrival)

        def finish():
            for index in range(len(pieces)):
                store(index).wait()
            for number in numbers:
                swap(number).wait_send()
            for index, piece in enumerate(pieces):
                number, rows, columns = piece[0], piece[5], piece[7]

                def span(chunks, core_at, piece=piece, number=number, rows=rows, columns=columns):
                    half = WIDTHS[number] // 2
                    first = aligned(piece[2] + core_at * half + piece[6], 128)
                    return wholes[piece[1]].at[pl.ds(0, chunks * rows), pl.ds(first, columns)]

                def wait_send(chunks, sem, index=index, span=span):
                    pltpu.make_async_remote_copy(
                        src_ref=span(chunks, core),
                        dst_ref=span(chunks, core),
                        send_sem=sem,
                        recv_sem=recv_sem.at[index, 0],
                        device_id=partner,
                        device_id_type=MESH,
                    ).wait_send()

                before = 1
                for axis in piece[8]:
                    if axis == "z":
                        for at in range(NZ):

                            @pl.when(z == at)
                            def _(at=at, before=before, index=index, wait_send=wait_send):
                                if at < NZ - 1:
                                    wait_send(before * (at + 1), send_sem.at[index, 0])
                                if at > 0:
                                    wait_send(before * (NZ - at), send_sem.at[index, 1])

                        before *= NZ
                    else:
                        wait_send(before, send_sem.at[index, 2 if axis == "x" else 3])
                        before *= 2
                wait_send(CHIPS, core_send.at[index])
                pltpu.make_async_remote_copy(
                    src_ref=span(CHIPS, 1 - core),
                    dst_ref=span(CHIPS, 1 - core),
                    send_sem=core_send.at[index],
                    recv_sem=core_recv.at[index],
                    device_id=partner,
                    device_id_type=MESH,
                ).wait_recv()

        actions = [start] + [functools.partial(own, number) for number in numbers]
        for away in offsets():
            if away != (0, 0, 0):
                actions += [functools.partial(event, away, index) for index in range(len(pieces))]
        return actions + [finish]


def slot_of(order, side, source):
    sizes = {"z": NZ, "y": NY, "x": NX}
    base = 0
    ahead = 1
    number = 0
    for axis in order:
        at = source[AXIS[axis]]
        for here in ["up", "down"] if axis == "z" else [axis]:
            if axis == "z":
                if here == side:
                    return base + number * NZ + at
                base += ahead * NZ
            else:
                if here == side:
                    return base + number
                base += ahead
        number = number * sizes[axis] + at
        ahead *= sizes[axis]
    return base


def slot_count(order):
    return slot_of(order, None, (0, 0, 0))


class ScatterJob(Job):
    def __init__(self, pieces):
        super().__init__(pieces)
        self.inputs = len(self.arrays)
        self.first = {}
        width = 0
        for number in self.numbers:
            if number != 3:
                self.first[number] = width
                width += WIDTHS[number]
        self.first[3] = 0
        self.outputs = (
            jax.ShapeDtypeStruct((OWN_ROWS[0], width), jnp.float32),
            jax.ShapeDtypeStruct((OWN_ROWS[3], WIDTHS[3]), jnp.float32),
        )
        count = len(pieces)
        most = max(slot_count(p[8]) for p in pieces)
        self.scratch = (
            self.scratch_of(32, jnp.bfloat16)
            + self.scratch_of(32, jnp.bfloat16)
            + self.scratch_of(2, jnp.float32)
            + self.scratch_of(1, jnp.float32)
            + [pltpu.VMEM((slot_count(p[8]), p[5], p[7]), jnp.bfloat16) for p in pieces]
            + [
                pltpu.SemaphoreType.DMA((8,)),
                pltpu.SemaphoreType.DMA((8,)),
                pltpu.SemaphoreType.DMA((8,)),
                pltpu.SemaphoreType.DMA((count, CHIPS)),
                pltpu.SemaphoreType.DMA((count, most)),
                pltpu.SemaphoreType.DMA((8,)),
                pltpu.SemaphoreType.DMA((8,)),
                pltpu.SemaphoreType.DMA((16,)),
            ]
        )

    def bind(self, inputs, outputs, scratch):
        pieces, numbers = self.pieces, self.numbers
        many = len(numbers)
        take = iter(scratch)
        named = lambda: dict(zip(numbers, [next(take) for _ in range(many)]))
        partials = dict(zip(self.arrays, inputs))
        outs = {n: outputs[1 if n == 3 else 0] for n in numbers}
        starts = self.first
        own, pair, total, handed = named(), named(), named(), named()
        slots = [next(take) for _ in pieces]
        own_sem, pair_send, pair_recv, send_sem, recv_sem, end_send, end_recv, out_sem = take
        base = {p[0]: p[2] for p in pieces}
        array = {p[0]: p[1] for p in pieces}
        spot = place()
        z, y, x, core = spot
        partner = neighbour("core", spot)

        def columns_of(number, side):
            half = WIDTHS[number] // 2
            first = aligned(base[number] + side * half, 128)
            return partials[array[number]].at[:, pl.ds(first, half)]

        def load(number):
            return pltpu.make_async_copy(columns_of(number, core), own[number], own_sem.at[number])

        def swap(number):
            return pltpu.make_async_remote_copy(
                src_ref=columns_of(number, 1 - core),
                dst_ref=pair[number],
                send_sem=pair_send.at[number],
                recv_sem=pair_recv.at[number],
                device_id=partner,
                device_id_type=MESH,
            )

        def start():
            for number in numbers:
                load(number).start()
                swap(number).start()

        def ready(number):
            load(number).wait()
            swap(number).wait_recv()

        def view_of(piece, source):
            _, _, _, chip_rows, low, rows, column, columns, _ = piece
            return pl.ds(aligned(source * chip_rows + low, 16), rows), pl.ds(column, columns)

        def event(away, index):
            piece = pieces[index]
            number, _, _, chip_rows, low, rows, column, columns, order = piece
            sz, sy, sx, valid = source_of(spot, away)
            where = (sz, sy, sx)
            source = chip_number(sz, sy, sx)
            last = last_axis(order, away)

            def act():
                kids = children(order, away)
                for side in kids:

                    def arrived(side=side):
                        slot = slot_of(order, side, where)
                        pltpu.make_async_remote_copy(
                            src_ref=slots[index].at[slot],
                            dst_ref=slots[index].at[slot],
                            send_sem=send_sem.at[index, 0],
                            recv_sem=recv_sem.at[index, slot],
                            device_id=partner,
                            device_id_type=MESH,
                        ).wait_recv()

                    guarded(exists(side, z), arrived)
                view = view_of(piece, source)
                value = own[number][view].astype(jnp.float32) + pair[number][view].astype(jnp.float32)
                for side in kids:
                    landed = slots[index][slot_of(order, side, where)].astype(jnp.float32)
                    there = exists(side, z)
                    value = value + (landed if there is None else jnp.where(there, landed, 0.0))
                if last < 0:
                    total[number][pl.ds(low, rows), pl.ds(column, columns)] = value
                    return
                pair[number][view] = value.astype(jnp.bfloat16)
                axis = order[last]
                if axis == "z":
                    side = "up" if away[0] < 0 else "down"
                    parent = neighbour("down" if away[0] < 0 else "up", spot)
                else:
                    side = axis
                    parent = neighbour(axis, spot)
                slot = slot_of(order, side, where)
                pltpu.make_async_remote_copy(
                    src_ref=pair[number].at[view],
                    dst_ref=slots[index].at[slot],
                    send_sem=send_sem.at[index, source],
                    recv_sem=recv_sem.at[index, slot],
                    device_id=parent,
                    device_id_type=MESH,
                ).start()

            guarded(valid, act)

        def end(number):
            rows = OWN_ROWS[number]
            return pltpu.make_async_remote_copy(
                src_ref=total[number].at[pl.ds(aligned((1 - core) * rows, 8), rows)],
                dst_ref=handed[number],
                send_sem=end_send.at[number],
                recv_sem=end_recv.at[number],
                device_id=partner,
                device_id_type=MESH,
            )

        def write(number, other):
            half = WIDTHS[number] // 2
            rows = OWN_ROWS[number]
            source = handed[number] if other else total[number].at[pl.ds(aligned(core * rows, 8), rows)]
            side = 1 - core if other else core
            return pltpu.make_async_copy(
                source,
                outs[number].at[:, pl.ds(aligned(starts[number] + side * half, 128), half)],
                out_sem.at[number + 8 * other],
            )

        def finish():
            for number in numbers:
                end(number).start()
            for number in numbers:
                write(number, 0).start()
            for number in numbers:
                end(number).wait_recv()
                write(number, 1).start()
            for number in numbers:
                write(number, 0).wait()
                write(number, 1).wait()
                end(number).wait_send()
                swap(number).wait_send()
            for index, piece in enumerate(pieces):
                for away in offsets():
                    if away == (0, 0, 0):
                        continue
                    sz, sy, sx, valid = source_of(spot, away)
                    source = chip_number(sz, sy, sx)

                    def sent(index=index, piece=piece, source=source):
                        pltpu.make_async_remote_copy(
                            src_ref=pair[piece[0]].at[view_of(piece, source)],
                            dst_ref=slots[index].at[0],
                            send_sem=send_sem.at[index, source],
                            recv_sem=recv_sem.at[index, 0],
                            device_id=partner,
                            device_id_type=MESH,
                        ).wait_send()

                    guarded(valid, sent)

        actions = [start]
        known = set()
        level = lambda away: NZ + 1 - (abs(away[0]) + away[1] + away[2])
        events = [
            (level(away) + LAG[index], index, place_at, away)
            for place_at, away in enumerate(reversed(offsets()))
            for index in range(len(pieces))
        ]
        for _, index, _, away in sorted(events):
            number = pieces[index][0]
            if number not in known:
                known.add(number)
                actions.append(functools.partial(ready, number))
            actions.append(functools.partial(event, away, index))
        return actions + [finish]


def alone(job, arrays, name, ident):
    anywhere = pl.BlockSpec(memory_space=pl.ANY)

    def kernel(*refs):
        first, second = job.inputs, job.inputs + len(job.outputs)
        greet(place())
        for action in job.bind(refs[:first], refs[first:second], refs[second:]):
            action()

    return pl.pallas_call(
        kernel,
        out_shape=job.outputs,
        in_specs=[anywhere] * job.inputs,
        out_specs=tuple([anywhere] * len(job.outputs)),
        scratch_shapes=job.scratch,
        name=name,
        compiler_params=pltpu.CompilerParams(
            collective_id=ident, has_side_effects=True, vmem_limit_bytes=60 << 20
        ),
        cost_estimate=pl.CostEstimate(flops=0, bytes_accessed=int(2e8), transcendentals=0),
    )(*arrays)


def normalize(values):
    centred = values - jnp.mean(values, axis=-1, keepdims=True)
    inverse = lax.rsqrt(jnp.mean(centred * centred, axis=-1, keepdims=True) + EPSILON)
    return (centred * inverse, inverse)


def normalize_back(grad_normed, normed, inverse):
    return inverse * (
        grad_normed
        - jnp.mean(grad_normed, axis=-1, keepdims=True)
        - normed * jnp.mean(grad_normed * normed, axis=-1, keepdims=True)
    )


def rotary_tables(relative):
    lane = jnp.arange(2 * HEAD_DIM, dtype=jnp.int32)
    indices = (lane % (HEAD_DIM // 2)).astype(jnp.float32)
    frequency = jnp.exp(indices * (-2.0 * math.log(10000.0) / HEAD_DIM))
    phase = relative.astype(jnp.float32)[:, None] * frequency[None, :]
    sign = jnp.where(lane % HEAD_DIM < HEAD_DIM // 2, -1.0, 1.0)
    return jnp.cos(phase), jnp.sin(phase) * sign[None, :]


BAND = 128
VARIANTS = (3, 4, 5, 6, 7, 9)
STEP_COLUMNS = 384
BLOCK = 512
F32 = jnp.float32
BF16 = jnp.bfloat16
MATMUL = (((1,), (0,)), ((), ()))
MATMUL_RIGHT = (((1,), (1,)), ((), ()))
MATMUL_LEFT = (((0,), (0,)), ((), ()))


def product(left, right, dims=MATMUL):
    return lax.dot_general(left, right, dims, preferred_element_type=F32)


def vmem(limit=56):
    return pltpu.CompilerParams(vmem_limit_bytes=limit << 20)


def cost(flops, moved):
    return pl.CostEstimate(flops=int(flops), bytes_accessed=int(moved), transcendentals=0)


def swap_halves(values):
    lane = lax.broadcasted_iota(jnp.int32, values.shape, 1)
    low = lax.rem(lane, HEAD_DIM) < HEAD_DIM // 2
    return jnp.where(
        low,
        pltpu.roll(values, 2 * HEAD_DIM - HEAD_DIM // 2, 1),
        pltpu.roll(values, HEAD_DIM // 2, 1),
    )


def turn(values, cosine, sine):
    parts = []
    for at in range(0, values.shape[1], 128):
        part = values[:, at : at + 128]
        parts.append(part * cosine + swap_halves(part) * sine)
    return jnp.concatenate(parts, axis=1)


def beside():
    dp, fs = lax.axis_index("dp"), lax.axis_index("fsdp")
    return ((dp, fs - 1), fs > 0), ((dp, fs + 1), fs < lax.axis_size("fsdp") - 1)


def greet_beside():
    barrier = pltpu.get_barrier_semaphore()
    count = 0
    for device_at, there in beside():

        @pl.when(there)
        def _(device_at=device_at):
            pl.semaphore_signal(barrier, inc=1, device_id=device_at, device_id_type=MESH)

        count = count + jnp.where(there, 1, 0)
    pl.semaphore_wait(barrier, count)


def halo_copies(sources, landing, send_sem, recv_sem):
    return [
        (
            there,
            pltpu.make_async_remote_copy(
                src_ref=sources[side],
                dst_ref=landing.at[1 - side],
                send_sem=send_sem.at[side],
                recv_sem=recv_sem.at[1 - side],
                device_id=device_at,
                device_id_type=MESH,
            ),
        )
        for side, (device_at, there) in enumerate(beside())
    ]


def halo_start(sources, landing, send_sem, recv_sem):
    for there, copy in halo_copies(sources, landing, send_sem, recv_sem):
        pl.when(there)(copy.start)


def halo_wait(sources, landing, send_sem, recv_sem):
    sides = beside()
    for side, (there, copy) in enumerate(halo_copies(sources, landing, send_sem, recv_sem)):
        pl.when(there)(copy.wait_send)
        device_at, _ = sides[side]

        @pl.when(there)
        def _(side=side, device_at=device_at):
            pltpu.make_async_remote_copy(
                src_ref=sources[side],
                dst_ref=landing.at[side],
                send_sem=send_sem.at[side],
                recv_sem=recv_sem.at[side],
                device_id=device_at,
                device_id_type=MESH,
            ).wait_recv()

        @pl.when(jnp.logical_not(there))
        def _(side=side):
            landing[side] = jnp.zeros(landing.shape[1:], landing.dtype)


def project_kernel(
    x_ref, w_ref, bias_ref, mod_ref, cos_ref, sin_ref, q_ref, own_ref, low_ref, high_ref, h_ref, halo_ref,
    mine, landing, send_sem, recv_sem,
):
    step = pl.program_id(0)
    rows = x_ref.shape[0]

    @pl.when(step == 0)
    def _():
        normed, _ = normalize(x_ref[...].astype(F32))
        hidden_in = (normed * (1.0 + mod_ref[0, 1:2]) + mod_ref[0, 0:1]).astype(BF16)
        mine[...] = hidden_in
        h_ref[...] = hidden_in
        greet_beside()
        halo_start((mine, mine), landing, send_sem, recv_sem)

    def own_turned(y):
        return turn(y, cos_ref[WIN_MAX : WIN_MAX + rows], sin_ref[WIN_MAX : WIN_MAX + rows]).astype(BF16)

    @pl.when(step < 6)
    def _():
        y = product(mine[...], w_ref[...]) + bias_ref[0]

        @pl.when(step < 2)
        def _():
            q_ref[...] = own_turned(y)

        @pl.when((step >= 2) & (step < 4))
        def _():
            own_ref[0] = own_turned(y)

        @pl.when(step >= 4)
        def _():
            own_ref[0] = y.astype(BF16)

    @pl.when(step == 6)
    def _():
        halo_wait((mine, mine), landing, send_sem, recv_sem)
        halo_ref[...] = landing[...]

    @pl.when(step >= 6)
    def _():
        for side, out_ref, first in ((0, low_ref, 0), (1, high_ref, WIN_MAX + rows)):
            y = product(landing[side], w_ref[...]) + bias_ref[0]

            @pl.when(step < 8)
            def _(y=y, out_ref=out_ref, first=first):
                table = slice(first, first + WIN_MAX)
                out_ref[0] = turn(y, cos_ref[table], sin_ref[table]).astype(BF16)

            @pl.when(step >= 8)
            def _(y=y, out_ref=out_ref):
                out_ref[0] = y.astype(BF16)


def project(layer, stream, square, bias, modulation, cosine, sine, ident):
    rows = stream.shape[0]
    whole = lambda shape: pl.BlockSpec(shape, lambda c: (0,) * len(shape))

    def halves(first):
        def index(c):
            at = jnp.clip(c - first, 0, 3)
            return (at // 2, 0, at % 2)

        return pl.BlockSpec((1, rows, STEP_COLUMNS), index)

    column = lambda c: (0, jnp.where(c < 6, c, c - 4))
    pair = jax.ShapeDtypeStruct((2, rows, D), BF16)
    single = jax.ShapeDtypeStruct((rows, D), BF16)
    return pl.pallas_call(
        project_kernel,
        grid=(10,),
        in_specs=[
            whole((rows, D)),
            pl.BlockSpec((D, STEP_COLUMNS), column),
            pl.BlockSpec((1, 1, STEP_COLUMNS), lambda c: (layer, *column(c))),
            pl.BlockSpec((1, 4, D), lambda c: (layer, 0, 0)),
            whole((rows + 2 * WIN_MAX, 128)),
            whole((rows + 2 * WIN_MAX, 128)),
        ],
        out_specs=(
            pl.BlockSpec((rows, STEP_COLUMNS), lambda c: (0, jnp.minimum(c, 1))),
            halves(2),
            halves(6),
            halves(6),
            whole((rows, D)),
            whole((2, rows, D)),
        ),
        out_shape=(single, pair, pair, pair, single, pair),
        scratch_shapes=[
            pltpu.VMEM((rows, D), BF16),
            pltpu.VMEM((2, rows, D), BF16),
            pltpu.SemaphoreType.DMA((2,)),
            pltpu.SemaphoreType.DMA((2,)),
        ],
        compiler_params=pltpu.CompilerParams(
            vmem_limit_bytes=56 << 20, collective_id=ident, has_side_effects=True
        ),
        cost_estimate=cost(2 * rows * D * 7 * D, 8e6),
        name="project",
    )(stream, square, bias, modulation, cosine, sine)


def stack_heads(pair):
    lane = lax.broadcasted_iota(jnp.int32, pair.shape, 1)
    zero = jnp.zeros_like(pair)
    return jnp.concatenate(
        [jnp.where(lane < HEAD_DIM, pair, zero), jnp.where(lane < HEAD_DIM, zero, pair)], axis=0
    )


def merge_heads(stacked):
    rows = stacked.shape[0] // 2
    lane = lax.broadcasted_iota(jnp.int32, (rows, stacked.shape[1]), 1)
    return jnp.where(lane < HEAD_DIM, stacked[:rows], stacked[rows:])


def over_bands(bounds_ref, count, action):
    def one(number, carry):
        low, need = bounds_ref[0, number], bounds_ref[1, number]
        before = 0
        for size in VARIANTS:

            @pl.when((need > before) & (need <= size))
            def _(size=size):
                start = jnp.minimum(low, count - size) * BAND
                action(pl.multiple_of(number * BAND, BAND), pl.multiple_of(start, BAND), size * BAND)

            before = size
        return carry

    lax.fori_loop(0, bounds_ref.shape[1], one, 0)


PAIRS = 2
LANES = 128 * PAIRS


def load_band(ext, low_ref, own_ref, high_ref):
    rows = own_ref.shape[1]
    for at in range(2):
        ext[at, :WIN_MAX] = low_ref[at]
        ext[at, WIN_MAX : WIN_MAX + rows] = own_ref[at]
        ext[at, WIN_MAX + rows :] = high_ref[at]


def attend_kernel(bounds_ref, q_ref, low_ref, own_ref, high_ref, idq_ref, idk_ref, o_ref, lse_ref, ext):
    rows = own_ref.shape[1]
    load_band(ext, low_ref, own_ref, high_ref)

    def block(first, start, size):
        mine = pl.ds(first, BAND)
        band = pl.ds(start, size)
        ids = idq_ref[mine, :]
        allowed = jnp.concatenate([ids] * (size // BAND), axis=1) == idk_ref[0:1, band]
        allowed = jnp.concatenate([allowed, allowed], axis=0)
        pairs = range(PAIRS)
        lanes = [slice(128 * p, 128 * p + 128) for p in pairs]
        queries = [stack_heads(q_ref[mine, lanes[p]]) * jnp.asarray(HEAD_DIM**-0.5, BF16) for p in pairs]
        scores = [product(queries[p], ext[0, band, lanes[p]], MATMUL_RIGHT) for p in pairs]
        scores = [jnp.where(allowed, scores[p], NEGATIVE) for p in pairs]
        peaks = [jnp.max(scores[p], axis=1, keepdims=True) for p in pairs]
        weights = [jnp.exp(scores[p] - peaks[p]) for p in pairs]
        totals = [jnp.sum(weights[p], axis=1, keepdims=True) for p in pairs]
        mixed = [product(weights[p].astype(BF16), ext[1, band, lanes[p]]) for p in pairs]
        for p in pairs:
            o_ref[mine, lanes[p]] = merge_heads(mixed[p] * (1.0 / totals[p])).astype(BF16)
            wide = jnp.broadcast_to(peaks[p] + jnp.log(totals[p]), (2 * BAND, BAND))
            lse_ref[p, 0:1, mine] = wide[:BAND].T[0:1]
            lse_ref[p, 1:2, mine] = wide[BAND:].T[0:1]

    over_bands(bounds_ref, (rows + 2 * WIN_MAX) // BAND, block)


def pair_spec(rows):
    return pl.BlockSpec((2, rows, LANES), lambda j, b: (0, 0, j))


def attend(bounds, queries, low, own, high, ids_query, ids_key):
    rows = queries.shape[0]
    wide = rows + 2 * WIN_MAX
    column = pl.BlockSpec((rows, LANES), lambda j, b: (0, j))
    return pl.pallas_call(
        attend_kernel,
        grid_spec=pltpu.PrefetchScalarGridSpec(
            num_scalar_prefetch=1,
            grid=(D // LANES,),
            in_specs=[
                column,
                pair_spec(WIN_MAX),
                pair_spec(rows),
                pair_spec(WIN_MAX),
                pl.BlockSpec((rows, 128), lambda j, b: (0, 0)),
                pl.BlockSpec((8, wide), lambda j, b: (0, 0)),
            ],
            out_specs=(column, pl.BlockSpec((PAIRS, 8, rows), lambda j, b: (j, 0, 0))),
            scratch_shapes=[pltpu.VMEM((2, wide, LANES), BF16)],
        ),
        out_shape=(
            jax.ShapeDtypeStruct((rows, D), BF16),
            jax.ShapeDtypeStruct((HEADS // 2, 8, rows), F32),
        ),
        compiler_params=vmem(),
        cost_estimate=cost(5e9, 8e6),
        name="attend",
    )(bounds, queries, low, own, high, ids_query, ids_key)


def attend_back_kernel(
    bounds_ref, q_ref, g_ref, o_ref, lse_ref, low_ref, own_ref, high_ref, idq_ref, idk_ref,
    cos_ref, sin_ref, dq_ref, dlow_ref, down_ref, dhigh_ref, ext, dext,
):
    rows = own_ref.shape[1]
    load_band(ext, low_ref, own_ref, high_ref)
    dext[...] = jnp.zeros_like(dext)

    def delta_of(mine, lanes):
        both_heads = (g_ref[mine, lanes].astype(F32) * o_ref[mine, lanes].astype(F32)).T
        return jnp.concatenate(
            [
                jnp.sum(both_heads[:HEAD_DIM], axis=0, keepdims=True),
                jnp.sum(both_heads[HEAD_DIM:], axis=0, keepdims=True),
            ],
            axis=1,
        )

    def block(first, start, size):
        mine = pl.ds(first, BAND)
        band = pl.ds(start, size)
        ids = idk_ref[band, :] == idq_ref[0:1, mine]
        allowed = jnp.concatenate([ids, ids], axis=1)
        pairs = range(PAIRS)
        lanes = [slice(128 * p, 128 * p + 128) for p in pairs]
        queries = [stack_heads(q_ref[mine, lanes[p]]) * jnp.asarray(HEAD_DIM**-0.5, BF16) for p in pairs]
        grads = [stack_heads(g_ref[mine, lanes[p]]) for p in pairs]
        keys = [ext[0, band, lanes[p]] for p in pairs]
        scores = [product(keys[p], queries[p], MATMUL_RIGHT) for p in pairs]
        grad_weights = [product(ext[1, band, lanes[p]], grads[p], MATMUL_RIGHT) for p in pairs]
        lse = [
            jnp.concatenate([lse_ref[p, 0:1, mine], lse_ref[p, 1:2, mine]], axis=1) for p in pairs
        ]
        deltas = [delta_of(mine, lanes[p]) for p in pairs]
        weights = [jnp.where(allowed, jnp.exp(scores[p] - lse[p]), 0.0) for p in pairs]
        grad_scores = [(weights[p] * (grad_weights[p] - deltas[p])).astype(BF16) for p in pairs]
        table = pl.ds(pl.multiple_of(first + WIN_MAX, BAND), BAND)
        cosine, sine = cos_ref[table, :], -sin_ref[table, :]
        for p in pairs:
            dext[0, band, lanes[p]] += product(grad_scores[p], queries[p])
            dext[1, band, lanes[p]] += product(weights[p].astype(BF16), grads[p])
            turned = merge_heads(product(grad_scores[p], keys[p], MATMUL_LEFT)) * HEAD_DIM**-0.5
            dq_ref[mine, lanes[p]] = turn(turned, cosine, sine).astype(BF16)

    over_bands(bounds_ref, (rows + 2 * WIN_MAX) // BAND, block)
    for out_ref, part in (
        (dlow_ref, slice(0, WIN_MAX)),
        (down_ref, slice(WIN_MAX, WIN_MAX + rows)),
        (dhigh_ref, slice(WIN_MAX + rows, 2 * WIN_MAX + rows)),
    ):
        out_ref[0] = turn(dext[0, part], cos_ref[part], -sin_ref[part]).astype(BF16)
        out_ref[1] = dext[1, part].astype(BF16)


def attend_back(bounds, queries, grads, attended, lse, low, own, high, ids_query, ids_key, cosine, sine):
    rows = queries.shape[0]
    wide = rows + 2 * WIN_MAX
    column = pl.BlockSpec((rows, LANES), lambda j, b: (0, j))
    fixed = lambda shape: pl.BlockSpec(shape, lambda j, b: (0,) * len(shape))
    return pl.pallas_call(
        attend_back_kernel,
        grid_spec=pltpu.PrefetchScalarGridSpec(
            num_scalar_prefetch=1,
            grid=(D // LANES,),
            in_specs=[
                column,
                column,
                column,
                pl.BlockSpec((PAIRS, 8, rows), lambda j, b: (j, 0, 0)),
                pair_spec(WIN_MAX),
                pair_spec(rows),
                pair_spec(WIN_MAX),
                fixed((8, rows)),
                fixed((wide, 128)),
                fixed((wide, 128)),
                fixed((wide, 128)),
            ],
            out_specs=(column, pair_spec(WIN_MAX), pair_spec(rows), pair_spec(WIN_MAX)),
            scratch_shapes=[pltpu.VMEM((2, wide, LANES), BF16), pltpu.VMEM((2, wide, LANES), F32)],
        ),
        out_shape=(
            jax.ShapeDtypeStruct((rows, D), BF16),
            jax.ShapeDtypeStruct((2, WIN_MAX, D), BF16),
            jax.ShapeDtypeStruct((2, rows, D), BF16),
            jax.ShapeDtypeStruct((2, WIN_MAX, D), BF16),
        ),
        compiler_params=vmem(),
        cost_estimate=cost(12e9, 16e6),
        name="attend_back",
    )(bounds, queries, grads, attended, lse, low, own, high, ids_query, ids_key, cosine, sine)


def feed_kernel(
    o_ref, x_ref, wo_ref, we_ref, ws_ref, bo_ref, be_ref, bs_ref, mod_ref,
    mid_ref, h_ref, z_ref, slope_ref, out_ref,
):
    step = pl.program_id(0)

    @pl.when(step == 0)
    def _():
        middle = x_ref[...].astype(F32) + (product(o_ref[...], wo_ref[...]) + bo_ref[0])
        mid_ref[...] = middle
        normed, _ = normalize(middle)
        h_ref[...] = (normed * (1.0 + mod_ref[0, 3:4]) + mod_ref[0, 2:3]).astype(BF16)
        out_ref[...] = middle + bs_ref[0]

    u = product(h_ref[...], we_ref[...]) + be_ref[0]
    share = 0.5 + 0.5 * lax.erf(u * (0.5**0.5))
    active = (u * share).astype(BF16)
    z_ref[...] = active
    slope_ref[...] = (share + u * (jnp.exp(-0.5 * u * u) * (2.0 * math.pi) ** -0.5)).astype(BF16)
    out_ref[...] += product(active, ws_ref[...])


def feed(layer, attended, stream, square, shrink, bias, modulation):
    rows = stream.shape[0]
    whole = lambda shape: pl.BlockSpec(shape, lambda c: (0,) * len(shape))
    width = STEP_COLUMNS
    return pl.pallas_call(
        feed_kernel,
        grid=(FF // width,),
        in_specs=[
            whole((rows, D)),
            whole((rows, D)),
            pl.BlockSpec((D, D), lambda c: (0, 3)),
            pl.BlockSpec((D, width), lambda c: (0, 4 * D // width + c)),
            pl.BlockSpec((width, D), lambda c: (c, 0)),
            pl.BlockSpec((1, 1, D), lambda c: (layer, 0, 3)),
            pl.BlockSpec((1, 1, width), lambda c: (layer, 0, 4 * D // width + c)),
            pl.BlockSpec((1, 1, D), lambda c: (layer, 0, 8)),
            pl.BlockSpec((1, 4, D), lambda c: (layer, 0, 0)),
        ],
        out_specs=(
            whole((rows, D)),
            whole((rows, D)),
            pl.BlockSpec((rows, width), lambda c: (0, c)),
            pl.BlockSpec((rows, width), lambda c: (0, c)),
            whole((rows, D)),
        ),
        out_shape=(
            jax.ShapeDtypeStruct((rows, D), F32),
            jax.ShapeDtypeStruct((rows, D), BF16),
            jax.ShapeDtypeStruct((rows, FF), BF16),
            jax.ShapeDtypeStruct((rows, FF), BF16),
            jax.ShapeDtypeStruct((rows, D), F32),
        ),
        compiler_params=vmem(),
        cost_estimate=cost(2 * rows * D * (D + 2 * FF), 24e6),
        name="feed",
    )(attended, stream, square, square, shrink, bias, bias, bias, modulation)


def feed_back_kernel(
    g_ref, z_ref, slope_ref, h_ref, mid_ref, o_ref, we_ref, ws_ref, wo_ref, mod_ref,
    dexp_ref, dout_ref, dshr_ref, mid_grad_ref, do_ref, dbe_ref, sums_ref,
    low, turned, total,
):
    step = pl.program_id(0)
    chunks = FF // STEP_COLUMNS

    @pl.when(step == 0)
    def _():
        low[...] = g_ref[...].astype(BF16)
        turned[...] = h_ref[...].T
        total[...] = jnp.zeros_like(total)
        sums_ref[3:4] = jnp.sum(low[...].astype(F32), axis=0, keepdims=True)

    @pl.when(step < chunks)
    def _():
        grad_active = product(low[...], ws_ref[...], MATMUL_RIGHT)
        grad_hidden = (grad_active * slope_ref[...].astype(F32)).astype(BF16)
        dbe_ref[...] = jnp.sum(grad_hidden.astype(F32), axis=0, keepdims=True)
        dshr_ref[...] = product(z_ref[...], low[...], MATMUL_LEFT).astype(BF16)
        dexp_ref[...] = product(turned[...], grad_hidden).astype(BF16)
        total[...] += product(grad_hidden, we_ref[...], MATMUL_RIGHT)

    @pl.when(step == chunks)
    def _():
        normed, inverse = normalize(mid_ref[...])
        grad = total[...]
        sums_ref[0:1] = jnp.sum(grad, axis=0, keepdims=True)
        sums_ref[1:2] = jnp.sum(grad * normed, axis=0, keepdims=True)
        middle = g_ref[...].astype(F32) + normalize_back(grad * (1.0 + mod_ref[0, 3:4]), normed, inverse)
        mid_grad_ref[...] = middle
        low[...] = middle.astype(BF16)
        sums_ref[2:3] = jnp.sum(low[...].astype(F32), axis=0, keepdims=True)
        do_ref[...] = product(low[...], wo_ref[...], MATMUL_RIGHT).astype(BF16)
        turned[...] = o_ref[...].T
        dout_ref[...] = product(turned[...], low[:, :STEP_COLUMNS]).astype(BF16)

    @pl.when(step == chunks + 1)
    def _():
        dout_ref[...] = product(turned[...], low[:, STEP_COLUMNS:]).astype(BF16)


def feed_back(layer, grad, active, slope, hidden_in, middle, attended, square, shrink, modulation):
    rows = grad.shape[0]
    whole = lambda shape: pl.BlockSpec(shape, lambda c: (0,) * len(shape))
    width = STEP_COLUMNS
    chunks = FF // width
    upto = lambda c: jnp.minimum(c, chunks - 1)
    return pl.pallas_call(
        feed_back_kernel,
        grid=(chunks + 2,),
        in_specs=[
            whole((rows, D)),
            pl.BlockSpec((rows, width), lambda c: (0, upto(c))),
            pl.BlockSpec((rows, width), lambda c: (0, upto(c))),
            whole((rows, D)),
            whole((rows, D)),
            whole((rows, D)),
            pl.BlockSpec((D, width), lambda c: (0, 4 * D // width + upto(c))),
            pl.BlockSpec((width, D), lambda c: (upto(c), 0)),
            pl.BlockSpec((D, D), lambda c: (0, 3)),
            pl.BlockSpec((1, 4, D), lambda c: (layer, 0, 0)),
        ],
        out_specs=(
            pl.BlockSpec((D, width), lambda c: (0, upto(c))),
            pl.BlockSpec((D, width), lambda c: (0, jnp.clip(c - chunks, 0, 1))),
            pl.BlockSpec((width, D), lambda c: (upto(c), 0)),
            whole((rows, D)),
            whole((rows, D)),
            pl.BlockSpec((1, width), lambda c: (0, upto(c))),
            whole((4, D)),
        ),
        out_shape=(
            jax.ShapeDtypeStruct((D, FF), BF16),
            jax.ShapeDtypeStruct((D, D), BF16),
            jax.ShapeDtypeStruct((FF, D), BF16),
            jax.ShapeDtypeStruct((rows, D), F32),
            jax.ShapeDtypeStruct((rows, D), BF16),
            jax.ShapeDtypeStruct((1, FF), F32),
            jax.ShapeDtypeStruct((4, D), F32),
        ),
        scratch_shapes=[
            pltpu.VMEM((rows, D), BF16),
            pltpu.VMEM((D, rows), BF16),
            pltpu.VMEM((rows, D), F32),
        ],
        compiler_params=vmem(),
        cost_estimate=cost(4 * rows * D * (D + 2 * FF), 40e6),
        name="feed_back",
    )(grad, active, slope, hidden_in, middle, attended, square, shrink, square, modulation)


def project_back_kernel(
    dq_ref, low_ref, own_ref, high_ref, h_ref, halo_ref, x_ref, mid_grad_ref, w_ref, mod_ref,
    square_ref, out_ref, db_ref, sums_ref,
    turned, total, around, sending, landing, send_sem, recv_sem,
):
    step = pl.program_id(0)
    rows = x_ref.shape[0]
    middle = slice(WIN_MAX, WIN_MAX + rows)
    sources = (sending.at[0], sending.at[1])

    @pl.when(step == 0)
    def _():
        around[...] = jnp.zeros_like(around)
        total[...] = jnp.zeros_like(total)
        greet_beside()

    @pl.when(step < 4)
    def _():
        around[0] += product(low_ref[0], w_ref[...], MATMUL_RIGHT)
        around[1] += product(high_ref[0], w_ref[...], MATMUL_RIGHT)

    @pl.when(step == 3)
    def _():
        sending[...] = around[...].astype(BF16)
        halo_start(sources, landing, send_sem, recv_sem)
        turned[:, :WIN_MAX] = halo_ref[0].T
        turned[:, middle] = h_ref[...].T
        turned[:, WIN_MAX + rows :] = halo_ref[1].T

    @pl.when((step >= 4) & (step < 6))
    def _():
        grad = dq_ref[...]
        db_ref[...] = jnp.sum(grad.astype(F32), axis=0, keepdims=True)
        square_ref[...] = product(turned[:, middle], grad).astype(BF16)
        total[...] += product(grad, w_ref[...], MATMUL_RIGHT)

    @pl.when(step >= 6)
    def _():
        grad = jnp.concatenate([low_ref[0], own_ref[0], high_ref[0]], axis=0)
        db_ref[...] = jnp.sum(grad.astype(F32), axis=0, keepdims=True)
        square_ref[...] = product(turned[...], grad).astype(BF16)
        total[...] += product(own_ref[0], w_ref[...], MATMUL_RIGHT)

    @pl.when(step == 9)
    def _():
        halo_wait(sources, landing, send_sem, recv_sem)
        normed, inverse = normalize(x_ref[...].astype(F32))
        grad = total[...] + landing[0].astype(F32) + landing[1].astype(F32)
        sums_ref[0:1] = jnp.sum(grad, axis=0, keepdims=True)
        sums_ref[1:2] = jnp.sum(grad * normed, axis=0, keepdims=True)
        out_ref[...] = mid_grad_ref[...] + normalize_back(
            grad * (1.0 + mod_ref[0, 1:2]), normed, inverse
        )


def project_back(layer, dq, low, own, high, hidden_in, halo, stream, mid_grad, square, modulation, ident):
    rows = dq.shape[0]
    width = STEP_COLUMNS
    whole = lambda shape: pl.BlockSpec(shape, lambda c: (0,) * len(shape))

    def halves(c):
        at = jnp.where(c < 4, c, jnp.clip(c - 6, 0, 3))
        return (at // 2, 0, at % 2)

    later = pl.BlockSpec((1, rows, width), halves)
    own_columns = lambda c: (0, jnp.clip(c - 4, 0, 5))
    return pl.pallas_call(
        project_back_kernel,
        grid=(10,),
        in_specs=[
            pl.BlockSpec((rows, width), lambda c: (0, jnp.clip(c - 4, 0, 1))),
            later,
            later,
            later,
            whole((rows, D)),
            whole((2, rows, D)),
            whole((rows, D)),
            whole((rows, D)),
            pl.BlockSpec((D, width), lambda c: (0, jnp.where(c < 4, c + 2, c - 4))),
            pl.BlockSpec((1, 4, D), lambda c: (layer, 0, 0)),
        ],
        out_specs=(
            pl.BlockSpec((D, width), own_columns),
            whole((rows, D)),
            pl.BlockSpec((1, width), own_columns),
            whole((2, D)),
        ),
        out_shape=(
            jax.ShapeDtypeStruct((D, 3 * D), BF16),
            jax.ShapeDtypeStruct((rows, D), F32),
            jax.ShapeDtypeStruct((1, 3 * D), F32),
            jax.ShapeDtypeStruct((2, D), F32),
        ),
        scratch_shapes=[
            pltpu.VMEM((D, rows + 2 * WIN_MAX), BF16),
            pltpu.VMEM((rows, D), F32),
            pltpu.VMEM((2, rows, D), F32),
            pltpu.VMEM((2, rows, D), BF16),
            pltpu.VMEM((2, rows, D), BF16),
            pltpu.SemaphoreType.DMA((2,)),
            pltpu.SemaphoreType.DMA((2,)),
        ],
        compiler_params=pltpu.CompilerParams(
            vmem_limit_bytes=56 << 20, collective_id=ident, has_side_effects=True
        ),
        cost_estimate=cost(4 * rows * D * 6 * D, 20e6),
        name="project_back",
    )(dq, low, own, high, hidden_in, halo, stream, mid_grad, square, modulation)


def direct():
    return lax.axis_size("dp") == NZ * NY and lax.axis_size("fsdp") == NX * 2


BOTH = ("dp", "fsdp")


def pack_small(bias, table):
    flat = jnp.concatenate([bias.reshape(-1), table.reshape(-1)])
    flat = jnp.pad(flat, (0, OWN_ROWS[4] * SMALL - flat.shape[0]))
    return flat.reshape(1, OWN_ROWS[4], SMALL)


def unpack_small(whole, lead_row):
    count = lax.axis_size("dp") * lax.axis_size("fsdp")
    flat = whole.reshape(count, -1).astype(F32)
    wide = LAYERS * 9 * D // count
    bias = flat[:, :wide].reshape(count, LAYERS, 9, -1).transpose(1, 2, 0, 3).reshape(LAYERS, 1, 9 * D)
    table = flat[:, wide : wide + LAYERS * LEADS * 4 * D // count].reshape(count, LAYERS, LEADS, -1)
    rows = lax.dynamic_index_in_dim(table, lead_row, 2, keepdims=False)
    return bias, rows.transpose(1, 0, 2).reshape(LAYERS, 4, D)


def plain_fetch(masters, layer):
    square = jnp.concatenate([masters[n][layer].astype(BF16) for n in range(3)], axis=1)
    shrink = masters[3][layer].astype(BF16)
    return (
        lax.all_gather(square, BOTH, axis=0, tiled=True),
        lax.all_gather(shrink, BOTH, axis=0, tiled=True),
    )


def plain_small(masters, lead_row):
    bias = lax.all_gather(masters[4].astype(BF16), BOTH, axis=2, tiled=True)
    table = lax.all_gather(masters[5].astype(BF16), BOTH, axis=2, tiled=True)
    modulation = lax.dynamic_index_in_dim(table, lead_row, 1, keepdims=False)
    return bias.astype(F32).reshape(LAYERS, 1, 9 * D), modulation.astype(F32).reshape(LAYERS, 4, D)


def plain_reduce(whole):
    return lax.psum_scatter(whole, BOTH, scatter_dimension=0, tiled=True).astype(F32)


def reduce_small_inputs(bias_grads, rows_grads, lead_hot):
    count = lax.axis_size("dp") * lax.axis_size("fsdp")
    bias = bias_grads.reshape(LAYERS * 9, count, -1).transpose(1, 0, 2).reshape(count, -1)
    rows = rows_grads.reshape(LAYERS, 1, count, -1) * lead_hot[None, :, None, None]
    rows = rows.transpose(2, 0, 1, 3).reshape(count, -1)
    flat = jnp.concatenate([bias, rows], axis=1)
    used = flat.shape[1]
    flat = jnp.pad(flat, ((0, 0), (0, OWN_ROWS[4] * SMALL - used)))
    return flat.reshape(-1, SMALL).astype(BF16)


def split_small(own):
    count = lax.axis_size("dp") * lax.axis_size("fsdp")
    flat = own.reshape(-1)
    wide = LAYERS * 9 * D // count
    used = wide + LAYERS * LEADS * 4 * D // count
    return flat[:wide].reshape(LAYERS, 9, -1), flat[wide:used].reshape(LAYERS, LEADS, -1)


def bands(segment_ids, segment_starts, padding_mask, offset, rows):
    length = segment_ids.shape[0]
    position = jnp.arange(length, dtype=jnp.int32)
    real = padding_mask == 1
    names = jnp.where(real, segment_ids, length + position)
    fill = jnp.full((WIN_MAX,), -1, jnp.int32)
    wide = lax.dynamic_slice_in_dim(
        jnp.concatenate([fill, names, fill - 1]), offset, rows + 2 * WIN_MAX
    )
    own = lax.dynamic_slice_in_dim(names, offset, rows)
    piece = lambda array: lax.dynamic_slice_in_dim(array, offset, rows).reshape(-1, BAND)
    at = offset + jnp.arange(rows // BAND, dtype=jnp.int32) * BAND
    starts, windows, kept = piece(segment_starts), piece(segment_ids), piece(padding_mask) == 1
    begins = jnp.where(kept[:, 0], starts[:, 0], at)
    ends = jnp.sum((segment_ids[None, :] <= windows[:, -1:]).astype(jnp.int32), axis=1)
    ends = jnp.where(kept[:, -1], ends, at + BAND)
    low = (begins - offset + WIN_MAX) // BAND
    need = (ends - offset + WIN_MAX + BAND - 1) // BAND - low
    return jnp.stack([low, need]), own, wide


def adam_update(weight, gradient, moment, square, step_rate, decay_rate):
    moment = BETA_ONE * moment + (1.0 - BETA_ONE) * gradient
    square = BETA_TWO * square + (1.0 - BETA_TWO) * gradient * gradient
    first_fix = 1.0 - BETA_ONE**STEP
    second_fix = 1.0 - BETA_TWO**STEP
    update = moment / first_fix / (jnp.sqrt(square / second_fix) + ADAM_EPSILON)
    weight = weight - step_rate * (update + decay_rate * weight)
    return (weight, moment, square, weight.astype(jnp.bfloat16))


def shards(
    tokens,
    cotangent,
    segment_ids,
    segment_starts,
    padding_mask,
    lead_index,
    input_weights,
    input_moment,
    input_square,
    output_weights,
    output_moment,
    output_square,
    expand_weights,
    expand_moment,
    expand_square,
    shrink_weights,
    shrink_moment,
    shrink_square,
    bias_vector,
    bias_moment,
    bias_square,
    lead_table,
    lead_moment,
    lead_square,
):
    rows = tokens.shape[0]
    offset = lax.axis_index("fsdp") * rows
    bounds, own_names, wide_names = bands(segment_ids, segment_starts, padding_mask, offset, rows)
    ids_query = jnp.broadcast_to(own_names[:, None], (rows, 128))
    ids_key = jnp.broadcast_to(wide_names[None, :], (8, wide_names.shape[0]))
    ids_query_row = jnp.broadcast_to(own_names[None, :], (8, rows))
    ids_key_column = jnp.broadcast_to(wide_names[:, None], (wide_names.shape[0], 128))
    fill = jnp.zeros((WIN_MAX,), jnp.int32)
    relative = jnp.arange(segment_starts.shape[0], dtype=jnp.int32) - segment_starts
    relative = jnp.concatenate([fill, relative, fill])
    cosine, sine = rotary_tables(
        lax.dynamic_slice_in_dim(relative, offset, rows + 2 * WIN_MAX)
    )
    lead_row = lead_index[0]
    lead_hot = (jnp.arange(LEADS, dtype=jnp.int32) == lead_row).astype(F32)
    masters = (input_weights, output_weights, expand_weights, shrink_weights, bias_vector, lead_table)
    linked = direct()
    if linked:
        small = pack_small(bias_vector, lead_table)
        small_full, *first = alone(
            GatherJob(GATHERED, 0), (small, *masters[:4]), "gather_first", 0
        )
        bias, modulation = unpack_small(small_full, lead_row)
        layers = [first]
    else:
        layers = [plain_fetch(masters, 0)]
        bias, modulation = plain_small(masters, lead_row)
    layers += [plain_fetch(masters, layer) for layer in range(1, LAYERS)]
    stream = tokens
    saved = []
    for layer in range(LAYERS):
        square, shrink = layers[layer]
        queries, own, low, high, first_in, halo = project(
            layer, stream, square, bias, modulation, cosine, sine, 10 + layer
        )
        attended, lse = attend(bounds, queries, low, own, high, ids_query, ids_key)
        middle, second_in, active, slope, result = feed(
            layer, attended, stream, square, shrink, bias, modulation
        )
        saved.append(
            (stream, queries, low, own, high, first_in, halo, attended, lse, middle, second_in, active, slope)
        )
        stream = result
    grad = cotangent
    partials = [None] * LAYERS
    bias_grads = [None] * LAYERS
    rows_grads = [None] * LAYERS
    reduced = [[None] * 4 for _ in range(LAYERS)]
    for layer in reversed(range(LAYERS)):
        square, shrink = layers[layer]
        (
            before, queries, low, own, high, first_in, halo, attended, lse, middle, second_in, active, slope,
        ) = saved[layer]
        expand_grad, output_grad, shrink_grad, mid_grad, attended_grad, expand_bias, sums = feed_back(
            layer, grad, active, slope, second_in, middle, attended, square, shrink, modulation
        )
        dq, low_grad, own_grad, high_grad = attend_back(
            bounds, queries, attended_grad, attended, lse, low, own, high, ids_query_row,
            ids_key_column, cosine, sine,
        )
        input_grad, grad, input_bias, more_sums = project_back(
            layer, dq, low_grad, own_grad, high_grad, first_in, halo, before, mid_grad, square, modulation,
            20 + layer,
        )
        bias_grads[layer] = jnp.concatenate([input_bias[0], sums[2], expand_bias[0], sums[3]])
        rows_grads[layer] = jnp.concatenate([more_sums[0], more_sums[1], sums[0], sums[1]])
        partials[layer] = (input_grad, output_grad, expand_grad, shrink_grad)
        if not linked:
            reduced[layer] = [plain_reduce(whole) for whole in partials[layer]]
        elif layer > 0:
            later_shrink = lax.psum_scatter(shrink_grad, BOTH, scatter_dimension=0, tiled=True)
    if linked:
        small = reduce_small_inputs(jnp.stack(bias_grads), jnp.stack(rows_grads), lead_hot)
        small, later_shrink = lax.optimization_barrier((small, later_shrink))
        reduced[1][3] = later_shrink.astype(F32)
        job = ScatterJob(SCATTERED)
        input_grad, output_grad, expand_grad, shrink_grad = partials[0]
        wide, reduced[0][3] = alone(
            job,
            (*partials[1][:3], expand_grad, shrink_grad, input_grad, output_grad, small),
            "scatter_last",
            1,
        )
        part = lambda n: wide[:, job.first[n] : job.first[n] + WIDTHS[n]]
        reduced[0][:3] = [part(0), part(1), part(2)]
        reduced[1][:3] = [part(5), part(6), part(7)]
        bias_grad, lead_grad = lax.optimization_barrier(split_small(part(4)))
    else:
        bias_grad = lax.psum_scatter(
            jnp.stack(bias_grads).reshape(LAYERS, 9, D), BOTH, scatter_dimension=2, tiled=True
        )
        lead_grad = lax.psum_scatter(
            jnp.stack(rows_grads)[:, None, :] * lead_hot[None, :, None], BOTH, scatter_dimension=2,
            tiled=True,
        )
    moments = (input_moment, output_moment, expand_moment, shrink_moment, bias_moment, lead_moment)
    squares = (input_square, output_square, expand_square, shrink_square, bias_square, lead_square)
    results = []
    for number in range(6):
        if number < 4:
            gradient = jnp.stack([reduced[layer][number] for layer in range(LAYERS)])
        else:
            gradient = (bias_grad, lead_grad)[number - 4]
        results.append(
            adam_update(
                masters[number],
                gradient,
                moments[number],
                squares[number],
                RATE_MATRIX if number < 4 else RATE_VECTOR,
                DECAY if number < 4 else 0.0,
            )
        )
    return (stream, grad, *(array for four in results for array in four))


def solution(mesh):
    rows = P(("dp", "fsdp"), None)
    matrix = P(None, ("dp", "fsdp"), None)
    vector = P(None, None, ("dp", "fsdp"))
    return jax.shard_map(
        shards,
        mesh=mesh,
        in_specs=(rows,) * 2 + (P("dp"),) * 4 + (matrix,) * 12 + (vector,) * 6,
        out_specs=(rows,) * 2 + (matrix,) * 16 + (vector,) * 8,
        check_vma=False,
    )
```

```python
import functools
import math

import jax
import jax.numpy as jnp
from jax import lax
from jax.experimental import pallas as pl
from jax.experimental.pallas import tpu as pltpu
from jax.sharding import PartitionSpec as P

D = 768
FF = 3072
HEADS = 12
HEAD_DIM = 64
LEADS = 20
LAYERS = 2
WIN_MAX = 512
STEP = 10

EPSILON = 1e-06
NEGATIVE = -1e30
BETA_ONE = 0.5
BETA_TWO = 0.5
RATE_MATRIX = 0.08
RATE_VECTOR = 0.3
DECAY = 0.1
ADAM_EPSILON = 1e-08

MESH = pl.DeviceIdType.MESH
NZ, NY, NX = 4, 2, 2
CHIPS = NZ * NY * NX
SMALL = 256
GATHERED = (
    (4, "small", 0, 48, 0, 48, 0, 128, "zxy"),
    (0, "square", 0, 48, 0, 48, 0, 1152, "xzy"),
    (1, "square", 2304, 48, 0, 48, 0, 384, "yzx"),
    (2, "square", 3072, 48, 0, 48, 0, 768, "yzx"),
    (2, "square", 3072, 48, 0, 48, 768, 768, "zxy"),
    (3, "shrink", 0, 192, 0, 48, 0, 384, "zxy"),
    (3, "shrink", 0, 192, 48, 144, 0, 384, "zyx"),
)
SCATTERED = (
    (5, "later_in", 0, 48, 0, 48, 0, 384, "xzy"),
    (5, "later_in", 0, 48, 0, 48, 384, 384, "yzx"),
    (5, "later_in", 0, 48, 0, 48, 768, 384, "zxy"),
    (6, "later_out", 0, 48, 0, 48, 0, 384, "zyx"),
    (7, "later_expand", 0, 48, 0, 48, 0, 384, "xzy"),
    (7, "later_expand", 0, 48, 0, 48, 384, 384, "yzx"),
    (7, "later_expand", 0, 48, 0, 48, 768, 384, "zxy"),
    (7, "later_expand", 0, 48, 0, 48, 1152, 384, "zyx"),
    (2, "expand", 0, 48, 0, 48, 0, 768, "xzy"),
    (2, "expand", 0, 48, 0, 48, 768, 768, "yzx"),
    (3, "shrink", 0, 192, 0, 96, 0, 384, "zxy"),
    (3, "shrink", 0, 192, 96, 96, 0, 384, "zyx"),
    (0, "in", 0, 48, 0, 48, 0, 384, "xzy"),
    (0, "in", 0, 48, 0, 48, 384, 384, "yzx"),
    (0, "in", 0, 48, 0, 48, 768, 384, "zxy"),
    (1, "out", 0, 48, 0, 48, 0, 384, "zyx"),
    (4, "small", 0, 48, 0, 48, 0, 128, "zyx"),
)
LAG = (0.0,) * 4 + (0.5,) * 4 + (1.0,) * 2 + (1.5,) * 2 + (2.0,) * 5
WIDTHS = (2304, 768, 3072, 768, SMALL, 2304, 768, 3072)
OWN_ROWS = (24, 24, 24, 96, 24, 24, 24, 24)
WHOLES = {"square": (768, 6144), "shrink": (3072, 768), "small": (768, SMALL)}
AXIS = {"z": 0, "y": 1, "x": 2}


def place():
    dp, fs = lax.axis_index("dp"), lax.axis_index("fsdp")
    return lax.div(dp, NY), lax.rem(dp, NY), lax.div(fs, 2), lax.rem(fs, 2)


def device(z, y, x, core):
    return (z * NY + y, x * 2 + core)


def offsets():
    found = [
        (dz, dy, dx)
        for dz in range(1 - NZ, NZ)
        for dy in range(NY)
        for dx in range(NX)
    ]
    return sorted(found, key=lambda d: (abs(d[0]) + d[1] + d[2], abs(d[0])))


def last_axis(order, away):
    last = -1
    for number, axis in enumerate(order):
        if away[AXIS[axis]] != 0:
            last = number
    return last


def children(order, away):
    last = last_axis(order, away)
    found = []
    for number, axis in enumerate(order):
        if number < last:
            continue
        if axis == "z":
            if number > last:
                found += ["up", "down"]
            else:
                found += ["up"] if away[0] < 0 else ["down"]
        elif number > last:
            found.append(axis)
    return found


def exists(side, z):
    return {"up": z < NZ - 1, "down": z > 0}.get(side)


def neighbour(side, spot):
    z, y, x, core = spot
    return {
        "up": device(z + 1, y, x, core),
        "down": device(z - 1, y, x, core),
        "y": device(z, 1 - y, x, core),
        "x": device(z, y, 1 - x, core),
        "core": device(z, y, x, 1 - core),
    }[side]


def guarded(condition, action):
    if condition is None:
        action()
    else:
        pl.when(condition)(action)


def both(first, second):
    if first is None:
        return second
    if second is None:
        return first
    return first & second


def greet(spot):
    barrier = pltpu.get_barrier_semaphore()
    z, y, x, core = spot
    sides = [(neighbour(side, spot), exists(side, z)) for side in ("up", "down", "x", "y", "core")]
    count = 3
    for target, there in sides:

        def hello(target=target):
            pl.semaphore_signal(barrier, inc=1, device_id=target, device_id_type=MESH)

        guarded(there, hello)
        if there is not None:
            count = count + jnp.where(there, 1, 0)
    pl.semaphore_wait(barrier, count)


def source_of(spot, away):
    z, y, x, _ = spot
    sz = z + away[0]
    sy = 1 - y if away[1] else y
    sx = 1 - x if away[2] else x
    valid = None
    if away[0] > 0:
        valid = sz < NZ
    elif away[0] < 0:
        valid = sz >= 0
    return sz, sy, sx, valid


def chip_number(sz, sy, sx):
    return (sz * NY + sy) * NX + sx


def aligned(value, by):
    return value if isinstance(value, int) else pl.multiple_of(value, by)


def piece_view(ref, piece, chip, core):
    number, _, base, chip_rows, low, rows, column, columns, _ = piece
    half = WIDTHS[number] // 2
    return ref.at[
        pl.ds(aligned(chip * chip_rows + low, 16), rows),
        pl.ds(aligned(base + core * half + column, 128), columns),
    ]


class Job:
    def __init__(self, pieces):
        self.pieces = pieces
        self.numbers = tuple(dict.fromkeys(p[0] for p in pieces))
        self.arrays = tuple(dict.fromkeys(p[1] for p in pieces))

    def scratch_of(self, rows, dtype):
        return [pltpu.VMEM((rows * OWN_ROWS[n], WIDTHS[n] // 2), dtype) for n in self.numbers]


class GatherJob(Job):
    def __init__(self, pieces, layer):
        super().__init__(pieces)
        self.layer = layer
        self.inputs = len(self.numbers)
        self.outputs = tuple(jax.ShapeDtypeStruct(WHOLES[a], jnp.bfloat16) for a in self.arrays)
        count = len(pieces)
        self.scratch = (
            self.scratch_of(1, jnp.float32)
            + self.scratch_of(1, jnp.float32)
            + self.scratch_of(2, jnp.bfloat16)
            + [
                pltpu.SemaphoreType.DMA((8,)),
                pltpu.SemaphoreType.DMA((8,)),
                pltpu.SemaphoreType.DMA((8,)),
                pltpu.SemaphoreType.DMA((count,)),
                pltpu.SemaphoreType.DMA((count, 4)),
                pltpu.SemaphoreType.DMA((count, CHIPS)),
                pltpu.SemaphoreType.DMA((count,)),
                pltpu.SemaphoreType.DMA((count,)),
            ]
        )

    def bind(self, inputs, outputs, scratch):
        pieces, numbers, layer = self.pieces, self.numbers, self.layer
        many = len(numbers)
        take = iter(scratch)
        named = lambda: dict(zip(numbers, [next(take) for _ in range(many)]))
        masters = dict(zip(numbers, inputs))
        wholes = dict(zip(self.arrays, outputs))
        mine, theirs, blocks = named(), named(), named()
        local_sem, pair_send, pair_recv, store_sem, send_sem, recv_sem, core_send, core_recv = take
        spot = place()
        z, y, x, core = spot
        me = chip_number(z, y, x)
        partner = neighbour("core", spot)

        def columns_of(number, side):
            half = WIDTHS[number] // 2
            which = 0 if number == 4 else layer
            return masters[number].at[which, :, pl.ds(aligned(side * half, 128), half)]

        def load(number):
            return pltpu.make_async_copy(columns_of(number, core), mine[number], local_sem.at[number])

        def swap(number):
            return pltpu.make_async_remote_copy(
                src_ref=columns_of(number, 1 - core),
                dst_ref=theirs[number],
                send_sem=pair_send.at[number],
                recv_sem=pair_recv.at[number],
                device_id=partner,
                device_id_type=MESH,
            )

        def relay(index, away, source, view):
            piece = pieces[index]
            for side in children(piece[8], away):

                def send(side=side):
                    pltpu.make_async_remote_copy(
                        src_ref=view,
                        dst_ref=piece_view(wholes[piece[1]], piece, source, core),
                        send_sem=send_sem.at[index, ("up", "down", "x", "y").index(side)],
                        recv_sem=recv_sem.at[index, source],
                        device_id=neighbour(side, spot),
                        device_id_type=MESH,
                    ).start()

                guarded(exists(side, z), send)
            pltpu.make_async_remote_copy(
                src_ref=view,
                dst_ref=piece_view(wholes[piece[1]], piece, source, core),
                send_sem=core_send.at[index],
                recv_sem=core_recv.at[index],
                device_id=partner,
                device_id_type=MESH,
            ).start()

        def own_view(index):
            piece = pieces[index]
            return blocks[piece[0]].at[pl.ds(piece[4], piece[5]), pl.ds(piece[6], piece[7])]

        def store(index):
            piece = pieces[index]
            return pltpu.make_async_copy(
                own_view(index), piece_view(wholes[piece[1]], piece, me, core), store_sem.at[index]
            )

        def start():
            for number in numbers:
                load(number).start()
            for number in numbers:
                swap(number).start()

        def own(number):
            load(number).wait()
            swap(number).wait_recv()
            own_rows, other_rows = mine[number][...], theirs[number][...]
            is_first = core == 0
            block = jnp.concatenate(
                [jnp.where(is_first, own_rows, other_rows), jnp.where(is_first, other_rows, own_rows)],
                axis=0,
            )
            blocks[number][...] = block.astype(jnp.bfloat16)
            for index, piece in enumerate(pieces):
                if piece[0] == number:
                    store(index).start()
                    relay(index, (0, 0, 0), me, own_view(index))

        def event(away, index):
            piece = pieces[index]
            sz, sy, sx, valid = source_of(spot, away)
            source = chip_number(sz, sy, sx)

            def arrival():
                view = piece_view(wholes[piece[1]], piece, source, core)
                pltpu.make_async_remote_copy(
                    src_ref=view,
                    dst_ref=view,
                    send_sem=send_sem.at[index, 0],
                    recv_sem=recv_sem.at[index, source],
                    device_id=partner,
                    device_id_type=MESH,
                ).wait_recv()
                relay(index, away, source, view)

            guarded(valid, arrival)

        def finish():
            for index in range(len(pieces)):
                store(index).wait()
            for number in numbers:
                swap(number).wait_send()
            for index, piece in enumerate(pieces):
                number, rows, columns = piece[0], piece[5], piece[7]

                def span(chunks, core_at, piece=piece, number=number, rows=rows, columns=columns):
                    half = WIDTHS[number] // 2
                    first = aligned(piece[2] + core_at * half + piece[6], 128)
                    return wholes[piece[1]].at[pl.ds(0, chunks * rows), pl.ds(first, columns)]

                def wait_send(chunks, sem, index=index, span=span):
                    pltpu.make_async_remote_copy(
                        src_ref=span(chunks, core),
                        dst_ref=span(chunks, core),
                        send_sem=sem,
                        recv_sem=recv_sem.at[index, 0],
                        device_id=partner,
                        device_id_type=MESH,
                    ).wait_send()

                before = 1
                for axis in piece[8]:
                    if axis == "z":
                        for at in range(NZ):

                            @pl.when(z == at)
                            def _(at=at, before=before, index=index, wait_send=wait_send):
                                if at < NZ - 1:
                                    wait_send(before * (at + 1), send_sem.at[index, 0])
                                if at > 0:
                                    wait_send(before * (NZ - at), send_sem.at[index, 1])

                        before *= NZ
                    else:
                        wait_send(before, send_sem.at[index, 2 if axis == "x" else 3])
                        before *= 2
                wait_send(CHIPS, core_send.at[index])
                pltpu.make_async_remote_copy(
                    src_ref=span(CHIPS, 1 - core),
                    dst_ref=span(CHIPS, 1 - core),
                    send_sem=core_send.at[index],
                    recv_sem=core_recv.at[index],
                    device_id=partner,
                    device_id_type=MESH,
                ).wait_recv()

        actions = [start] + [functools.partial(own, number) for number in numbers]
        for away in offsets():
            if away != (0, 0, 0):
                actions += [functools.partial(event, away, index) for index in range(len(pieces))]
        return actions + [finish]


def slot_of(order, side, source):
    sizes = {"z": NZ, "y": NY, "x": NX}
    base = 0
    ahead = 1
    number = 0
    for axis in order:
        at = source[AXIS[axis]]
        for here in ["up", "down"] if axis == "z" else [axis]:
            if axis == "z":
                if here == side:
                    return base + number * NZ + at
                base += ahead * NZ
            else:
                if here == side:
                    return base + number
                base += ahead
        number = number * sizes[axis] + at
        ahead *= sizes[axis]
    return base


def slot_count(order):
    return slot_of(order, None, (0, 0, 0))


class ScatterJob(Job):
    def __init__(self, pieces):
        super().__init__(pieces)
        self.inputs = len(self.arrays)
        self.first = {}
        width = 0
        for number in self.numbers:
            if number != 3:
                self.first[number] = width
                width += WIDTHS[number]
        self.first[3] = 0
        self.outputs = (
            jax.ShapeDtypeStruct((OWN_ROWS[0], width), jnp.float32),
            jax.ShapeDtypeStruct((OWN_ROWS[3], WIDTHS[3]), jnp.float32),
        )
        count = len(pieces)
        most = max(slot_count(p[8]) for p in pieces)
        self.scratch = (
            self.scratch_of(32, jnp.bfloat16)
            + self.scratch_of(32, jnp.bfloat16)
            + self.scratch_of(2, jnp.float32)
            + self.scratch_of(1, jnp.float32)
            + [pltpu.VMEM((slot_count(p[8]), p[5], p[7]), jnp.bfloat16) for p in pieces]
            + [
                pltpu.SemaphoreType.DMA((8,)),
                pltpu.SemaphoreType.DMA((8,)),
                pltpu.SemaphoreType.DMA((8,)),
                pltpu.SemaphoreType.DMA((count, CHIPS)),
                pltpu.SemaphoreType.DMA((count, most)),
                pltpu.SemaphoreType.DMA((8,)),
                pltpu.SemaphoreType.DMA((8,)),
                pltpu.SemaphoreType.DMA((16,)),
            ]
        )

    def bind(self, inputs, outputs, scratch):
        pieces, numbers = self.pieces, self.numbers
        many = len(numbers)
        take = iter(scratch)
        named = lambda: dict(zip(numbers, [next(take) for _ in range(many)]))
        partials = dict(zip(self.arrays, inputs))
        outs = {n: outputs[1 if n == 3 else 0] for n in numbers}
        starts = self.first
        own, pair, total, handed = named(), named(), named(), named()
        slots = [next(take) for _ in pieces]
        own_sem, pair_send, pair_recv, send_sem, recv_sem, end_send, end_recv, out_sem = take
        base = {p[0]: p[2] for p in pieces}
        array = {p[0]: p[1] for p in pieces}
        spot = place()
        z, y, x, core = spot
        partner = neighbour("core", spot)

        def columns_of(number, side):
            half = WIDTHS[number] // 2
            first = aligned(base[number] + side * half, 128)
            return partials[array[number]].at[:, pl.ds(first, half)]

        def load(number):
            return pltpu.make_async_copy(columns_of(number, core), own[number], own_sem.at[number])

        def swap(number):
            return pltpu.make_async_remote_copy(
                src_ref=columns_of(number, 1 - core),
                dst_ref=pair[number],
                send_sem=pair_send.at[number],
                recv_sem=pair_recv.at[number],
                device_id=partner,
                device_id_type=MESH,
            )

        def start():
            for number in numbers:
                load(number).start()
                swap(number).start()

        def ready(number):
            load(number).wait()
            swap(number).wait_recv()

        def view_of(piece, source):
            _, _, _, chip_rows, low, rows, column, columns, _ = piece
            return pl.ds(aligned(source * chip_rows + low, 16), rows), pl.ds(column, columns)

        def event(away, index):
            piece = pieces[index]
            number, _, _, chip_rows, low, rows, column, columns, order = piece
            sz, sy, sx, valid = source_of(spot, away)
            where = (sz, sy, sx)
            source = chip_number(sz, sy, sx)
            last = last_axis(order, away)

            def act():
                kids = children(order, away)
                for side in kids:

                    def arrived(side=side):
                        slot = slot_of(order, side, where)
                        pltpu.make_async_remote_copy(
                            src_ref=slots[index].at[slot],
                            dst_ref=slots[index].at[slot],
                            send_sem=send_sem.at[index, 0],
                            recv_sem=recv_sem.at[index, slot],
                            device_id=partner,
                            device_id_type=MESH,
                        ).wait_recv()

                    guarded(exists(side, z), arrived)
                view = view_of(piece, source)
                value = own[number][view].astype(jnp.float32) + pair[number][view].astype(jnp.float32)
                for side in kids:
                    landed = slots[index][slot_of(order, side, where)].astype(jnp.float32)
                    there = exists(side, z)
                    value = value + (landed if there is None else jnp.where(there, landed, 0.0))
                if last < 0:
                    total[number][pl.ds(low, rows), pl.ds(column, columns)] = value
                    return
                pair[number][view] = value.astype(jnp.bfloat16)
                axis = order[last]
                if axis == "z":
                    side = "up" if away[0] < 0 else "down"
                    parent = neighbour("down" if away[0] < 0 else "up", spot)
                else:
                    side = axis
                    parent = neighbour(axis, spot)
                slot = slot_of(order, side, where)
                pltpu.make_async_remote_copy(
                    src_ref=pair[number].at[view],
                    dst_ref=slots[index].at[slot],
                    send_sem=send_sem.at[index, source],
                    recv_sem=recv_sem.at[index, slot],
                    device_id=parent,
                    device_id_type=MESH,
                ).start()

            guarded(valid, act)

        def end(number):
            rows = OWN_ROWS[number]
            return pltpu.make_async_remote_copy(
                src_ref=total[number].at[pl.ds(aligned((1 - core) * rows, 8), rows)],
                dst_ref=handed[number],
                send_sem=end_send.at[number],
                recv_sem=end_recv.at[number],
                device_id=partner,
                device_id_type=MESH,
            )

        def write(number, other):
            half = WIDTHS[number] // 2
            rows = OWN_ROWS[number]
            source = handed[number] if other else total[number].at[pl.ds(aligned(core * rows, 8), rows)]
            side = 1 - core if other else core
            return pltpu.make_async_copy(
                source,
                outs[number].at[:, pl.ds(aligned(starts[number] + side * half, 128), half)],
                out_sem.at[number + 8 * other],
            )

        def finish():
            for number in numbers:
                end(number).start()
            for number in numbers:
                write(number, 0).start()
            for number in numbers:
                end(number).wait_recv()
                write(number, 1).start()
            for number in numbers:
                write(number, 0).wait()
                write(number, 1).wait()
                end(number).wait_send()
                swap(number).wait_send()
            for index, piece in enumerate(pieces):
                for away in offsets():
                    if away == (0, 0, 0):
                        continue
                    sz, sy, sx, valid = source_of(spot, away)
                    source = chip_number(sz, sy, sx)

                    def sent(index=index, piece=piece, source=source):
                        pltpu.make_async_remote_copy(
                            src_ref=pair[piece[0]].at[view_of(piece, source)],
                            dst_ref=slots[index].at[0],
                            send_sem=send_sem.at[index, source],
                            recv_sem=recv_sem.at[index, 0],
                            device_id=partner,
                            device_id_type=MESH,
                        ).wait_send()

                    guarded(valid, sent)

        actions = [start]
        known = set()
        level = lambda away: NZ + 1 - (abs(away[0]) + away[1] + away[2])
        events = [
            (level(away) + LAG[index], index, place_at, away)
            for place_at, away in enumerate(reversed(offsets()))
            for index in range(len(pieces))
        ]
        for _, index, _, away in sorted(events):
            number = pieces[index][0]
            if number not in known:
                known.add(number)
                actions.append(functools.partial(ready, number))
            actions.append(functools.partial(event, away, index))
        return actions + [finish]


def alone(job, arrays, name, ident):
    anywhere = pl.BlockSpec(memory_space=pl.ANY)

    def kernel(*refs):
        first, second = job.inputs, job.inputs + len(job.outputs)
        greet(place())
        for action in job.bind(refs[:first], refs[first:second], refs[second:]):
            action()

    return pl.pallas_call(
        kernel,
        out_shape=job.outputs,
        in_specs=[anywhere] * job.inputs,
        out_specs=tuple([anywhere] * len(job.outputs)),
        scratch_shapes=job.scratch,
        name=name,
        compiler_params=pltpu.CompilerParams(
            collective_id=ident, has_side_effects=True, vmem_limit_bytes=60 << 20
        ),
        cost_estimate=pl.CostEstimate(flops=0, bytes_accessed=int(2e8), transcendentals=0),
    )(*arrays)


def normalize(values):
    centred = values - jnp.mean(values, axis=-1, keepdims=True)
    inverse = lax.rsqrt(jnp.mean(centred * centred, axis=-1, keepdims=True) + EPSILON)
    return (centred * inverse, inverse)


def normalize_back(grad_normed, normed, inverse):
    return inverse * (
        grad_normed
        - jnp.mean(grad_normed, axis=-1, keepdims=True)
        - normed * jnp.mean(grad_normed * normed, axis=-1, keepdims=True)
    )


def rotary_tables(relative):
    lane = jnp.arange(2 * HEAD_DIM, dtype=jnp.int32)
    indices = (lane % (HEAD_DIM // 2)).astype(jnp.float32)
    frequency = jnp.exp(indices * (-2.0 * math.log(10000.0) / HEAD_DIM))
    phase = relative.astype(jnp.float32)[:, None] * frequency[None, :]
    sign = jnp.where(lane % HEAD_DIM < HEAD_DIM // 2, -1.0, 1.0)
    return jnp.cos(phase), jnp.sin(phase) * sign[None, :]


BAND = 128
VARIANTS = (3, 4, 5, 6, 7, 9)
STEP_COLUMNS = 384
BLOCK = 512
F32 = jnp.float32
BF16 = jnp.bfloat16
MATMUL = (((1,), (0,)), ((), ()))
MATMUL_RIGHT = (((1,), (1,)), ((), ()))
MATMUL_LEFT = (((0,), (0,)), ((), ()))


def product(left, right, dims=MATMUL):
    return lax.dot_general(left, right, dims, preferred_element_type=F32)


def vmem(limit=56):
    return pltpu.CompilerParams(vmem_limit_bytes=limit << 20)


def cost(flops, moved):
    return pl.CostEstimate(flops=int(flops), bytes_accessed=int(moved), transcendentals=0)


def swap_halves(values):
    lane = lax.broadcasted_iota(jnp.int32, values.shape, 1)
    low = lax.rem(lane, HEAD_DIM) < HEAD_DIM // 2
    return jnp.where(
        low,
        pltpu.roll(values, 2 * HEAD_DIM - HEAD_DIM // 2, 1),
        pltpu.roll(values, HEAD_DIM // 2, 1),
    )


def turn(values, cosine, sine):
    parts = []
    for at in range(0, values.shape[1], 128):
        part = values[:, at : at + 128]
        parts.append(part * cosine + swap_halves(part) * sine)
    return jnp.concatenate(parts, axis=1)


def beside():
    dp, fs = lax.axis_index("dp"), lax.axis_index("fsdp")
    return ((dp, fs - 1), fs > 0), ((dp, fs + 1), fs < lax.axis_size("fsdp") - 1)


def greet_beside():
    barrier = pltpu.get_barrier_semaphore()
    count = 0
    for device_at, there in beside():

        @pl.when(there)
        def _(device_at=device_at):
            pl.semaphore_signal(barrier, inc=1, device_id=device_at, device_id_type=MESH)

        count = count + jnp.where(there, 1, 0)
    pl.semaphore_wait(barrier, count)


def halo_copies(sources, landing, send_sem, recv_sem):
    return [
        (
            there,
            pltpu.make_async_remote_copy(
                src_ref=sources[side],
                dst_ref=landing.at[1 - side],
                send_sem=send_sem.at[side],
                recv_sem=recv_sem.at[1 - side],
                device_id=device_at,
                device_id_type=MESH,
            ),
        )
        for side, (device_at, there) in enumerate(beside())
    ]


def halo_start(sources, landing, send_sem, recv_sem):
    for there, copy in halo_copies(sources, landing, send_sem, recv_sem):
        pl.when(there)(copy.start)


def halo_wait(sources, landing, send_sem, recv_sem):
    sides = beside()
    for side, (there, copy) in enumerate(halo_copies(sources, landing, send_sem, recv_sem)):
        pl.when(there)(copy.wait_send)
        device_at, _ = sides[side]

        @pl.when(there)
        def _(side=side, device_at=device_at):
            pltpu.make_async_remote_copy(
                src_ref=sources[side],
                dst_ref=landing.at[side],
                send_sem=send_sem.at[side],
                recv_sem=recv_sem.at[side],
                device_id=device_at,
                device_id_type=MESH,
            ).wait_recv()

        @pl.when(jnp.logical_not(there))
        def _(side=side):
            landing[side] = jnp.zeros(landing.shape[1:], landing.dtype)


def project_kernel(
    x_ref, w_ref, bias_ref, mod_ref, cos_ref, sin_ref, q_ref, own_ref, low_ref, high_ref, h_ref, halo_ref,
    mine, landing, send_sem, recv_sem,
):
    step = pl.program_id(0)
    rows = x_ref.shape[0]

    @pl.when(step == 0)
    def _():
        normed, _ = normalize(x_ref[...].astype(F32))
        hidden_in = (normed * (1.0 + mod_ref[0, 1:2]) + mod_ref[0, 0:1]).astype(BF16)
        mine[...] = hidden_in
        h_ref[...] = hidden_in
        greet_beside()
        halo_start((mine, mine), landing, send_sem, recv_sem)

    def own_turned(y):
        return turn(y, cos_ref[WIN_MAX : WIN_MAX + rows], sin_ref[WIN_MAX : WIN_MAX + rows]).astype(BF16)

    @pl.when(step < 6)
    def _():
        y = product(mine[...], w_ref[...]) + bias_ref[0]

        @pl.when(step < 2)
        def _():
            q_ref[...] = own_turned(y)

        @pl.when((step >= 2) & (step < 4))
        def _():
            own_ref[0] = own_turned(y)

        @pl.when(step >= 4)
        def _():
            own_ref[0] = y.astype(BF16)

    @pl.when(step == 6)
    def _():
        halo_wait((mine, mine), landing, send_sem, recv_sem)
        halo_ref[...] = landing[...]

    @pl.when(step >= 6)
    def _():
        for side, out_ref, first in ((0, low_ref, 0), (1, high_ref, WIN_MAX + rows)):
            y = product(landing[side], w_ref[...]) + bias_ref[0]

            @pl.when(step < 8)
            def _(y=y, out_ref=out_ref, first=first):
                table = slice(first, first + WIN_MAX)
                out_ref[0] = turn(y, cos_ref[table], sin_ref[table]).astype(BF16)

            @pl.when(step >= 8)
            def _(y=y, out_ref=out_ref):
                out_ref[0] = y.astype(BF16)


def project(layer, stream, square, bias, modulation, cosine, sine, ident):
    rows = stream.shape[0]
    whole = lambda shape: pl.BlockSpec(shape, lambda c: (0,) * len(shape))

    def halves(first):
        def index(c):
            at = jnp.clip(c - first, 0, 3)
            return (at // 2, 0, at % 2)

        return pl.BlockSpec((1, rows, STEP_COLUMNS), index)

    column = lambda c: (0, jnp.where(c < 6, c, c - 4))
    pair = jax.ShapeDtypeStruct((2, rows, D), BF16)
    single = jax.ShapeDtypeStruct((rows, D), BF16)
    return pl.pallas_call(
        project_kernel,
        grid=(10,),
        in_specs=[
            whole((rows, D)),
            pl.BlockSpec((D, STEP_COLUMNS), column),
            pl.BlockSpec((1, 1, STEP_COLUMNS), lambda c: (layer, *column(c))),
            pl.BlockSpec((1, 4, D), lambda c: (layer, 0, 0)),
            whole((rows + 2 * WIN_MAX, 128)),
            whole((rows + 2 * WIN_MAX, 128)),
        ],
        out_specs=(
            pl.BlockSpec((rows, STEP_COLUMNS), lambda c: (0, jnp.minimum(c, 1))),
            halves(2),
            halves(6),
            halves(6),
            whole((rows, D)),
            whole((2, rows, D)),
        ),
        out_shape=(single, pair, pair, pair, single, pair),
        scratch_shapes=[
            pltpu.VMEM((rows, D), BF16),
            pltpu.VMEM((2, rows, D), BF16),
            pltpu.SemaphoreType.DMA((2,)),
            pltpu.SemaphoreType.DMA((2,)),
        ],
        compiler_params=pltpu.CompilerParams(
            vmem_limit_bytes=56 << 20, collective_id=ident, has_side_effects=True
        ),
        cost_estimate=cost(2 * rows * D * 7 * D, 8e6),
        name="project",
    )(stream, square, bias, modulation, cosine, sine)


def stack_heads(pair):
    lane = lax.broadcasted_iota(jnp.int32, pair.shape, 1)
    zero = jnp.zeros_like(pair)
    return jnp.concatenate(
        [jnp.where(lane < HEAD_DIM, pair, zero), jnp.where(lane < HEAD_DIM, zero, pair)], axis=0
    )


def merge_heads(stacked):
    rows = stacked.shape[0] // 2
    lane = lax.broadcasted_iota(jnp.int32, (rows, stacked.shape[1]), 1)
    return jnp.where(lane < HEAD_DIM, stacked[:rows], stacked[rows:])


def over_bands(bounds_ref, count, action):
    def one(number, carry):
        low, need = bounds_ref[0, number], bounds_ref[1, number]
        before = 0
        for size in VARIANTS:

            @pl.when((need > before) & (need <= size))
            def _(size=size):
                start = jnp.minimum(low, count - size) * BAND
                action(pl.multiple_of(number * BAND, BAND), pl.multiple_of(start, BAND), size * BAND)

            before = size
        return carry

    lax.fori_loop(0, bounds_ref.shape[1], one, 0)


PAIRS = 2
LANES = 128 * PAIRS


def load_band(ext, low_ref, own_ref, high_ref):
    rows = own_ref.shape[1]
    for at in range(2):
        ext[at, :WIN_MAX] = low_ref[at]
        ext[at, WIN_MAX : WIN_MAX + rows] = own_ref[at]
        ext[at, WIN_MAX + rows :] = high_ref[at]


def attend_kernel(bounds_ref, q_ref, low_ref, own_ref, high_ref, idq_ref, idk_ref, o_ref, lse_ref, ext):
    rows = own_ref.shape[1]
    load_band(ext, low_ref, own_ref, high_ref)

    def block(first, start, size):
        mine = pl.ds(first, BAND)
        band = pl.ds(start, size)
        ids = idq_ref[mine, :]
        allowed = jnp.concatenate([ids] * (size // BAND), axis=1) == idk_ref[0:1, band]
        allowed = jnp.concatenate([allowed, allowed], axis=0)
        pairs = range(PAIRS)
        lanes = [slice(128 * p, 128 * p + 128) for p in pairs]
        queries = [stack_heads(q_ref[mine, lanes[p]]) * jnp.asarray(HEAD_DIM**-0.5, BF16) for p in pairs]
        scores = [product(queries[p], ext[0, band, lanes[p]], MATMUL_RIGHT) for p in pairs]
        scores = [jnp.where(allowed, scores[p], NEGATIVE) for p in pairs]
        peaks = [jnp.max(scores[p], axis=1, keepdims=True) for p in pairs]
        weights = [jnp.exp(scores[p] - peaks[p]) for p in pairs]
        totals = [jnp.sum(weights[p], axis=1, keepdims=True) for p in pairs]
        mixed = [product(weights[p].astype(BF16), ext[1, band, lanes[p]]) for p in pairs]
        for p in pairs:
            o_ref[mine, lanes[p]] = merge_heads(mixed[p] * (1.0 / totals[p])).astype(BF16)
            wide = jnp.broadcast_to(peaks[p] + jnp.log(totals[p]), (2 * BAND, BAND))
            lse_ref[p, 0:1, mine] = wide[:BAND].T[0:1]
            lse_ref[p, 1:2, mine] = wide[BAND:].T[0:1]

    over_bands(bounds_ref, (rows + 2 * WIN_MAX) // BAND, block)


def pair_spec(rows):
    return pl.BlockSpec((2, rows, LANES), lambda j, b: (0, 0, j))


def attend(bounds, queries, low, own, high, ids_query, ids_key):
    rows = queries.shape[0]
    wide = rows + 2 * WIN_MAX
    column = pl.BlockSpec((rows, LANES), lambda j, b: (0, j))
    return pl.pallas_call(
        attend_kernel,
        grid_spec=pltpu.PrefetchScalarGridSpec(
            num_scalar_prefetch=1,
            grid=(D // LANES,),
            in_specs=[
                column,
                pair_spec(WIN_MAX),
                pair_spec(rows),
                pair_spec(WIN_MAX),
                pl.BlockSpec((rows, 128), lambda j, b: (0, 0)),
                pl.BlockSpec((8, wide), lambda j, b: (0, 0)),
            ],
            out_specs=(column, pl.BlockSpec((PAIRS, 8, rows), lambda j, b: (j, 0, 0))),
            scratch_shapes=[pltpu.VMEM((2, wide, LANES), BF16)],
        ),
        out_shape=(
            jax.ShapeDtypeStruct((rows, D), BF16),
            jax.ShapeDtypeStruct((HEADS // 2, 8, rows), F32),
        ),
        compiler_params=vmem(),
        cost_estimate=cost(5e9, 8e6),
        name="attend",
    )(bounds, queries, low, own, high, ids_query, ids_key)


def attend_back_kernel(
    bounds_ref, q_ref, g_ref, o_ref, lse_ref, low_ref, own_ref, high_ref, idq_ref, idk_ref,
    cos_ref, sin_ref, dq_ref, dlow_ref, down_ref, dhigh_ref, ext, dext,
):
    rows = own_ref.shape[1]
    load_band(ext, low_ref, own_ref, high_ref)
    dext[...] = jnp.zeros_like(dext)

    def delta_of(mine, lanes):
        both_heads = (g_ref[mine, lanes].astype(F32) * o_ref[mine, lanes].astype(F32)).T
        return jnp.concatenate(
            [
                jnp.sum(both_heads[:HEAD_DIM], axis=0, keepdims=True),
                jnp.sum(both_heads[HEAD_DIM:], axis=0, keepdims=True),
            ],
            axis=1,
        )

    def block(first, start, size):
        mine = pl.ds(first, BAND)
        band = pl.ds(start, size)
        ids = idk_ref[band, :] == idq_ref[0:1, mine]
        allowed = jnp.concatenate([ids, ids], axis=1)
        pairs = range(PAIRS)
        lanes = [slice(128 * p, 128 * p + 128) for p in pairs]
        queries = [stack_heads(q_ref[mine, lanes[p]]) * jnp.asarray(HEAD_DIM**-0.5, BF16) for p in pairs]
        grads = [stack_heads(g_ref[mine, lanes[p]]) for p in pairs]
        keys = [ext[0, band, lanes[p]] for p in pairs]
        scores = [product(keys[p], queries[p], MATMUL_RIGHT) for p in pairs]
        grad_weights = [product(ext[1, band, lanes[p]], grads[p], MATMUL_RIGHT) for p in pairs]
        lse = [
            jnp.concatenate([lse_ref[p, 0:1, mine], lse_ref[p, 1:2, mine]], axis=1) for p in pairs
        ]
        deltas = [delta_of(mine, lanes[p]) for p in pairs]
        weights = [jnp.where(allowed, jnp.exp(scores[p] - lse[p]), 0.0) for p in pairs]
        grad_scores = [(weights[p] * (grad_weights[p] - deltas[p])).astype(BF16) for p in pairs]
        table = pl.ds(pl.multiple_of(first + WIN_MAX, BAND), BAND)
        cosine, sine = cos_ref[table, :], -sin_ref[table, :]
        for p in pairs:
            dext[0, band, lanes[p]] += product(grad_scores[p], queries[p])
            dext[1, band, lanes[p]] += product(weights[p].astype(BF16), grads[p])
            turned = merge_heads(product(grad_scores[p], keys[p], MATMUL_LEFT)) * HEAD_DIM**-0.5
            dq_ref[mine, lanes[p]] = turn(turned, cosine, sine).astype(BF16)

    over_bands(bounds_ref, (rows + 2 * WIN_MAX) // BAND, block)
    for out_ref, part in (
        (dlow_ref, slice(0, WIN_MAX)),
        (down_ref, slice(WIN_MAX, WIN_MAX + rows)),
        (dhigh_ref, slice(WIN_MAX + rows, 2 * WIN_MAX + rows)),
    ):
        out_ref[0] = turn(dext[0, part], cos_ref[part], -sin_ref[part]).astype(BF16)
        out_ref[1] = dext[1, part].astype(BF16)


def attend_back(bounds, queries, grads, attended, lse, low, own, high, ids_query, ids_key, cosine, sine):
    rows = queries.shape[0]
    wide = rows + 2 * WIN_MAX
    column = pl.BlockSpec((rows, LANES), lambda j, b: (0, j))
    fixed = lambda shape: pl.BlockSpec(shape, lambda j, b: (0,) * len(shape))
    return pl.pallas_call(
        attend_back_kernel,
        grid_spec=pltpu.PrefetchScalarGridSpec(
            num_scalar_prefetch=1,
            grid=(D // LANES,),
            in_specs=[
                column,
                column,
                column,
                pl.BlockSpec((PAIRS, 8, rows), lambda j, b: (j, 0, 0)),
                pair_spec(WIN_MAX),
                pair_spec(rows),
                pair_spec(WIN_MAX),
                fixed((8, rows)),
                fixed((wide, 128)),
                fixed((wide, 128)),
                fixed((wide, 128)),
            ],
            out_specs=(column, pair_spec(WIN_MAX), pair_spec(rows), pair_spec(WIN_MAX)),
            scratch_shapes=[pltpu.VMEM((2, wide, LANES), BF16), pltpu.VMEM((2, wide, LANES), F32)],
        ),
        out_shape=(
            jax.ShapeDtypeStruct((rows, D), BF16),
            jax.ShapeDtypeStruct((2, WIN_MAX, D), BF16),
            jax.ShapeDtypeStruct((2, rows, D), BF16),
            jax.ShapeDtypeStruct((2, WIN_MAX, D), BF16),
        ),
        compiler_params=vmem(),
        cost_estimate=cost(12e9, 16e6),
        name="attend_back",
    )(bounds, queries, grads, attended, lse, low, own, high, ids_query, ids_key, cosine, sine)


def feed_kernel(
    o_ref, x_ref, wo_ref, we_ref, ws_ref, bo_ref, be_ref, bs_ref, mod_ref,
    mid_ref, h_ref, z_ref, slope_ref, out_ref,
):
    step = pl.program_id(0)

    @pl.when(step == 0)
    def _():
        middle = x_ref[...].astype(F32) + (product(o_ref[...], wo_ref[...]) + bo_ref[0])
        mid_ref[...] = middle
        normed, _ = normalize(middle)
        h_ref[...] = (normed * (1.0 + mod_ref[0, 3:4]) + mod_ref[0, 2:3]).astype(BF16)
        out_ref[...] = middle + bs_ref[0]

    u = product(h_ref[...], we_ref[...]) + be_ref[0]
    share = 0.5 + 0.5 * lax.erf(u * (0.5**0.5))
    active = (u * share).astype(BF16)
    z_ref[...] = active
    slope_ref[...] = (share + u * (jnp.exp(-0.5 * u * u) * (2.0 * math.pi) ** -0.5)).astype(BF16)
    out_ref[...] += product(active, ws_ref[...])


def feed(layer, attended, stream, square, shrink, bias, modulation):
    rows = stream.shape[0]
    whole = lambda shape: pl.BlockSpec(shape, lambda c: (0,) * len(shape))
    width = STEP_COLUMNS
    return pl.pallas_call(
        feed_kernel,
        grid=(FF // width,),
        in_specs=[
            whole((rows, D)),
            whole((rows, D)),
            pl.BlockSpec((D, D), lambda c: (0, 3)),
            pl.BlockSpec((D, width), lambda c: (0, 4 * D // width + c)),
            pl.BlockSpec((width, D), lambda c: (c, 0)),
            pl.BlockSpec((1, 1, D), lambda c: (layer, 0, 3)),
            pl.BlockSpec((1, 1, width), lambda c: (layer, 0, 4 * D // width + c)),
            pl.BlockSpec((1, 1, D), lambda c: (layer, 0, 8)),
            pl.BlockSpec((1, 4, D), lambda c: (layer, 0, 0)),
        ],
        out_specs=(
            whole((rows, D)),
            whole((rows, D)),
            pl.BlockSpec((rows, width), lambda c: (0, c)),
            pl.BlockSpec((rows, width), lambda c: (0, c)),
            whole((rows, D)),
        ),
        out_shape=(
            jax.ShapeDtypeStruct((rows, D), F32),
            jax.ShapeDtypeStruct((rows, D), BF16),
            jax.ShapeDtypeStruct((rows, FF), BF16),
            jax.ShapeDtypeStruct((rows, FF), BF16),
            jax.ShapeDtypeStruct((rows, D), F32),
        ),
        compiler_params=vmem(),
        cost_estimate=cost(2 * rows * D * (D + 2 * FF), 24e6),
        name="feed",
    )(attended, stream, square, square, shrink, bias, bias, bias, modulation)


def feed_back_kernel(
    g_ref, z_ref, slope_ref, h_ref, mid_ref, o_ref, we_ref, ws_ref, wo_ref, mod_ref,
    dexp_ref, dout_ref, dshr_ref, mid_grad_ref, do_ref, dbe_ref, sums_ref,
    low, turned, total,
):
    step = pl.program_id(0)
    chunks = FF // STEP_COLUMNS

    @pl.when(step == 0)
    def _():
        low[...] = g_ref[...].astype(BF16)
        turned[...] = h_ref[...].T
        total[...] = jnp.zeros_like(total)
        sums_ref[3:4] = jnp.sum(low[...].astype(F32), axis=0, keepdims=True)

    @pl.when(step < chunks)
    def _():
        grad_active = product(low[...], ws_ref[...], MATMUL_RIGHT)
        grad_hidden = (grad_active * slope_ref[...].astype(F32)).astype(BF16)
        dbe_ref[...] = jnp.sum(grad_hidden.astype(F32), axis=0, keepdims=True)
        dshr_ref[...] = product(z_ref[...], low[...], MATMUL_LEFT).astype(BF16)
        dexp_ref[...] = product(turned[...], grad_hidden).astype(BF16)
        total[...] += product(grad_hidden, we_ref[...], MATMUL_RIGHT)

    @pl.when(step == chunks)
    def _():
        normed, inverse = normalize(mid_ref[...])
        grad = total[...]
        sums_ref[0:1] = jnp.sum(grad, axis=0, keepdims=True)
        sums_ref[1:2] = jnp.sum(grad * normed, axis=0, keepdims=True)
        middle = g_ref[...].astype(F32) + normalize_back(grad * (1.0 + mod_ref[0, 3:4]), normed, inverse)
        mid_grad_ref[...] = middle
        low[...] = middle.astype(BF16)
        sums_ref[2:3] = jnp.sum(low[...].astype(F32), axis=0, keepdims=True)
        do_ref[...] = product(low[...], wo_ref[...], MATMUL_RIGHT).astype(BF16)
        turned[...] = o_ref[...].T
        dout_ref[...] = product(turned[...], low[:, :STEP_COLUMNS]).astype(BF16)

    @pl.when(step == chunks + 1)
    def _():
        dout_ref[...] = product(turned[...], low[:, STEP_COLUMNS:]).astype(BF16)


def feed_back(layer, grad, active, slope, hidden_in, middle, attended, square, shrink, modulation):
    rows = grad.shape[0]
    whole = lambda shape: pl.BlockSpec(shape, lambda c: (0,) * len(shape))
    width = STEP_COLUMNS
    chunks = FF // width
    upto = lambda c: jnp.minimum(c, chunks - 1)
    return pl.pallas_call(
        feed_back_kernel,
        grid=(chunks + 2,),
        in_specs=[
            whole((rows, D)),
            pl.BlockSpec((rows, width), lambda c: (0, upto(c))),
            pl.BlockSpec((rows, width), lambda c: (0, upto(c))),
            whole((rows, D)),
            whole((rows, D)),
            whole((rows, D)),
            pl.BlockSpec((D, width), lambda c: (0, 4 * D // width + upto(c))),
            pl.BlockSpec((width, D), lambda c: (upto(c), 0)),
            pl.BlockSpec((D, D), lambda c: (0, 3)),
            pl.BlockSpec((1, 4, D), lambda c: (layer, 0, 0)),
        ],
        out_specs=(
            pl.BlockSpec((D, width), lambda c: (0, upto(c))),
            pl.BlockSpec((D, width), lambda c: (0, jnp.clip(c - chunks, 0, 1))),
            pl.BlockSpec((width, D), lambda c: (upto(c), 0)),
            whole((rows, D)),
            whole((rows, D)),
            pl.BlockSpec((1, width), lambda c: (0, upto(c))),
            whole((4, D)),
        ),
        out_shape=(
            jax.ShapeDtypeStruct((D, FF), BF16),
            jax.ShapeDtypeStruct((D, D), BF16),
            jax.ShapeDtypeStruct((FF, D), BF16),
            jax.ShapeDtypeStruct((rows, D), F32),
            jax.ShapeDtypeStruct((rows, D), BF16),
            jax.ShapeDtypeStruct((1, FF), F32),
            jax.ShapeDtypeStruct((4, D), F32),
        ),
        scratch_shapes=[
            pltpu.VMEM((rows, D), BF16),
            pltpu.VMEM((D, rows), BF16),
            pltpu.VMEM((rows, D), F32),
        ],
        compiler_params=vmem(),
        cost_estimate=cost(4 * rows * D * (D + 2 * FF), 40e6),
        name="feed_back",
    )(grad, active, slope, hidden_in, middle, attended, square, shrink, square, modulation)


def project_back_kernel(
    dq_ref, low_ref, own_ref, high_ref, h_ref, halo_ref, x_ref, mid_grad_ref, w_ref, mod_ref,
    square_ref, out_ref, db_ref, sums_ref,
    turned, total, around, sending, landing, send_sem, recv_sem,
):
    step = pl.program_id(0)
    rows = x_ref.shape[0]
    middle = slice(WIN_MAX, WIN_MAX + rows)
    sources = (sending.at[0], sending.at[1])

    @pl.when(step == 0)
    def _():
        around[...] = jnp.zeros_like(around)
        total[...] = jnp.zeros_like(total)
        greet_beside()

    @pl.when(step < 4)
    def _():
        around[0] += product(low_ref[0], w_ref[...], MATMUL_RIGHT)
        around[1] += product(high_ref[0], w_ref[...], MATMUL_RIGHT)

    @pl.when(step == 3)
    def _():
        sending[...] = around[...].astype(BF16)
        halo_start(sources, landing, send_sem, recv_sem)
        turned[:, :WIN_MAX] = halo_ref[0].T
        turned[:, middle] = h_ref[...].T
        turned[:, WIN_MAX + rows :] = halo_ref[1].T

    @pl.when((step >= 4) & (step < 6))
    def _():
        grad = dq_ref[...]
        db_ref[...] = jnp.sum(grad.astype(F32), axis=0, keepdims=True)
        square_ref[...] = product(turned[:, middle], grad).astype(BF16)
        total[...] += product(grad, w_ref[...], MATMUL_RIGHT)

    @pl.when(step >= 6)
    def _():
        grad = jnp.concatenate([low_ref[0], own_ref[0], high_ref[0]], axis=0)
        db_ref[...] = jnp.sum(grad.astype(F32), axis=0, keepdims=True)
        square_ref[...] = product(turned[...], grad).astype(BF16)
        total[...] += product(own_ref[0], w_ref[...], MATMUL_RIGHT)

    @pl.when(step == 9)
    def _():
        halo_wait(sources, landing, send_sem, recv_sem)
        normed, inverse = normalize(x_ref[...].astype(F32))
        grad = total[...] + landing[0].astype(F32) + landing[1].astype(F32)
        sums_ref[0:1] = jnp.sum(grad, axis=0, keepdims=True)
        sums_ref[1:2] = jnp.sum(grad * normed, axis=0, keepdims=True)
        out_ref[...] = mid_grad_ref[...] + normalize_back(
            grad * (1.0 + mod_ref[0, 1:2]), normed, inverse
        )


def project_back(layer, dq, low, own, high, hidden_in, halo, stream, mid_grad, square, modulation, ident):
    rows = dq.shape[0]
    width = STEP_COLUMNS
    whole = lambda shape: pl.BlockSpec(shape, lambda c: (0,) * len(shape))

    def halves(c):
        at = jnp.where(c < 4, c, jnp.clip(c - 6, 0, 3))
        return (at // 2, 0, at % 2)

    later = pl.BlockSpec((1, rows, width), halves)
    own_columns = lambda c: (0, jnp.clip(c - 4, 0, 5))
    return pl.pallas_call(
        project_back_kernel,
        grid=(10,),
        in_specs=[
            pl.BlockSpec((rows, width), lambda c: (0, jnp.clip(c - 4, 0, 1))),
            later,
            later,
            later,
            whole((rows, D)),
            whole((2, rows, D)),
            whole((rows, D)),
            whole((rows, D)),
            pl.BlockSpec((D, width), lambda c: (0, jnp.where(c < 4, c + 2, c - 4))),
            pl.BlockSpec((1, 4, D), lambda c: (layer, 0, 0)),
        ],
        out_specs=(
            pl.BlockSpec((D, width), own_columns),
            whole((rows, D)),
            pl.BlockSpec((1, width), own_columns),
            whole((2, D)),
        ),
        out_shape=(
            jax.ShapeDtypeStruct((D, 3 * D), BF16),
            jax.ShapeDtypeStruct((rows, D), F32),
            jax.ShapeDtypeStruct((1, 3 * D), F32),
            jax.ShapeDtypeStruct((2, D), F32),
        ),
        scratch_shapes=[
            pltpu.VMEM((D, rows + 2 * WIN_MAX), BF16),
            pltpu.VMEM((rows, D), F32),
            pltpu.VMEM((2, rows, D), F32),
            pltpu.VMEM((2, rows, D), BF16),
            pltpu.VMEM((2, rows, D), BF16),
            pltpu.SemaphoreType.DMA((2,)),
            pltpu.SemaphoreType.DMA((2,)),
        ],
        compiler_params=pltpu.CompilerParams(
            vmem_limit_bytes=56 << 20, collective_id=ident, has_side_effects=True
        ),
        cost_estimate=cost(4 * rows * D * 6 * D, 20e6),
        name="project_back",
    )(dq, low, own, high, hidden_in, halo, stream, mid_grad, square, modulation)


def direct():
    return lax.axis_size("dp") == NZ * NY and lax.axis_size("fsdp") == NX * 2


BOTH = ("dp", "fsdp")


def pack_small(bias, table):
    flat = jnp.concatenate([bias.reshape(-1), table.reshape(-1)])
    flat = jnp.pad(flat, (0, OWN_ROWS[4] * SMALL - flat.shape[0]))
    return flat.reshape(1, OWN_ROWS[4], SMALL)


def unpack_small(whole, lead_row):
    count = lax.axis_size("dp") * lax.axis_size("fsdp")
    flat = whole.reshape(count, -1).astype(F32)
    wide = LAYERS * 9 * D // count
    bias = flat[:, :wide].reshape(count, LAYERS, 9, -1).transpose(1, 2, 0, 3).reshape(LAYERS, 1, 9 * D)
    table = flat[:, wide : wide + LAYERS * LEADS * 4 * D // count].reshape(count, LAYERS, LEADS, -1)
    rows = lax.dynamic_index_in_dim(table, lead_row, 2, keepdims=False)
    return bias, rows.transpose(1, 0, 2).reshape(LAYERS, 4, D)


def plain_fetch(masters, layer):
    square = jnp.concatenate([masters[n][layer].astype(BF16) for n in range(3)], axis=1)
    shrink = masters[3][layer].astype(BF16)
    return (
        lax.all_gather(square, BOTH, axis=0, tiled=True),
        lax.all_gather(shrink, BOTH, axis=0, tiled=True),
    )


def plain_small(masters, lead_row):
    bias = lax.all_gather(masters[4].astype(BF16), BOTH, axis=2, tiled=True)
    table = lax.all_gather(masters[5].astype(BF16), BOTH, axis=2, tiled=True)
    modulation = lax.dynamic_index_in_dim(table, lead_row, 1, keepdims=False)
    return bias.astype(F32).reshape(LAYERS, 1, 9 * D), modulation.astype(F32).reshape(LAYERS, 4, D)


def plain_reduce(whole):
    return lax.psum_scatter(whole, BOTH, scatter_dimension=0, tiled=True).astype(F32)


def reduce_small_inputs(bias_grads, rows_grads, lead_hot):
    count = lax.axis_size("dp") * lax.axis_size("fsdp")
    bias = bias_grads.reshape(LAYERS, 9, count, -1).transpose(2, 1, 0, 3).reshape(count, -1)
    rows = rows_grads.reshape(LAYERS, 1, count, -1) * lead_hot[None, :, None, None]
    rows = rows.transpose(2, 1, 0, 3).reshape(count, -1)
    flat = jnp.concatenate([bias, rows], axis=1)
    used = flat.shape[1]
    flat = jnp.pad(flat, ((0, 0), (0, OWN_ROWS[4] * SMALL - used)))
    return flat.reshape(-1, SMALL).astype(BF16)


def split_small(own):
    count = lax.axis_size("dp") * lax.axis_size("fsdp")
    flat = own.reshape(-1)
    wide = LAYERS * 9 * D // count
    used = wide + LAYERS * LEADS * 4 * D // count
    bias = flat[:wide].reshape(9, LAYERS, -1)
    rows = flat[wide:used].reshape(LEADS, LAYERS, -1)
    return bias.transpose(1, 0, 2), rows.transpose(1, 0, 2)


def bands(segment_ids, segment_starts, padding_mask, offset, rows):
    length = segment_ids.shape[0]
    position = jnp.arange(length, dtype=jnp.int32)
    real = padding_mask == 1
    names = jnp.where(real, segment_ids, length + position)
    fill = jnp.full((WIN_MAX,), -1, jnp.int32)
    wide = lax.dynamic_slice_in_dim(
        jnp.concatenate([fill, names, fill - 1]), offset, rows + 2 * WIN_MAX
    )
    own = lax.dynamic_slice_in_dim(names, offset, rows)
    piece = lambda array: lax.dynamic_slice_in_dim(array, offset, rows).reshape(-1, BAND)
    at = offset + jnp.arange(rows // BAND, dtype=jnp.int32) * BAND
    starts, windows, kept = piece(segment_starts), piece(segment_ids), piece(padding_mask) == 1
    begins = jnp.where(kept[:, 0], starts[:, 0], at)
    ends = jnp.sum((segment_ids[None, :] <= windows[:, -1:]).astype(jnp.int32), axis=1)
    ends = jnp.where(kept[:, -1], ends, at + BAND)
    low = (begins - offset + WIN_MAX) // BAND
    need = (ends - offset + WIN_MAX + BAND - 1) // BAND - low
    return jnp.stack([low, need]), own, wide


def adam_update(weight, gradient, moment, square, step_rate, decay_rate):
    moment = BETA_ONE * moment + (1.0 - BETA_ONE) * gradient
    square = BETA_TWO * square + (1.0 - BETA_TWO) * gradient * gradient
    first_fix = 1.0 - BETA_ONE**STEP
    second_fix = 1.0 - BETA_TWO**STEP
    update = moment / first_fix / (jnp.sqrt(square / second_fix) + ADAM_EPSILON)
    weight = weight - step_rate * (update + decay_rate * weight)
    return (weight, moment, square, weight.astype(jnp.bfloat16))


def shards(
    tokens,
    cotangent,
    segment_ids,
    segment_starts,
    padding_mask,
    lead_index,
    input_weights,
    input_moment,
    input_square,
    output_weights,
    output_moment,
    output_square,
    expand_weights,
    expand_moment,
    expand_square,
    shrink_weights,
    shrink_moment,
    shrink_square,
    bias_vector,
    bias_moment,
    bias_square,
    lead_table,
    lead_moment,
    lead_square,
):
    rows = tokens.shape[0]
    offset = lax.axis_index("fsdp") * rows
    bounds, own_names, wide_names = bands(segment_ids, segment_starts, padding_mask, offset, rows)
    ids_query = jnp.broadcast_to(own_names[:, None], (rows, 128))
    ids_key = jnp.broadcast_to(wide_names[None, :], (8, wide_names.shape[0]))
    ids_query_row = jnp.broadcast_to(own_names[None, :], (8, rows))
    ids_key_column = jnp.broadcast_to(wide_names[:, None], (wide_names.shape[0], 128))
    fill = jnp.zeros((WIN_MAX,), jnp.int32)
    relative = jnp.arange(segment_starts.shape[0], dtype=jnp.int32) - segment_starts
    relative = jnp.concatenate([fill, relative, fill])
    cosine, sine = rotary_tables(
        lax.dynamic_slice_in_dim(relative, offset, rows + 2 * WIN_MAX)
    )
    lead_row = lead_index[0]
    lead_hot = (jnp.arange(LEADS, dtype=jnp.int32) == lead_row).astype(F32)
    masters = (input_weights, output_weights, expand_weights, shrink_weights, bias_vector, lead_table)
    linked = direct()
    if linked:
        small = pack_small(bias_vector, lead_table)
        small_full, *first = alone(
            GatherJob(GATHERED, 0), (small, *masters[:4]), "gather_first", 0
        )
        bias, modulation = unpack_small(small_full, lead_row)
        layers = [first]
    else:
        layers = [plain_fetch(masters, 0)]
        bias, modulation = plain_small(masters, lead_row)
    layers += [plain_fetch(masters, layer) for layer in range(1, LAYERS)]
    stream = tokens
    saved = []
    for layer in range(LAYERS):
        square, shrink = layers[layer]
        queries, own, low, high, first_in, halo = project(
            layer, stream, square, bias, modulation, cosine, sine, 10 + layer
        )
        attended, lse = attend(bounds, queries, low, own, high, ids_query, ids_key)
        middle, second_in, active, slope, result = feed(
            layer, attended, stream, square, shrink, bias, modulation
        )
        saved.append(
            (stream, queries, low, own, high, first_in, halo, attended, lse, middle, second_in, active, slope)
        )
        stream = result
    grad = cotangent
    partials = [None] * LAYERS
    bias_grads = [None] * LAYERS
    rows_grads = [None] * LAYERS
    reduced = [[None] * 4 for _ in range(LAYERS)]
    for layer in reversed(range(LAYERS)):
        square, shrink = layers[layer]
        (
            before, queries, low, own, high, first_in, halo, attended, lse, middle, second_in, active, slope,
        ) = saved[layer]
        expand_grad, output_grad, shrink_grad, mid_grad, attended_grad, expand_bias, sums = feed_back(
            layer, grad, active, slope, second_in, middle, attended, square, shrink, modulation
        )
        dq, low_grad, own_grad, high_grad = attend_back(
            bounds, queries, attended_grad, attended, lse, low, own, high, ids_query_row,
            ids_key_column, cosine, sine,
        )
        input_grad, grad, input_bias, more_sums = project_back(
            layer, dq, low_grad, own_grad, high_grad, first_in, halo, before, mid_grad, square, modulation,
            20 + layer,
        )
        bias_grads[layer] = jnp.concatenate([input_bias[0], sums[2], expand_bias[0], sums[3]])
        rows_grads[layer] = jnp.concatenate([more_sums[0], more_sums[1], sums[0], sums[1]])
        partials[layer] = (input_grad, output_grad, expand_grad, shrink_grad)
        if not linked:
            reduced[layer] = [plain_reduce(whole) for whole in partials[layer]]
        elif layer > 0:
            later_shrink = lax.psum_scatter(shrink_grad, BOTH, scatter_dimension=0, tiled=True)
    if linked:
        small = reduce_small_inputs(jnp.stack(bias_grads), jnp.stack(rows_grads), lead_hot)
        small, later_shrink = lax.optimization_barrier((small, later_shrink))
        reduced[1][3] = later_shrink.astype(F32)
        job = ScatterJob(SCATTERED)
        input_grad, output_grad, expand_grad, shrink_grad = partials[0]
        wide, reduced[0][3] = alone(
            job,
            (*partials[1][:3], expand_grad, shrink_grad, input_grad, output_grad, small),
            "scatter_last",
            1,
        )
        part = lambda n: wide[:, job.first[n] : job.first[n] + WIDTHS[n]]
        reduced[0][:3] = [part(0), part(1), part(2)]
        reduced[1][:3] = [part(5), part(6), part(7)]
        bias_grad, lead_grad = split_small(part(4))
    else:
        bias_grad = lax.psum_scatter(
            jnp.stack(bias_grads).reshape(LAYERS, 9, D), BOTH, scatter_dimension=2, tiled=True
        )
        lead_grad = lax.psum_scatter(
            jnp.stack(rows_grads)[:, None, :] * lead_hot[None, :, None], BOTH, scatter_dimension=2,
            tiled=True,
        )
    moments = (input_moment, output_moment, expand_moment, shrink_moment, bias_moment, lead_moment)
    squares = (input_square, output_square, expand_square, shrink_square, bias_square, lead_square)
    results = []
    for number in range(6):
        if number < 4:
            gradient = jnp.stack([reduced[layer][number] for layer in range(LAYERS)])
        else:
            gradient = (bias_grad, lead_grad)[number - 4]
        results.append(
            adam_update(
                masters[number],
                gradient,
                moments[number],
                squares[number],
                RATE_MATRIX if number < 4 else RATE_VECTOR,
                DECAY if number < 4 else 0.0,
            )
        )
    return (stream, grad, *(array for four in results for array in four))


def solution(mesh):
    rows = P(("dp", "fsdp"), None)
    matrix = P(None, ("dp", "fsdp"), None)
    vector = P(None, None, ("dp", "fsdp"))
    return jax.shard_map(
        shards,
        mesh=mesh,
        in_specs=(rows,) * 2 + (P("dp"),) * 4 + (matrix,) * 12 + (vector,) * 6,
        out_specs=(rows,) * 2 + (matrix,) * 16 + (vector,) * 8,
        check_vma=False,
    )
```
